32 devices in a mesh: ctx: 8 (over y, x, core), head: 4 (over z).
Axes of the slice: x: 2, y: 2, z: 4, core: 2. Of those that a mesh axis runs over, the one named last changes fastest.
Arguments:
- queries: bfloat16 [1024, 512], P('ctx', 'head'), may hold values from -6 to 6
- key_rows: bfloat16 [1024, 512], P('ctx', 'head'), may hold values from -6 to 6
- value_rows: bfloat16 [1024, 512], P('ctx', 'head'), may hold values from -6 to 6
- out_grad: bfloat16 [1024, 512], P('ctx', 'head'), may hold values from -24 to 24
- attn_out: bfloat16 [1024, 512], P('ctx', 'head'), may hold values from -6 to 6
- log_norm: float32 [1024, 4], P('ctx', 'head'), as said below
- query_weight: bfloat16 [4096, 512], P(None, 'head'), may hold values from -0.5 to 0.5
- key_weight: bfloat16 [4096, 512], P(None, 'head'), may hold values from -0.5 to 0.5
- value_weight: bfloat16 [4096, 512], P(None, 'head'), may hold values from -0.5 to 0.5
Outputs:
- input_grad: bfloat16 [1024, 4096], P('ctx', 'head')
The draws below stay inside these ranges and needn't reach their ends.
Inputs may be any that keep to these rules, and one draw needn't show every extreme that they name: log_norm[t, h] lies between log(1 + t) and log(1 + t) + 1.5, with t the token's position.
All inputs are finite; a program needn't handle non-finite values.
Results may differ from the reference program's by a relative error of at most 0.009.
Values may be sent and summed in bfloat16 or wider, within the bound.
No kernel may reach another device: no remote copies, remote signals or barrier semaphores. Data moves between devices by JAX's collectives and lax.ppermute only.
A program may use at most 128 MiB of HBM per device.

```python
import math
import jax
import jax.numpy as jnp
from jax import lax

D = 4096
HD = 128
HEADS_DEV = 1
HEADS = 4
TOKENS = 1024
N_HEAD = 4


def draw_log_norm(key, part):
    key = jax.random.fold_in(key, 11)
    positions = jnp.arange(TOKENS, dtype=jnp.float32)
    offset = jax.random.uniform(key, (TOKENS, HEADS), jnp.float32, 0.25, 1.25)
    return jnp.log1p(positions)[:, None] + offset


def levels(rng, dims, split, low, high):
    def one(axis_at, parts):
        heights = jax.random.uniform(jax.random.fold_in(jax.random.fold_in(rng, 6), axis_at), (parts,), jnp.float32, low / len(split), high / len(split))
        return jnp.repeat(jnp.exp(heights), dims[axis_at] // parts).reshape((-1,) + (1,) * (len(dims) - axis_at - 1))

    level = one(*split[0])
    for cut in split[1:]:
        level = level * one(*cut)
    return level


def centred(key, dims, spread, reach, pieces=(), kind=jnp.bfloat16):
    values = jax.random.normal(key, dims, jnp.float32) * spread
    if len(pieces) > 0:
        values = levels(key, dims, pieces, -0.22, 0.18) * values
    return jnp.clip(values, min=-reach, max=reach).astype(kind)


def setup_inputs(seed: int = 0) -> dict:
    arg_keys = jax.random.split(jax.random.key(seed), 10)
    queries = centred(arg_keys[0], (TOKENS, HEADS * HD), 1.0, 6.0, ((0, 8), (1, 4)))
    key_rows = centred(arg_keys[1], (TOKENS, HEADS * HD), 1.0, 6.0, ((0, 8), (1, 4)))
    value_rows = centred(arg_keys[2], (TOKENS, HEADS * HD), 1.0, 6.0, ((0, 8), (1, 4)))
    out_grad = centred(arg_keys[3], (TOKENS, HEADS * HD), 4.0, 24.0, ((0, 8), (1, 4)))
    attn_out = centred(arg_keys[4], (TOKENS, HEADS * HD), 1.0, 6.0, ((0, 8), (1, 4)))
    log_norm = draw_log_norm(jax.random.fold_in(arg_keys[9], 71), 0)
    query_weight = centred(arg_keys[6], (D, HEADS * HD), HD ** -0.5, 0.5, ((1, 4),))
    key_weight = centred(arg_keys[7], (D, HEADS * HD), HD ** -0.5, 0.5, ((1, 4),))
    value_weight = centred(arg_keys[8], (D, HEADS * HD), HD ** -0.5, 0.5, ((1, 4),))
    return {"queries": queries, "key_rows": key_rows, "value_rows": value_rows, "out_grad": out_grad, "attn_out": attn_out, "log_norm": log_norm, "query_weight": query_weight, "key_weight": key_weight, "value_weight": value_weight}


def block_terms(query_blk, grad_blk, norm_blk, delta_blk, query_pos, key_blk, value_blk, key_pos, score_scale):
    count = query_blk.shape[0]
    query_wide = query_blk.astype(jnp.float32).reshape(count, HEADS, HD)
    grad_wide = grad_blk.astype(jnp.float32).reshape(count, HEADS, HD)
    key_wide = key_blk.astype(jnp.float32).reshape(count, HEADS, HD)
    value_wide = value_blk.astype(jnp.float32).reshape(count, HEADS, HD)
    scores = score_scale * jnp.einsum("qhd,khd->hqk", query_wide, key_wide)
    visible = key_pos[None, None, :] <= query_pos[None, :, None]
    probs = jnp.where(visible, jnp.exp(scores - norm_blk.T[:, :, None]), 0.0)
    prob_grad = jnp.einsum("qhd,khd->hqk", grad_wide, value_wide)
    score_grad = probs * (prob_grad - delta_blk.T[:, :, None])
    score_low = lax.optimization_barrier(score_grad.astype(jnp.bfloat16)).astype(jnp.float32)
    probs_low = lax.optimization_barrier(probs.astype(jnp.bfloat16)).astype(jnp.float32)
    query_part = score_scale * jnp.einsum("hqk,khd->qhd", score_low, key_wide)
    key_part = score_scale * jnp.einsum("hqk,qhd->khd", score_low, query_wide)
    value_part = jnp.einsum("hqk,qhd->khd", probs_low, grad_wide)
    width = HEADS * HD
    return (query_part.reshape(count, width), key_part.reshape(count, width), value_part.reshape(count, width))


def reference(queries, key_rows, value_rows, out_grad, attn_out, log_norm, query_weight, key_weight, value_weight):
    width = HEADS * HD
    score_scale = HD ** -0.5
    delta_rows = jnp.sum((out_grad.astype(jnp.float32) * attn_out.astype(jnp.float32)).reshape(TOKENS, HEADS, HD), axis=2)
    block = math.gcd(TOKENS, 1024)
    blocks = TOKENS // block
    positions = jnp.arange(TOKENS, dtype=jnp.int32)

    def cut_rows(source, index):
        return lax.dynamic_slice_in_dim(source, (index * block).astype(jnp.int32), block, 0)

    def outer(carry, query_index):
        def inner(inner_carry, key_index):
            query_acc, key_grad, value_grad = inner_carry

            def compute():
                return block_terms(cut_rows(queries, query_index), cut_rows(out_grad, query_index),
                                   cut_rows(log_norm, query_index), cut_rows(delta_rows, query_index),
                                   cut_rows(positions, query_index), cut_rows(key_rows, key_index),
                                   cut_rows(value_rows, key_index), cut_rows(positions, key_index), score_scale)

            def skipped():
                empty = jnp.zeros((block, width), jnp.float32)
                return (empty, empty, empty)

            term_list = lax.cond(key_index <= query_index, compute, skipped)
            start_row = (key_index * block).astype(jnp.int32)
            key_grad = lax.dynamic_update_slice_in_dim(key_grad, cut_rows(key_grad, key_index) + term_list[1], start_row, 0)
            value_grad = lax.dynamic_update_slice_in_dim(value_grad, cut_rows(value_grad, key_index) + term_list[2], start_row, 0)
            return (query_acc + term_list[0], key_grad, value_grad), None

        start_acc = jnp.zeros((block, width), jnp.float32)
        (query_acc, key_grad, value_grad), unused = lax.scan(inner, (start_acc, carry[0], carry[1]), jnp.arange(blocks, dtype=jnp.int32))
        return (key_grad, value_grad), query_acc

    empty_all = jnp.zeros((TOKENS, width), jnp.float32)
    (key_grad, value_grad), query_parts = lax.scan(outer, (empty_all, empty_all), jnp.arange(blocks, dtype=jnp.int32))
    query_low = query_parts.reshape(TOKENS, width).astype(jnp.bfloat16)
    key_low = key_grad.astype(jnp.bfloat16)
    value_low = value_grad.astype(jnp.bfloat16)
    group = HEADS_DEV * HD
    total = jnp.zeros((TOKENS, D), jnp.float32)
    for group_index in range(N_HEAD):
        lower = group_index * group
        upper = lower + group
        partial_value = jnp.dot(query_low[:, lower:upper], query_weight[:, lower:upper].T, preferred_element_type=jnp.float32)
        partial_value = partial_value + jnp.dot(key_low[:, lower:upper], key_weight[:, lower:upper].T, preferred_element_type=jnp.float32)
        partial_value = partial_value + jnp.dot(value_low[:, lower:upper], value_weight[:, lower:upper].T, preferred_element_type=jnp.float32)
        total = total + lax.optimization_barrier(partial_value.astype(jnp.bfloat16)).astype(jnp.float32)
    return total.astype(jnp.bfloat16)
```

```python
import functools
import math

import jax
import jax.numpy as jnp
from jax import lax
from jax.experimental import pallas as pl
from jax.experimental.pallas import tpu as pltpu
from jax.sharding import PartitionSpec as P

NT = (((1,), (1,)), ((), ()))
PIECES = 3


def dot_nt(left, right):
    return lax.dot_general(left, right, NT, preferred_element_type=jnp.float32)


def pieces_of(column):
    out = []
    rest = column
    for _ in range(PIECES):
        low = rest.astype(jnp.bfloat16).astype(jnp.float32)
        out.append(low)
        rest = rest - low
    return out


def pack_kernel(norm_scale, k_ref, v_ref, q_ref, g_ref, a_ref, n_ref, out_ref):
    rows, width = q_ref.shape
    grad = g_ref[...]
    delta = jnp.sum(
        grad.astype(jnp.float32) * a_ref[...].astype(jnp.float32), axis=1, keepdims=True
    )
    row_at = lax.broadcasted_iota(jnp.int32, (rows, rows), 0)
    col_at = lax.broadcasted_iota(jnp.int32, (rows, rows), 1)
    norm = jnp.sum(
        jnp.where(row_at == col_at, n_ref[...] * norm_scale, 0.0), axis=1, keepdims=True
    )
    lane = lax.broadcasted_iota(jnp.int32, (rows, width), 1)
    extra = jnp.zeros((rows, width), jnp.float32)
    for at, piece in enumerate(pieces_of(norm) + pieces_of(delta)):
        extra = jnp.where(lane == at, piece, extra)
    out_ref[:, :width] = k_ref[...]
    out_ref[:, width : 2 * width] = v_ref[...]
    out_ref[:, 2 * width : 3 * width] = q_ref[...]
    out_ref[:, 3 * width : 4 * width] = extra.astype(jnp.bfloat16)
    out_ref[:, 4 * width :] = grad


def main_kernel(
    chunk, cols, scale, me_ref, all_ref, own_ref, wq_ref, wk_ref, wv_ref, out_ref, w_all, grads, sems
):
    rows = own_ref.shape[0]
    width = wq_ref.shape[1]
    copies = [
        pltpu.make_async_copy(ref, w_all.at[:, at * width : (at + 1) * width], sems.at[at])
        for at, ref in enumerate((wq_ref, wk_ref, wv_ref))
    ]
    for copy in copies:
        copy.start()
    first = me_ref[0] * rows
    exponent = scale * math.log2(math.e)
    key = own_ref[:, :width]
    value = own_ref[:, width : 2 * width]
    query = own_ref[:, 2 * width : 3 * width]
    extra = own_ref[:, 3 * width : 4 * width].astype(jnp.float32)
    grad = own_ref[:, 4 * width :]
    lane = lax.broadcasted_iota(jnp.int32, (rows, width), 1)
    in_norm = lane < PIECES
    in_delta = jnp.logical_and(lane >= PIECES, lane < 2 * PIECES)
    norm = jnp.sum(jnp.where(in_norm, extra, 0.0), axis=1, keepdims=True)
    delta = jnp.sum(jnp.where(in_delta, extra, 0.0), axis=1, keepdims=True)
    key_wide = jnp.concatenate([key, jnp.where(in_norm, -1.0, 0.0).astype(jnp.bfloat16)], axis=1)
    value_wide = jnp.concatenate(
        [jnp.where(in_delta, -1.0, 0.0).astype(jnp.bfloat16), value], axis=1
    )
    own_at = first + lax.broadcasted_iota(jnp.int32, (rows, chunk), 0)
    lane_at = lax.broadcasted_iota(jnp.int32, (rows, chunk), 1)

    def step(at, sums):
        query_sum, key_sum, value_sum = sums
        span = pl.ds(pl.multiple_of(at * chunk, chunk), chunk)
        other_at = lane_at + at * chunk
        keys = all_ref[span, :width]
        scores = dot_nt(query, keys)
        probs = jnp.where(other_at <= own_at, jnp.exp2(exponent * (scores - norm)), 0.0)
        prob_grad = dot_nt(grad, all_ref[span, width : 2 * width])
        score_low = (probs * (prob_grad - delta)).astype(jnp.bfloat16)
        query_sum += jnp.dot(score_low, keys, preferred_element_type=jnp.float32)
        scores = dot_nt(key_wide, all_ref[span, 2 * width : 4 * width])
        probs = jnp.where(own_at <= other_at, jnp.exp2(exponent * scores), 0.0)
        prob_grad = dot_nt(value_wide, all_ref[span, 3 * width :])
        score_low = (probs * prob_grad).astype(jnp.bfloat16)
        key_sum += jnp.dot(
            score_low, all_ref[span, 2 * width : 3 * width], preferred_element_type=jnp.float32
        )
        value_sum += jnp.dot(
            probs.astype(jnp.bfloat16), all_ref[span, 4 * width :], preferred_element_type=jnp.float32
        )
        return query_sum, key_sum, value_sum

    zero = jnp.zeros((rows, width), jnp.float32)
    count = all_ref.shape[0] // chunk
    if count == 1:
        sums = step(0, (zero, zero, zero))
    else:
        sums = lax.fori_loop(0, count, step, (zero, zero, zero))
    grads[:, :width] = (scale * sums[0]).astype(jnp.bfloat16)
    grads[:, width : 2 * width] = (scale * sums[1]).astype(jnp.bfloat16)
    grads[:, 2 * width :] = sums[2].astype(jnp.bfloat16)
    for copy in copies:
        copy.wait()
    for at in range(0, w_all.shape[0], cols):
        out_ref[:, at : at + cols] = dot_nt(grads[...], w_all[at : at + cols, :]).astype(jnp.bfloat16)


def body(
    queries,
    key_rows,
    value_rows,
    out_grad,
    attn_out,
    log_norm,
    query_weight,
    key_weight,
    value_weight,
):
    rows, width = queries.shape
    depth = query_weight.shape[0]
    scale = width ** (-0.5)
    vmem = pl.BlockSpec(memory_space=pltpu.VMEM)
    packed = pl.pallas_call(
        functools.partial(pack_kernel, 1.0 / scale),
        out_shape=jax.ShapeDtypeStruct((rows, 5 * width), jnp.bfloat16),
        in_specs=[vmem] * 6,
        out_specs=vmem,
    )(key_rows, value_rows, queries, out_grad, attn_out, log_norm.reshape(1, rows))
    gathered = lax.all_gather(packed, "ctx", axis=0, tiled=True)
    me = lax.axis_index("ctx").astype(jnp.int32).reshape(1)
    total = gathered.shape[0]
    chunk = math.gcd(total, 1024)
    hbm = pl.BlockSpec(memory_space=pl.ANY)
    partial_value = pl.pallas_call(
        functools.partial(main_kernel, chunk, math.gcd(depth, 512), scale),
        out_shape=jax.ShapeDtypeStruct((rows, depth), jnp.bfloat16),
        in_specs=[pl.BlockSpec(memory_space=pltpu.SMEM), vmem, vmem, hbm, hbm, hbm],
        out_specs=vmem,
        scratch_shapes=[
            pltpu.VMEM((depth, 3 * width), jnp.bfloat16),
            pltpu.VMEM((rows, 3 * width), jnp.bfloat16),
            pltpu.SemaphoreType.DMA((3,)),
        ],
        compiler_params=pltpu.CompilerParams(vmem_limit_bytes=48 * 1024 * 1024),
        cost_estimate=pl.CostEstimate(
            flops=14 * rows * total * width + 6 * rows * width * depth,
            bytes_accessed=6 * depth * width + 10 * total * width,
            transcendentals=2 * rows * total,
        ),
    )(me, gathered, packed, query_weight, key_weight, value_weight)
    return lax.psum_scatter(partial_value, "head", scatter_dimension=1, tiled=True)


def solution(mesh):
    return jax.shard_map(
        body,
        mesh=mesh,
        in_specs=(P("ctx", "head"),) * 6 + (P(None, "head"),) * 3,
        out_specs=P("ctx", "head"),
        check_vma=False,
    )
```

```python
import functools
import math

import jax
import jax.numpy as jnp
from jax import lax
from jax.experimental import pallas as pl
from jax.experimental.pallas import tpu as pltpu
from jax.sharding import PartitionSpec as P

NT = (((1,), (1,)), ((), ()))
TN = (((0,), (0,)), ((), ()))
PIECES = 3
EXTRA = 16
MIB = 1024 * 1024


def dot_nt(left, right):
    return lax.dot_general(left, right, NT, preferred_element_type=jnp.float32)


def dot_tn(left, right):
    return lax.dot_general(left, right, TN, preferred_element_type=jnp.float32)


def dot_nn(left, right):
    return jnp.dot(left, right, preferred_element_type=jnp.float32)


def pieces_of(value):
    out = []
    rest = value
    for _ in range(PIECES):
        low = rest.astype(jnp.bfloat16).astype(jnp.float32)
        out.append(low)
        rest = rest - low
    return out


def diagonal(rows):
    row_at = lax.broadcasted_iota(jnp.int32, (rows, rows), 0)
    col_at = lax.broadcasted_iota(jnp.int32, (rows, rows), 1)
    return row_at == col_at


def delta_of(grad, attn):
    return jnp.sum(grad.astype(jnp.float32) * attn.astype(jnp.float32), axis=1, keepdims=True)


def pack_kernel(me_ref, q_ref, k_ref, v_ref, g_ref, a_ref, n_ref, out_ref):
    rows, width = q_ref.shape
    me = me_ref[0]
    delta = delta_of(g_ref[...], a_ref[...])
    delta = jnp.sum(jnp.where(diagonal(rows), delta, 0.0), axis=0, keepdims=True)
    row = lax.broadcasted_iota(jnp.int32, (EXTRA, rows), 0)
    extra = jnp.zeros((EXTRA, rows), jnp.float32)
    for at, piece in enumerate(pieces_of(n_ref[...]) + pieces_of(delta)):
        extra = jnp.where(row == at, piece, extra)
    extra = extra.astype(jnp.bfloat16)

    def for_later(at, carry):
        out_ref[at, :rows, :width] = k_ref[...]
        out_ref[at, :rows, width:] = v_ref[...]
        out_ref[at, rows:, :] = jnp.zeros((EXTRA, 2 * width), jnp.bfloat16)
        return carry

    def for_earlier(at, carry):
        out_ref[at, :rows, :width] = q_ref[...]
        out_ref[at, :rows, width:] = g_ref[...]
        out_ref[at, rows:, :width] = extra
        out_ref[at, rows:, width:] = jnp.zeros((EXTRA, width), jnp.bfloat16)
        return carry

    lax.fori_loop(0, me + 1, for_earlier, 0)
    lax.fori_loop(me + 1, out_ref.shape[0], for_later, 0)


def main_kernel(
    group,
    scale,
    me_ref,
    got_ref,
    q_ref,
    k_ref,
    v_ref,
    g_ref,
    a_ref,
    n_ref,
    wq_ref,
    wk_ref,
    wv_ref,
    out_ref,
    w_all,
    grads,
    sems,
):
    rows, width = q_ref.shape
    copies = [
        pltpu.make_async_copy(ref, w_all.at[:, at * width : (at + 1) * width], sems.at[at])
        for at, ref in enumerate((wq_ref, wk_ref, wv_ref))
    ]
    for copy in copies:
        copy.start()
    me = me_ref[0]
    exponent = scale * math.log2(math.e)
    query, key, value, grad = q_ref[...], k_ref[...], v_ref[...], g_ref[...]
    eye = diagonal(rows)
    norm = (1.0 / scale) * jnp.sum(jnp.where(eye, n_ref[...], 0.0), axis=1, keepdims=True)
    delta = delta_of(grad, a_ref[...])

    row_at = lax.broadcasted_iota(jnp.int32, (rows, rows), 0)
    col_at = lax.broadcasted_iota(jnp.int32, (rows, rows), 1)
    probs = jnp.where(col_at <= row_at, jnp.exp2(exponent * (dot_nt(query, key) - norm)), 0.0)
    score_low = (probs * (dot_nt(grad, value) - delta)).astype(jnp.bfloat16)
    query_sum = dot_nn(score_low, key)
    key_sum = dot_tn(score_low, query)
    value_sum = dot_tn(probs.astype(jnp.bfloat16), grad)

    first_side = jnp.concatenate([query, key], axis=0)
    second_side = jnp.concatenate([grad, value], axis=0)

    def step(at, sums):
        both_sum, value_sum = sums
        blocks = [at * group + i for i in range(group)]
        first = jnp.concatenate([got_ref[b, :rows, :width] for b in blocks], axis=0)
        second = jnp.concatenate([got_ref[b, :rows, width:] for b in blocks], axis=0)
        extra = jnp.concatenate([got_ref[b, rows:, :width] for b in blocks], axis=1)
        extra = extra.astype(jnp.float32)
        norms = (1.0 / scale) * jnp.sum(extra[:PIECES], axis=0, keepdims=True)
        deltas = jnp.sum(extra[PIECES : 2 * PIECES], axis=0, keepdims=True)
        block = at * group + lax.broadcasted_iota(jnp.int32, (rows, group * rows), 1) // rows
        earlier, later = block < me, block > me
        scores = dot_nt(first_side, first)
        scores = jnp.where(earlier, scores[:rows] - norm, scores[rows:] - norms)
        probs = jnp.exp2(exponent * jnp.where(block == me, 0.0, scores))
        prob_grad = dot_nt(second_side, second)
        prob_grad = jnp.where(earlier, prob_grad[:rows] - delta, prob_grad[rows:] - deltas)
        score_grad = probs * prob_grad
        sides = jnp.concatenate(
            [jnp.where(earlier, score_grad, 0.0), jnp.where(later, score_grad, 0.0)], axis=0
        ).astype(jnp.bfloat16)
        both_sum += dot_nn(sides, first)
        value_sum += dot_nn(jnp.where(later, probs, 0.0).astype(jnp.bfloat16), second)
        return both_sum, value_sum

    sums = (jnp.concatenate([query_sum, key_sum], axis=0), value_sum)
    count = got_ref.shape[0] // group
    if count == 1:
        sums = step(0, sums)
    else:
        sums = lax.fori_loop(0, count, step, sums)
    grads[:, :width] = (scale * sums[0][:rows]).astype(jnp.bfloat16)
    grads[:, width : 2 * width] = (scale * sums[0][rows:]).astype(jnp.bfloat16)
    grads[:, 2 * width :] = sums[1].astype(jnp.bfloat16)
    for copy in copies:
        copy.wait()
    parts, _, part = out_ref.shape
    cols = math.gcd(part, 512)
    for h in range(parts):
        for at in range(0, part, cols):
            weight = w_all[h * part + at : h * part + at + cols, :]
            out_ref[h, :, at : at + cols] = dot_nt(grads[...], weight).astype(jnp.bfloat16)


def body(
    queries,
    key_rows,
    value_rows,
    out_grad,
    attn_out,
    log_norm,
    query_weight,
    key_weight,
    value_weight,
):
    rows, width = queries.shape
    depth = query_weight.shape[0]
    scale = width ** (-0.5)
    ctx = lax.axis_size("ctx")
    parts = lax.axis_size("head")
    vmem = pl.BlockSpec(memory_space=pltpu.VMEM)
    smem = pl.BlockSpec(memory_space=pltpu.SMEM)
    hbm = pl.BlockSpec(memory_space=pltpu.HBM)
    me = lax.axis_index("ctx").astype(jnp.int32).reshape(1)
    own = (queries, key_rows, value_rows, out_grad, attn_out, log_norm.reshape(1, rows))
    packed = pl.pallas_call(
        pack_kernel,
        out_shape=jax.ShapeDtypeStruct((ctx, rows + EXTRA, 2 * width), jnp.bfloat16),
        in_specs=[smem] + [vmem] * 6,
        out_specs=vmem,
        compiler_params=pltpu.CompilerParams(vmem_limit_bytes=32 * MIB),
    )(me, *own)
    got = lax.all_to_all(packed, "ctx", split_axis=0, concat_axis=0, tiled=True)
    total = ctx * rows
    group = math.gcd(ctx, 8)
    parted = pl.pallas_call(
        functools.partial(main_kernel, group, scale),
        out_shape=jax.ShapeDtypeStruct((parts, rows, depth // parts), jnp.bfloat16),
        in_specs=[smem] + [vmem] * 7 + [hbm] * 3,
        out_specs=vmem,
        scratch_shapes=[
            pltpu.VMEM((depth, 3 * width), jnp.bfloat16),
            pltpu.VMEM((rows, 3 * width), jnp.bfloat16),
            pltpu.SemaphoreType.DMA((3,)),
        ],
        compiler_params=pltpu.CompilerParams(vmem_limit_bytes=48 * MIB),
        cost_estimate=pl.CostEstimate(
            flops=14 * rows * total * width + 6 * rows * width * depth,
            bytes_accessed=6 * depth * width + 10 * total * width,
            transcendentals=2 * rows * total,
        ),
    )(me, got, *own, query_weight, key_weight, value_weight)
    swapped = lax.all_to_all(parted, "head", split_axis=0, concat_axis=0, tiled=True)
    return jnp.sum(swapped.astype(jnp.float32), axis=0).astype(jnp.bfloat16)


def solution(mesh):
    return jax.shard_map(
        body,
        mesh=mesh,
        in_specs=(P("ctx", "head"),) * 6 + (P(None, "head"),) * 3,
        out_specs=P("ctx", "head"),
        check_vma=False,
    )
```

```python
import functools
import math

import jax
import jax.numpy as jnp
from jax import lax
from jax.experimental import pallas as pl
from jax.experimental.pallas import tpu as pltpu
from jax.sharding import PartitionSpec as P

NT = (((1,), (1,)), ((), ()))
TN = (((0,), (0,)), ((), ()))
PIECES = 3
EXTRA = 16
MIB = 1024 * 1024


def dot_nt(left, right):
    return lax.dot_general(left, right, NT, preferred_element_type=jnp.float32)


def dot_tn(left, right):
    return lax.dot_general(left, right, TN, preferred_element_type=jnp.float32)


def dot_nn(left, right):
    return jnp.dot(left, right, preferred_element_type=jnp.float32)


def pieces_of(value):
    out = []
    rest = value
    for _ in range(PIECES):
        low = rest.astype(jnp.bfloat16).astype(jnp.float32)
        out.append(low)
        rest = rest - low
    return out


def diagonal(rows):
    row_at = lax.broadcasted_iota(jnp.int32, (rows, rows), 0)
    col_at = lax.broadcasted_iota(jnp.int32, (rows, rows), 1)
    return row_at == col_at


def delta_of(grad, attn):
    return jnp.sum(grad.astype(jnp.float32) * attn.astype(jnp.float32), axis=1, keepdims=True)


def pack_kernel(me_ref, q_ref, k_ref, v_ref, g_ref, a_ref, n_ref, out_ref):
    rows, width = q_ref.shape
    me = me_ref[0]
    delta = delta_of(g_ref[...], a_ref[...])
    delta = jnp.sum(jnp.where(diagonal(rows), delta, 0.0), axis=0, keepdims=True)
    row = lax.broadcasted_iota(jnp.int32, (EXTRA, rows), 0)
    extra = jnp.zeros((EXTRA, rows), jnp.float32)
    for at, piece in enumerate(pieces_of(n_ref[...]) + pieces_of(delta)):
        extra = jnp.where(row == at, piece, extra)
    extra = extra.astype(jnp.bfloat16)

    def for_later(at, carry):
        out_ref[at, :rows, :width] = k_ref[...]
        out_ref[at, :rows, width:] = v_ref[...]
        out_ref[at, rows:, :] = jnp.zeros((EXTRA, 2 * width), jnp.bfloat16)
        return carry

    def for_earlier(at, carry):
        out_ref[at, :rows, :width] = q_ref[...]
        out_ref[at, :rows, width:] = g_ref[...]
        out_ref[at, rows:, :width] = extra
        out_ref[at, rows:, width:] = jnp.zeros((EXTRA, width), jnp.bfloat16)
        return carry

    lax.fori_loop(0, me + 1, for_earlier, 0)
    lax.fori_loop(me + 1, out_ref.shape[0], for_later, 0)


def main_kernel(
    group,
    scale,
    me_ref,
    got_ref,
    q_ref,
    k_ref,
    v_ref,
    g_ref,
    a_ref,
    n_ref,
    wq_ref,
    wk_ref,
    wv_ref,
    out_ref,
    w_all,
    grads,
    sems,
):
    rows, width = q_ref.shape
    copies = [
        pltpu.make_async_copy(ref, w_all.at[:, at * width : (at + 1) * width], sems.at[at])
        for at, ref in enumerate((wq_ref, wk_ref, wv_ref))
    ]
    for copy in copies:
        copy.start()
    me = me_ref[0]
    exponent = scale * math.log2(math.e)
    query, key, value, grad = q_ref[...], k_ref[...], v_ref[...], g_ref[...]
    eye = diagonal(rows)
    norm = (1.0 / scale) * jnp.sum(jnp.where(eye, n_ref[...], 0.0), axis=1, keepdims=True)
    delta = delta_of(grad, a_ref[...])

    row_at = lax.broadcasted_iota(jnp.int32, (rows, rows), 0)
    col_at = lax.broadcasted_iota(jnp.int32, (rows, rows), 1)
    probs = jnp.where(col_at <= row_at, jnp.exp2(exponent * (dot_nt(query, key) - norm)), 0.0)
    score_low = (probs * (dot_nt(grad, value) - delta)).astype(jnp.bfloat16)
    query_sum = dot_nn(score_low, key)
    key_sum = dot_tn(score_low, query)
    value_sum = dot_tn(probs.astype(jnp.bfloat16), grad)

    first_side = jnp.concatenate([query, key], axis=0)
    second_side = jnp.concatenate([grad, value], axis=0)

    def step(at, sums):
        both_sum, value_sum = sums
        blocks = [at * group + i for i in range(group)]
        first = jnp.concatenate([got_ref[b, :rows, :width] for b in blocks], axis=0)
        second = jnp.concatenate([got_ref[b, :rows, width:] for b in blocks], axis=0)
        extra = jnp.concatenate([got_ref[b, rows:, :width] for b in blocks], axis=1)
        extra = extra.astype(jnp.float32)
        norms = (1.0 / scale) * jnp.sum(extra[:PIECES], axis=0, keepdims=True)
        deltas = jnp.sum(extra[PIECES : 2 * PIECES], axis=0, keepdims=True)
        block = at * group + lax.broadcasted_iota(jnp.int32, (rows, group * rows), 1) // rows
        earlier, later = block < me, block > me
        scores = dot_nt(first_side, first)
        scores = jnp.where(earlier, scores[:rows] - norm, scores[rows:] - norms)
        probs = jnp.exp2(exponent * jnp.where(block == me, 0.0, scores))
        prob_grad = dot_nt(second_side, second)
        prob_grad = jnp.where(earlier, prob_grad[:rows] - delta, prob_grad[rows:] - deltas)
        score_grad = probs * prob_grad
        sides = jnp.concatenate(
            [jnp.where(earlier, score_grad, 0.0), jnp.where(later, score_grad, 0.0)], axis=0
        ).astype(jnp.bfloat16)
        both_sum += dot_nn(sides, first)
        value_sum += dot_nn(jnp.where(later, probs, 0.0).astype(jnp.bfloat16), second)
        return both_sum, value_sum

    sums = (jnp.concatenate([query_sum, key_sum], axis=0), value_sum)
    count = got_ref.shape[0] // group
    if count == 1:
        sums = step(0, sums)
    else:
        sums = lax.fori_loop(0, count, step, sums)
    grads[:, :width] = (scale * sums[0][:rows]).astype(jnp.bfloat16)
    grads[:, width : 2 * width] = (scale * sums[0][rows:]).astype(jnp.bfloat16)
    grads[:, 2 * width :] = sums[1].astype(jnp.bfloat16)
    for copy in copies:
        copy.wait()
    parts, _, part = out_ref.shape
    cols = math.gcd(part, 512)
    for h in range(parts):
        for at in range(0, part, cols):
            weight = w_all[h * part + at : h * part + at + cols, :]
            out_ref[h, :, at : at + cols] = dot_nt(grads[...], weight).astype(jnp.bfloat16)


def send_kernel(
    spot_ref, q_in, k_in, v_in, g_in, a_in, n_ref, wq_ref, wk_ref, wv_ref, *refs
):
    q_ref, k_ref, v_ref, g_ref, a_ref, in_sems, w_sems = refs[-7:]
    outs = refs[:-7]
    me, head = spot_ref[0], spot_ref[1]
    rows, width = q_ref.shape
    hops = [ref for ref in outs if ref.shape[0] == rows + EXTRA]
    blocks = [ref for ref in outs if ref.shape[0] != rows + EXTRA]
    part = wq_ref.shape[0] // (len(blocks) + 1)
    piece = blocks[0].shape[0]
    loads = [
        pltpu.make_async_copy(src, dst, in_sems.at[at])
        for at, (src, dst) in enumerate(
            ((k_in, k_ref), (v_in, v_ref), (q_in, q_ref), (g_in, g_ref), (a_in, a_ref))
        )
    ]
    for load in loads:
        load.start()
    moves = []
    for at, block in enumerate(blocks):
        start = pl.multiple_of((head ^ (at + 1)) * part + me * piece, piece)
        for col, weight in enumerate((wq_ref, wk_ref, wv_ref)):
            moves.append(
                pltpu.make_async_copy(
                    weight.at[pl.ds(start, piece), :],
                    block.at[:, col * width : (col + 1) * width],
                    w_sems.at[3 * at + col],
                )
            )
    for move in moves:
        move.start()
    for load in loads:
        load.wait()
    delta = delta_of(g_ref[...], a_ref[...])
    delta = jnp.sum(jnp.where(diagonal(rows), delta, 0.0), axis=0, keepdims=True)
    row = lax.broadcasted_iota(jnp.int32, (EXTRA, rows), 0)
    extra = jnp.zeros((EXTRA, rows), jnp.float32)
    for at, value in enumerate(pieces_of(n_ref[...]) + pieces_of(delta)):
        extra = jnp.where(row == at, value, extra)
    extra = extra.astype(jnp.bfloat16)
    for at, hop in enumerate(hops):
        later = (me ^ (at + 1)) > me
        hop[:rows, :width] = jnp.where(later, k_ref[...], q_ref[...])
        hop[:rows, width:] = jnp.where(later, v_ref[...], g_ref[...])
        hop[rows:, :width] = extra
        hop[rows:, width:] = jnp.zeros((EXTRA, width), jnp.bfloat16)
    for move in moves:
        move.wait()


def grad_kernel(scale, spot_ref, q_ref, k_ref, v_ref, g_ref, a_ref, n_ref, *refs):
    out_ref = refs[-1]
    got = refs[:-1]
    rows, width = q_ref.shape
    me = spot_ref[0]
    exponent = scale * math.log2(math.e)
    query, key, value, grad = q_ref[...], k_ref[...], v_ref[...], g_ref[...]
    norm = (1.0 / scale) * jnp.sum(
        jnp.where(diagonal(rows), n_ref[...], 0.0), axis=1, keepdims=True
    )
    delta = delta_of(grad, a_ref[...])
    row_at = lax.broadcasted_iota(jnp.int32, (rows, rows), 0)
    col_at = lax.broadcasted_iota(jnp.int32, (rows, rows), 1)
    probs = jnp.where(col_at <= row_at, jnp.exp2(exponent * (dot_nt(query, key) - norm)), 0.0)
    score_low = (probs * (dot_nt(grad, value) - delta)).astype(jnp.bfloat16)
    query_sum = dot_nn(score_low, key)
    key_sum = dot_tn(score_low, query)
    value_sum = dot_tn(probs.astype(jnp.bfloat16), grad)

    first = jnp.concatenate([ref[:rows, :width] for ref in got], axis=0)
    second = jnp.concatenate([ref[:rows, width:] for ref in got], axis=0)
    extra = jnp.concatenate([ref[rows:, :width] for ref in got], axis=1).astype(jnp.float32)
    norms = (1.0 / scale) * jnp.sum(extra[:PIECES], axis=0, keepdims=True)
    deltas = jnp.sum(extra[PIECES : 2 * PIECES], axis=0, keepdims=True)
    lanes = lax.broadcasted_iota(jnp.int32, (rows, len(got) * rows), 1)
    earlier = ((lanes // rows + 1) ^ me) < me
    scores = dot_nt(jnp.concatenate([query, key], axis=0), first)
    scores = jnp.where(earlier, scores[:rows] - norm, scores[rows:] - norms)
    probs = jnp.exp2(exponent * scores)
    prob_grad = dot_nt(jnp.concatenate([grad, value], axis=0), second)
    prob_grad = jnp.where(earlier, prob_grad[:rows] - delta, prob_grad[rows:] - deltas)
    score_grad = probs * prob_grad
    sides = jnp.concatenate(
        [jnp.where(earlier, score_grad, 0.0), jnp.where(earlier, 0.0, score_grad)], axis=0
    ).astype(jnp.bfloat16)
    both_sum = dot_nn(sides, first)
    value_sum += dot_nn(jnp.where(earlier, 0.0, probs).astype(jnp.bfloat16), second)
    out_ref[:, :width] = (scale * (query_sum + both_sum[:rows])).astype(jnp.bfloat16)
    out_ref[:, width : 2 * width] = (scale * (key_sum + both_sum[rows:])).astype(jnp.bfloat16)
    out_ref[:, 2 * width :] = value_sum.astype(jnp.bfloat16)


def project_kernel(count, order, spot_ref, wq_ref, wk_ref, wv_ref, *refs):
    grads = refs[:count]
    shares = refs[count:-3]
    out_ref, w_own, sems = refs[-3:]
    width = wq_ref.shape[1]
    part = out_ref.shape[1]
    me, head = spot_ref[0], spot_ref[1]
    start = pl.multiple_of(head * part, part)
    loads = [
        pltpu.make_async_copy(
            ref.at[pl.ds(start, part), :], w_own.at[:, at * width : (at + 1) * width], sems.at[at]
        )
        for at, ref in enumerate((wq_ref, wk_ref, wv_ref))
    ]
    for load in loads:
        load.start()
    for load in loads:
        load.wait()
    piece = shares[0].shape[1]
    for offset, share in zip(order, shares):
        at = pl.multiple_of((me ^ offset) * piece, piece)
        total = dot_nt(grads[0][...], w_own[pl.ds(at, piece), :])
        for other in range(count - 1):
            total += dot_nt(grads[other + 1][...], share[other])
        out_ref[:, pl.ds(at, piece)] = total.astype(jnp.bfloat16)


def swap(value, axis, offset):
    size = lax.axis_size(axis)
    return lax.ppermute(value, axis, [(at, at ^ offset) for at in range(size)])


def near_body(own, weights, spot, scale):
    rows, width = own[0].shape
    depth = weights[0].shape[0]
    ctx = lax.axis_size("ctx")
    parts = lax.axis_size("head")
    part = depth // parts
    piece = part // ctx
    vmem = pl.BlockSpec(memory_space=pltpu.VMEM)
    smem = pl.BlockSpec(memory_space=pltpu.SMEM)
    hbm = pl.BlockSpec(memory_space=pl.ANY)
    params = pltpu.CompilerParams(vmem_limit_bytes=58 * MIB)
    hop = jax.ShapeDtypeStruct((rows + EXTRA, 2 * width), jnp.bfloat16)
    block = jax.ShapeDtypeStruct((piece, 3 * width), jnp.bfloat16)
    sent = pl.pallas_call(
        send_kernel,
        out_shape=[hop] * (ctx - 1) + [block] * (parts - 1),
        in_specs=[smem] + [hbm] * 5 + [vmem] + [hbm] * 3,
        out_specs=[vmem] * (ctx + parts - 2),
        scratch_shapes=[pltpu.VMEM((rows, width), jnp.bfloat16)] * 5
        + [pltpu.SemaphoreType.DMA((5,)), pltpu.SemaphoreType.DMA((3 * (parts - 1),))],
        compiler_params=params,
    )(spot, *own, *weights)
    got = [swap(sent[at], "ctx", at + 1) for at in range(ctx - 1)]
    shares = {0: jnp.stack([swap(sent[ctx - 1 + at], "head", at + 1) for at in range(parts - 1)])}
    for offset in range(2, ctx, 2):
        shares[offset] = swap(shares[0], "ctx", offset)
    for offset in range(0, ctx, 2):
        shares[offset + 1] = swap(shares[offset], "ctx", 1)
    grads = pl.pallas_call(
        functools.partial(grad_kernel, scale),
        out_shape=jax.ShapeDtypeStruct((rows, 3 * width), jnp.bfloat16),
        in_specs=[smem] + [vmem] * (ctx + 5),
        out_specs=vmem,
        compiler_params=pltpu.CompilerParams(vmem_limit_bytes=32 * MIB),
        cost_estimate=pl.CostEstimate(
            flops=14 * rows * rows * ctx * width,
            bytes_accessed=4 * rows * ctx * width,
            transcendentals=rows * rows * ctx,
        ),
    )(spot, *own, *got)
    all_grads = [grads] + [swap(grads, "head", at) for at in range(1, parts)]
    return pl.pallas_call(
        functools.partial(project_kernel, parts, tuple(shares)),
        out_shape=jax.ShapeDtypeStruct((rows, part), jnp.bfloat16),
        in_specs=[smem] + [hbm] * 3 + [vmem] * (parts + ctx),
        out_specs=vmem,
        scratch_shapes=[
            pltpu.VMEM((part, 3 * width), jnp.bfloat16),
            pltpu.SemaphoreType.DMA((3,)),
        ],
        compiler_params=params,
        cost_estimate=pl.CostEstimate(
            flops=6 * rows * width * depth, bytes_accessed=6 * depth * width, transcendentals=0
        ),
    )(spot, *weights, *all_grads, *shares.values())


def far_body(own, weights, spot, scale):
    rows, width = own[0].shape
    depth = weights[0].shape[0]
    ctx = lax.axis_size("ctx")
    parts = lax.axis_size("head")
    vmem = pl.BlockSpec(memory_space=pltpu.VMEM)
    smem = pl.BlockSpec(memory_space=pltpu.SMEM)
    hbm = pl.BlockSpec(memory_space=pl.ANY)
    packed = pl.pallas_call(
        pack_kernel,
        out_shape=jax.ShapeDtypeStruct((ctx, rows + EXTRA, 2 * width), jnp.bfloat16),
        in_specs=[smem] + [vmem] * 6,
        out_specs=vmem,
        compiler_params=pltpu.CompilerParams(vmem_limit_bytes=32 * MIB),
    )(spot, *own)
    got = lax.all_to_all(packed, "ctx", split_axis=0, concat_axis=0, tiled=True)
    total = ctx * rows
    group = math.gcd(ctx, 8)
    parted = pl.pallas_call(
        functools.partial(main_kernel, group, scale),
        out_shape=jax.ShapeDtypeStruct((parts, rows, depth // parts), jnp.bfloat16),
        in_specs=[smem] + [vmem] * 7 + [hbm] * 3,
        out_specs=vmem,
        scratch_shapes=[
            pltpu.VMEM((depth, 3 * width), jnp.bfloat16),
            pltpu.VMEM((rows, 3 * width), jnp.bfloat16),
            pltpu.SemaphoreType.DMA((3,)),
        ],
        compiler_params=pltpu.CompilerParams(vmem_limit_bytes=48 * MIB),
        cost_estimate=pl.CostEstimate(
            flops=14 * rows * total * width + 6 * rows * width * depth,
            bytes_accessed=6 * depth * width + 10 * total * width,
            transcendentals=2 * rows * total,
        ),
    )(spot, got, *own, *weights)
    swapped = lax.all_to_all(parted, "head", split_axis=0, concat_axis=0, tiled=True)
    return jnp.sum(swapped.astype(jnp.float32), axis=0).astype(jnp.bfloat16)


def body(
    queries,
    key_rows,
    value_rows,
    out_grad,
    attn_out,
    log_norm,
    query_weight,
    key_weight,
    value_weight,
):
    rows, width = queries.shape
    ctx, parts = lax.axis_size("ctx"), lax.axis_size("head")
    spot = jnp.stack([lax.axis_index("ctx"), lax.axis_index("head")]).astype(jnp.int32)
    own = (queries, key_rows, value_rows, out_grad, attn_out, log_norm.reshape(1, rows))
    weights = (query_weight, key_weight, value_weight)
    near = ctx <= 8 and parts <= 4 and ctx & (ctx - 1) == 0 and parts & (parts - 1) == 0
    return (near_body if near else far_body)(own, weights, spot, width ** (-0.5))


def solution(mesh):
    return jax.shard_map(
        body,
        mesh=mesh,
        in_specs=(P("ctx", "head"),) * 6 + (P(None, "head"),) * 3,
        out_specs=P("ctx", "head"),
        check_vma=False,
    )
```

```python
import functools
import math

import jax
import jax.numpy as jnp
from jax import lax
from jax.experimental import pallas as pl
from jax.experimental.pallas import tpu as pltpu
from jax.sharding import PartitionSpec as P

NT = (((1,), (1,)), ((), ()))
TN = (((0,), (0,)), ((), ()))
PIECES = 3
EXTRA = 16
MIB = 1024 * 1024


def dot_nt(left, right):
    return lax.dot_general(left, right, NT, preferred_element_type=jnp.float32)


def dot_tn(left, right):
    return lax.dot_general(left, right, TN, preferred_element_type=jnp.float32)


def dot_nn(left, right):
    return jnp.dot(left, right, preferred_element_type=jnp.float32)


def pieces_of(value):
    out = []
    rest = value
    for _ in range(PIECES):
        low = rest.astype(jnp.bfloat16).astype(jnp.float32)
        out.append(low)
        rest = rest - low
    return out


def diagonal(rows):
    row_at = lax.broadcasted_iota(jnp.int32, (rows, rows), 0)
    col_at = lax.broadcasted_iota(jnp.int32, (rows, rows), 1)
    return row_at == col_at


def delta_of(grad, attn):
    return jnp.sum(grad.astype(jnp.float32) * attn.astype(jnp.float32), axis=1, keepdims=True)


def pack_kernel(me_ref, q_ref, k_ref, v_ref, g_ref, a_ref, n_ref, out_ref):
    rows, width = q_ref.shape
    me = me_ref[0]
    delta = delta_of(g_ref[...], a_ref[...])
    delta = jnp.sum(jnp.where(diagonal(rows), delta, 0.0), axis=0, keepdims=True)
    row = lax.broadcasted_iota(jnp.int32, (EXTRA, rows), 0)
    extra = jnp.zeros((EXTRA, rows), jnp.float32)
    for at, piece in enumerate(pieces_of(n_ref[...]) + pieces_of(delta)):
        extra = jnp.where(row == at, piece, extra)
    extra = extra.astype(jnp.bfloat16)

    def for_later(at, carry):
        out_ref[at, :rows, :width] = k_ref[...]
        out_ref[at, :rows, width:] = v_ref[...]
        out_ref[at, rows:, :] = jnp.zeros((EXTRA, 2 * width), jnp.bfloat16)
        return carry

    def for_earlier(at, carry):
        out_ref[at, :rows, :width] = q_ref[...]
        out_ref[at, :rows, width:] = g_ref[...]
        out_ref[at, rows:, :width] = extra
        out_ref[at, rows:, width:] = jnp.zeros((EXTRA, width), jnp.bfloat16)
        return carry

    lax.fori_loop(0, me + 1, for_earlier, 0)
    lax.fori_loop(me + 1, out_ref.shape[0], for_later, 0)


def main_kernel(
    group,
    scale,
    me_ref,
    got_ref,
    q_ref,
    k_ref,
    v_ref,
    g_ref,
    a_ref,
    n_ref,
    wq_ref,
    wk_ref,
    wv_ref,
    out_ref,
    w_all,
    grads,
    sems,
):
    rows, width = q_ref.shape
    copies = [
        pltpu.make_async_copy(ref, w_all.at[:, at * width : (at + 1) * width], sems.at[at])
        for at, ref in enumerate((wq_ref, wk_ref, wv_ref))
    ]
    for copy in copies:
        copy.start()
    me = me_ref[0]
    exponent = scale * math.log2(math.e)
    query, key, value, grad = q_ref[...], k_ref[...], v_ref[...], g_ref[...]
    eye = diagonal(rows)
    norm = (1.0 / scale) * jnp.sum(jnp.where(eye, n_ref[...], 0.0), axis=1, keepdims=True)
    delta = delta_of(grad, a_ref[...])

    row_at = lax.broadcasted_iota(jnp.int32, (rows, rows), 0)
    col_at = lax.broadcasted_iota(jnp.int32, (rows, rows), 1)
    probs = jnp.where(col_at <= row_at, jnp.exp2(exponent * (dot_nt(query, key) - norm)), 0.0)
    score_low = (probs * (dot_nt(grad, value) - delta)).astype(jnp.bfloat16)
    query_sum = dot_nn(score_low, key)
    key_sum = dot_tn(score_low, query)
    value_sum = dot_tn(probs.astype(jnp.bfloat16), grad)

    first_side = jnp.concatenate([query, key], axis=0)
    second_side = jnp.concatenate([grad, value], axis=0)

    def step(at, sums):
        both_sum, value_sum = sums
        blocks = [at * group + i for i in range(group)]
        first = jnp.concatenate([got_ref[b, :rows, :width] for b in blocks], axis=0)
        second = jnp.concatenate([got_ref[b, :rows, width:] for b in blocks], axis=0)
        extra = jnp.concatenate([got_ref[b, rows:, :width] for b in blocks], axis=1)
        extra = extra.astype(jnp.float32)
        norms = (1.0 / scale) * jnp.sum(extra[:PIECES], axis=0, keepdims=True)
        deltas = jnp.sum(extra[PIECES : 2 * PIECES], axis=0, keepdims=True)
        block = at * group + lax.broadcasted_iota(jnp.int32, (rows, group * rows), 1) // rows
        earlier, later = block < me, block > me
        scores = dot_nt(first_side, first)
        scores = jnp.where(earlier, scores[:rows] - norm, scores[rows:] - norms)
        probs = jnp.exp2(exponent * jnp.where(block == me, 0.0, scores))
        prob_grad = dot_nt(second_side, second)
        prob_grad = jnp.where(earlier, prob_grad[:rows] - delta, prob_grad[rows:] - deltas)
        score_grad = probs * prob_grad
        sides = jnp.concatenate(
            [jnp.where(earlier, score_grad, 0.0), jnp.where(later, score_grad, 0.0)], axis=0
        ).astype(jnp.bfloat16)
        both_sum += dot_nn(sides, first)
        value_sum += dot_nn(jnp.where(later, probs, 0.0).astype(jnp.bfloat16), second)
        return both_sum, value_sum

    sums = (jnp.concatenate([query_sum, key_sum], axis=0), value_sum)
    count = got_ref.shape[0] // group
    if count == 1:
        sums = step(0, sums)
    else:
        sums = lax.fori_loop(0, count, step, sums)
    grads[:, :width] = (scale * sums[0][:rows]).astype(jnp.bfloat16)
    grads[:, width : 2 * width] = (scale * sums[0][rows:]).astype(jnp.bfloat16)
    grads[:, 2 * width :] = sums[1].astype(jnp.bfloat16)
    for copy in copies:
        copy.wait()
    parts, _, part = out_ref.shape
    cols = math.gcd(part, 512)
    for h in range(parts):
        for at in range(0, part, cols):
            weight = w_all[h * part + at : h * part + at + cols, :]
            out_ref[h, :, at : at + cols] = dot_nt(grads[...], weight).astype(jnp.bfloat16)


def send_kernel(q_in, k_in, v_in, g_in, a_in, n_ref, *refs):
    q_ref, k_ref, v_ref, g_ref, a_ref, sems = refs[-6:]
    hops = refs[:-6]
    me = lax.axis_index("ctx")
    rows, width = q_ref.shape
    loads = [
        pltpu.make_async_copy(src, dst, sems.at[at])
        for at, (src, dst) in enumerate(
            ((k_in, k_ref), (v_in, v_ref), (q_in, q_ref), (g_in, g_ref), (a_in, a_ref))
        )
    ]
    for load in loads:
        load.start()
    for load in loads:
        load.wait()
    delta = delta_of(g_ref[...], a_ref[...])
    delta = jnp.sum(jnp.where(diagonal(rows), delta, 0.0), axis=0, keepdims=True)
    row = lax.broadcasted_iota(jnp.int32, (EXTRA, rows), 0)
    extra = jnp.zeros((EXTRA, rows), jnp.float32)
    for at, value in enumerate(pieces_of(n_ref[...]) + pieces_of(delta)):
        extra = jnp.where(row == at, value, extra)
    extra = extra.astype(jnp.bfloat16)
    for at, hop in enumerate(hops):
        later = (me ^ (at + 1)) > me

        @pl.when(later)
        def _():
            hop[:rows, :width] = k_ref[...]
            hop[:rows, width:] = v_ref[...]

        @pl.when(jnp.logical_not(later))
        def _():
            hop[:rows, :width] = q_ref[...]
            hop[:rows, width:] = g_ref[...]

        hop[rows:, :width] = extra
        hop[rows:, width:] = jnp.zeros((EXTRA, width), jnp.bfloat16)


def near_kernel(
    scale, parts, q_ref, k_ref, v_ref, g_ref, a_ref, n_ref, wq_ref, wk_ref, wv_ref, *refs
):
    w_all, grads, sems = refs[-3:]
    outs = refs[-3 - parts : -3]
    got = refs[: -3 - parts]
    rows, width = q_ref.shape
    copies = [
        pltpu.make_async_copy(ref, w_all.at[:, at * width : (at + 1) * width], sems.at[at])
        for at, ref in enumerate((wq_ref, wk_ref, wv_ref))
    ]
    for copy in copies:
        copy.start()
    me, head = lax.axis_index("ctx"), lax.axis_index("head")
    exponent = scale * math.log2(math.e)
    query, key, value, grad = q_ref[...], k_ref[...], v_ref[...], g_ref[...]
    norm = (1.0 / scale) * jnp.sum(
        jnp.where(diagonal(rows), n_ref[...], 0.0), axis=1, keepdims=True
    )
    delta = delta_of(grad, a_ref[...])
    row_at = lax.broadcasted_iota(jnp.int32, (rows, rows), 0)
    col_at = lax.broadcasted_iota(jnp.int32, (rows, rows), 1)
    probs = jnp.where(col_at <= row_at, jnp.exp2(exponent * (dot_nt(query, key) - norm)), 0.0)
    score_low = (probs * (dot_nt(grad, value) - delta)).astype(jnp.bfloat16)
    query_sum = dot_nn(score_low, key)
    key_sum = dot_tn(score_low, query)
    value_sum = dot_tn(probs.astype(jnp.bfloat16), grad)

    first = jnp.concatenate([ref[:rows, :width] for ref in got], axis=0)
    second = jnp.concatenate([ref[:rows, width:] for ref in got], axis=0)
    extra = jnp.concatenate([ref[rows:, :width] for ref in got], axis=1).astype(jnp.float32)
    norms = (1.0 / scale) * jnp.sum(extra[:PIECES], axis=0, keepdims=True)
    deltas = jnp.sum(extra[PIECES : 2 * PIECES], axis=0, keepdims=True)
    lanes = lax.broadcasted_iota(jnp.int32, (rows, len(got) * rows), 1)
    earlier = ((lanes // rows + 1) ^ me) < me
    scores = dot_nt(jnp.concatenate([query, key], axis=0), first)
    scores = jnp.where(earlier, scores[:rows] - norm, scores[rows:] - norms)
    probs = jnp.exp2(exponent * scores)
    prob_grad = dot_nt(jnp.concatenate([grad, value], axis=0), second)
    prob_grad = jnp.where(earlier, prob_grad[:rows] - delta, prob_grad[rows:] - deltas)
    score_grad = probs * prob_grad
    sides = jnp.concatenate(
        [jnp.where(earlier, score_grad, 0.0), jnp.where(earlier, 0.0, score_grad)], axis=0
    ).astype(jnp.bfloat16)
    both_sum = dot_nn(sides, first)
    value_sum += dot_nn(jnp.where(earlier, 0.0, probs).astype(jnp.bfloat16), second)
    grads[:, :width] = (scale * (query_sum + both_sum[:rows])).astype(jnp.bfloat16)
    grads[:, width : 2 * width] = (scale * (key_sum + both_sum[rows:])).astype(jnp.bfloat16)
    grads[:, 2 * width :] = value_sum.astype(jnp.bfloat16)
    for copy in copies:
        copy.wait()
    part = outs[0].shape[1]
    cols = math.gcd(part, 512)
    for offset in range(parts - 1, -1, -1):
        start = (head ^ offset) * part
        for at in range(0, part, cols):
            weight = w_all[pl.ds(pl.multiple_of(start + at, cols), cols), :]
            outs[offset][:, at : at + cols] = dot_nt(grads[...], weight).astype(jnp.bfloat16)


def swap(value, axis, offset):
    size = lax.axis_size(axis)
    return lax.ppermute(value, axis, [(at, at ^ offset) for at in range(size)])


def near_body(own, weights, scale):
    rows, width = own[0].shape
    depth = weights[0].shape[0]
    ctx = lax.axis_size("ctx")
    parts = lax.axis_size("head")
    vmem = pl.BlockSpec(memory_space=pltpu.VMEM)
    hbm = pl.BlockSpec(memory_space=pl.ANY)
    params = pltpu.CompilerParams(vmem_limit_bytes=60 * MIB)
    hop = jax.ShapeDtypeStruct((rows + EXTRA, 2 * width), jnp.bfloat16)
    sent = pl.pallas_call(
        send_kernel,
        out_shape=[hop] * (ctx - 1),
        in_specs=[hbm] * 5 + [vmem],
        out_specs=[vmem] * (ctx - 1),
        scratch_shapes=[pltpu.VMEM((rows, width), jnp.bfloat16)] * 5
        + [pltpu.SemaphoreType.DMA((5,))],
        compiler_params=params,
    )(*own)
    got = [swap(value, "ctx", at + 1) for at, value in enumerate(sent)]
    block = jax.ShapeDtypeStruct((rows, depth // parts), jnp.bfloat16)
    blocks = pl.pallas_call(
        functools.partial(near_kernel, scale, parts),
        out_shape=[block] * parts,
        in_specs=[vmem] * 6 + [hbm] * 3 + [vmem] * (ctx - 1),
        out_specs=[vmem] * parts,
        scratch_shapes=[
            pltpu.VMEM((depth, 3 * width), jnp.bfloat16),
            pltpu.VMEM((rows, 3 * width), jnp.bfloat16),
            pltpu.SemaphoreType.DMA((3,)),
        ],
        compiler_params=params,
        cost_estimate=pl.CostEstimate(
            flops=14 * rows * rows * ctx * width + 6 * rows * width * depth,
            bytes_accessed=4 * rows * ctx * width + 6 * depth * width,
            transcendentals=rows * rows * ctx,
        ),
    )(*own, *weights, *got)
    total = blocks[0].astype(jnp.float32)
    for at in range(1, parts):
        total = total + swap(blocks[at], "head", at).astype(jnp.float32)
    return total.astype(jnp.bfloat16)


def far_body(own, weights, scale):
    rows, width = own[0].shape
    depth = weights[0].shape[0]
    ctx = lax.axis_size("ctx")
    parts = lax.axis_size("head")
    spot = lax.axis_index("ctx").astype(jnp.int32).reshape(1)
    vmem = pl.BlockSpec(memory_space=pltpu.VMEM)
    smem = pl.BlockSpec(memory_space=pltpu.SMEM)
    hbm = pl.BlockSpec(memory_space=pl.ANY)
    packed = pl.pallas_call(
        pack_kernel,
        out_shape=jax.ShapeDtypeStruct((ctx, rows + EXTRA, 2 * width), jnp.bfloat16),
        in_specs=[smem] + [vmem] * 6,
        out_specs=vmem,
        compiler_params=pltpu.CompilerParams(vmem_limit_bytes=32 * MIB),
    )(spot, *own)
    got = lax.all_to_all(packed, "ctx", split_axis=0, concat_axis=0, tiled=True)
    total = ctx * rows
    group = math.gcd(ctx, 8)
    parted = pl.pallas_call(
        functools.partial(main_kernel, group, scale),
        out_shape=jax.ShapeDtypeStruct((parts, rows, depth // parts), jnp.bfloat16),
        in_specs=[smem] + [vmem] * 7 + [hbm] * 3,
        out_specs=vmem,
        scratch_shapes=[
            pltpu.VMEM((depth, 3 * width), jnp.bfloat16),
            pltpu.VMEM((rows, 3 * width), jnp.bfloat16),
            pltpu.SemaphoreType.DMA((3,)),
        ],
        compiler_params=pltpu.CompilerParams(vmem_limit_bytes=48 * MIB),
        cost_estimate=pl.CostEstimate(
            flops=14 * rows * total * width + 6 * rows * width * depth,
            bytes_accessed=6 * depth * width + 10 * total * width,
            transcendentals=2 * rows * total,
        ),
    )(spot, got, *own, *weights)
    swapped = lax.all_to_all(parted, "head", split_axis=0, concat_axis=0, tiled=True)
    return jnp.sum(swapped.astype(jnp.float32), axis=0).astype(jnp.bfloat16)


def body(
    queries,
    key_rows,
    value_rows,
    out_grad,
    attn_out,
    log_norm,
    query_weight,
    key_weight,
    value_weight,
):
    rows, width = queries.shape
    ctx, parts = lax.axis_size("ctx"), lax.axis_size("head")
    own = (queries, key_rows, value_rows, out_grad, attn_out, log_norm.reshape(1, rows))
    weights = (query_weight, key_weight, value_weight)
    near = ctx <= 8 and parts <= 4 and ctx & (ctx - 1) == 0 and parts & (parts - 1) == 0
    return (near_body if near else far_body)(own, weights, width ** (-0.5))


def solution(mesh):
    return jax.shard_map(
        body,
        mesh=mesh,
        in_specs=(P("ctx", "head"),) * 6 + (P(None, "head"),) * 3,
        out_specs=P("ctx", "head"),
        check_vma=False,
    )
```

```python
import functools
import math

import jax
import jax.numpy as jnp
from jax import lax
from jax.experimental import pallas as pl
from jax.experimental.pallas import tpu as pltpu
from jax.sharding import PartitionSpec as P

NT = (((1,), (1,)), ((), ()))
TN = (((0,), (0,)), ((), ()))
PIECES = 3
EXTRA = 16
MIB = 1024 * 1024


def dot_nt(left, right):
    return lax.dot_general(left, right, NT, preferred_element_type=jnp.float32)


def dot_tn(left, right):
    return lax.dot_general(left, right, TN, preferred_element_type=jnp.float32)


def dot_nn(left, right):
    return jnp.dot(left, right, preferred_element_type=jnp.float32)


def pieces_of(value):
    out = []
    rest = value
    for _ in range(PIECES):
        low = rest.astype(jnp.bfloat16).astype(jnp.float32)
        out.append(low)
        rest = rest - low
    return out


def diagonal(rows):
    row_at = lax.broadcasted_iota(jnp.int32, (rows, rows), 0)
    col_at = lax.broadcasted_iota(jnp.int32, (rows, rows), 1)
    return row_at == col_at


def delta_of(grad, attn):
    return jnp.sum(grad.astype(jnp.float32) * attn.astype(jnp.float32), axis=1, keepdims=True)


def pack_kernel(me_ref, q_ref, k_ref, v_ref, g_ref, a_ref, n_ref, out_ref):
    rows, width = q_ref.shape
    me = me_ref[0]
    delta = delta_of(g_ref[...], a_ref[...])
    delta = jnp.sum(jnp.where(diagonal(rows), delta, 0.0), axis=0, keepdims=True)
    row = lax.broadcasted_iota(jnp.int32, (EXTRA, rows), 0)
    extra = jnp.zeros((EXTRA, rows), jnp.float32)
    for at, piece in enumerate(pieces_of(n_ref[...]) + pieces_of(delta)):
        extra = jnp.where(row == at, piece, extra)
    extra = extra.astype(jnp.bfloat16)

    def for_later(at, carry):
        out_ref[at, :rows, :width] = k_ref[...]
        out_ref[at, :rows, width:] = v_ref[...]
        out_ref[at, rows:, :] = jnp.zeros((EXTRA, 2 * width), jnp.bfloat16)
        return carry

    def for_earlier(at, carry):
        out_ref[at, :rows, :width] = q_ref[...]
        out_ref[at, :rows, width:] = g_ref[...]
        out_ref[at, rows:, :width] = extra
        out_ref[at, rows:, width:] = jnp.zeros((EXTRA, width), jnp.bfloat16)
        return carry

    lax.fori_loop(0, me + 1, for_earlier, 0)
    lax.fori_loop(me + 1, out_ref.shape[0], for_later, 0)


def main_kernel(
    group,
    scale,
    me_ref,
    got_ref,
    q_ref,
    k_ref,
    v_ref,
    g_ref,
    a_ref,
    n_ref,
    wq_ref,
    wk_ref,
    wv_ref,
    out_ref,
    w_all,
    grads,
    sems,
):
    rows, width = q_ref.shape
    copies = [
        pltpu.make_async_copy(ref, w_all.at[:, at * width : (at + 1) * width], sems.at[at])
        for at, ref in enumerate((wq_ref, wk_ref, wv_ref))
    ]
    for copy in copies:
        copy.start()
    me = me_ref[0]
    exponent = scale * math.log2(math.e)
    query, key, value, grad = q_ref[...], k_ref[...], v_ref[...], g_ref[...]
    eye = diagonal(rows)
    norm = (1.0 / scale) * jnp.sum(jnp.where(eye, n_ref[...], 0.0), axis=1, keepdims=True)
    delta = delta_of(grad, a_ref[...])

    row_at = lax.broadcasted_iota(jnp.int32, (rows, rows), 0)
    col_at = lax.broadcasted_iota(jnp.int32, (rows, rows), 1)
    probs = jnp.where(col_at <= row_at, jnp.exp2(exponent * (dot_nt(query, key) - norm)), 0.0)
    score_low = (probs * (dot_nt(grad, value) - delta)).astype(jnp.bfloat16)
    query_sum = dot_nn(score_low, key)
    key_sum = dot_tn(score_low, query)
    value_sum = dot_tn(probs.astype(jnp.bfloat16), grad)

    first_side = jnp.concatenate([query, key], axis=0)
    second_side = jnp.concatenate([grad, value], axis=0)

    def step(at, sums):
        both_sum, value_sum = sums
        blocks = [at * group + i for i in range(group)]
        first = jnp.concatenate([got_ref[b, :rows, :width] for b in blocks], axis=0)
        second = jnp.concatenate([got_ref[b, :rows, width:] for b in blocks], axis=0)
        extra = jnp.concatenate([got_ref[b, rows:, :width] for b in blocks], axis=1)
        extra = extra.astype(jnp.float32)
        norms = (1.0 / scale) * jnp.sum(extra[:PIECES], axis=0, keepdims=True)
        deltas = jnp.sum(extra[PIECES : 2 * PIECES], axis=0, keepdims=True)
        block = at * group + lax.broadcasted_iota(jnp.int32, (rows, group * rows), 1) // rows
        earlier, later = block < me, block > me
        scores = dot_nt(first_side, first)
        scores = jnp.where(earlier, scores[:rows] - norm, scores[rows:] - norms)
        probs = jnp.exp2(exponent * jnp.where(block == me, 0.0, scores))
        prob_grad = dot_nt(second_side, second)
        prob_grad = jnp.where(earlier, prob_grad[:rows] - delta, prob_grad[rows:] - deltas)
        score_grad = probs * prob_grad
        sides = jnp.concatenate(
            [jnp.where(earlier, score_grad, 0.0), jnp.where(later, score_grad, 0.0)], axis=0
        ).astype(jnp.bfloat16)
        both_sum += dot_nn(sides, first)
        value_sum += dot_nn(jnp.where(later, probs, 0.0).astype(jnp.bfloat16), second)
        return both_sum, value_sum

    sums = (jnp.concatenate([query_sum, key_sum], axis=0), value_sum)
    count = got_ref.shape[0] // group
    if count == 1:
        sums = step(0, sums)
    else:
        sums = lax.fori_loop(0, count, step, sums)
    grads[:, :width] = (scale * sums[0][:rows]).astype(jnp.bfloat16)
    grads[:, width : 2 * width] = (scale * sums[0][rows:]).astype(jnp.bfloat16)
    grads[:, 2 * width :] = sums[1].astype(jnp.bfloat16)
    for copy in copies:
        copy.wait()
    parts, _, part = out_ref.shape
    cols = math.gcd(part, 512)
    for h in range(parts):
        for at in range(0, part, cols):
            weight = w_all[h * part + at : h * part + at + cols, :]
            out_ref[h, :, at : at + cols] = dot_nt(grads[...], weight).astype(jnp.bfloat16)


def split_rows(own_ref, rows):
    return [own_ref[at * rows : (at + 1) * rows, :] for at in range(5)]


def send_kernel(own_ref, n_ref, *hops):
    me = lax.axis_index("ctx")
    rows, width = n_ref.shape[1], own_ref.shape[1]
    query, key, value, grad, attn = split_rows(own_ref, rows)
    delta = delta_of(grad, attn)
    delta = jnp.sum(jnp.where(diagonal(rows), delta, 0.0), axis=0, keepdims=True)
    row = lax.broadcasted_iota(jnp.int32, (EXTRA, rows), 0)
    extra = jnp.zeros((EXTRA, rows), jnp.float32)
    for at, part in enumerate(pieces_of(n_ref[...]) + pieces_of(delta)):
        extra = jnp.where(row == at, part, extra)
    extra = extra.astype(jnp.bfloat16)
    for at, hop in enumerate(hops):
        later = (me ^ (at + 1)) > me

        @pl.when(later)
        def _():
            hop[:rows, :width] = key
            hop[:rows, width:] = value

        @pl.when(jnp.logical_not(later))
        def _():
            hop[:rows, :width] = query
            hop[:rows, width:] = grad

        hop[rows:, :width] = extra
        hop[rows:, width:] = jnp.zeros((EXTRA, width), jnp.bfloat16)


def project(grads, w_ref, start, out_ref):
    part = out_ref.shape[1]
    cols = math.gcd(part, 512)
    for at in range(0, part, cols):
        weight = w_ref[pl.ds(pl.multiple_of(start + at, cols), cols), :]
        out_ref[:, at : at + cols] = dot_nt(grads[...], weight).astype(out_ref.dtype)


def near_kernel(scale, part, own_ref, n_ref, w_ref, *refs):
    grads, front, back = refs[-3:]
    got = refs[:-3]
    rows, width = n_ref.shape[1], own_ref.shape[1]
    me, head = lax.axis_index("ctx"), lax.axis_index("head")
    exponent = scale * math.log2(math.e)
    query, key, value, grad, attn = split_rows(own_ref, rows)
    norm = (1.0 / scale) * jnp.sum(
        jnp.where(diagonal(rows), n_ref[...], 0.0), axis=1, keepdims=True
    )
    delta = delta_of(grad, attn)
    row_at = lax.broadcasted_iota(jnp.int32, (rows, rows), 0)
    col_at = lax.broadcasted_iota(jnp.int32, (rows, rows), 1)
    probs = jnp.where(col_at <= row_at, jnp.exp2(exponent * (dot_nt(query, key) - norm)), 0.0)
    score_low = (probs * (dot_nt(grad, value) - delta)).astype(jnp.bfloat16)
    query_sum = dot_nn(score_low, key)
    key_sum = dot_tn(score_low, query)
    value_sum = dot_tn(probs.astype(jnp.bfloat16), grad)

    first = jnp.concatenate([ref[:rows, :width] for ref in got], axis=0)
    second = jnp.concatenate([ref[:rows, width:] for ref in got], axis=0)
    extra = jnp.concatenate([ref[rows:, :width] for ref in got], axis=1).astype(jnp.float32)
    norms = (1.0 / scale) * jnp.sum(extra[:PIECES], axis=0, keepdims=True)
    deltas = jnp.sum(extra[PIECES : 2 * PIECES], axis=0, keepdims=True)
    lanes = lax.broadcasted_iota(jnp.int32, (rows, len(got) * rows), 1)
    earlier = ((lanes // rows + 1) ^ me) < me
    scores = dot_nt(jnp.concatenate([query, key], axis=0), first)
    scores = jnp.where(earlier, scores[:rows] - norm, scores[rows:] - norms)
    probs = jnp.exp2(exponent * scores)
    prob_grad = dot_nt(jnp.concatenate([grad, value], axis=0), second)
    prob_grad = jnp.where(earlier, prob_grad[:rows] - delta, prob_grad[rows:] - deltas)
    score_grad = probs * prob_grad
    sides = jnp.concatenate(
        [jnp.where(earlier, score_grad, 0.0), jnp.where(earlier, 0.0, score_grad)], axis=0
    ).astype(jnp.bfloat16)
    both_sum = dot_nn(sides, first)
    value_sum += dot_nn(jnp.where(earlier, 0.0, probs).astype(jnp.bfloat16), second)
    grads[:, :width] = (scale * (query_sum + both_sum[:rows])).astype(jnp.bfloat16)
    grads[:, width : 2 * width] = (scale * (key_sum + both_sum[rows:])).astype(jnp.bfloat16)
    grads[:, 2 * width :] = value_sum.astype(jnp.bfloat16)
    start = (head ^ 3) * part
    project(grads, w_ref, start, front)
    project(grads, w_ref, start + part // 2, back)


def rest_kernel(part, grads, w_ref, front, back, near, mine):
    head = lax.axis_index("head")
    project(grads, w_ref, (head ^ 2) * part, front)
    project(grads, w_ref, (head ^ 2) * part + part // 2, back)
    project(grads, w_ref, (head ^ 1) * part, near)
    project(grads, w_ref, head * part, mine)


def swap(value, axis, offset):
    size = lax.axis_size(axis)
    return lax.ppermute(value, axis, [(at, at ^ offset) for at in range(size)])


def near_body(own, weights, scale):
    rows, width = own[0].shape
    depth = weights[0].shape[0]
    ctx = lax.axis_size("ctx")
    part = depth // lax.axis_size("head")
    vmem = pl.BlockSpec(memory_space=pltpu.VMEM)
    params = pltpu.CompilerParams(vmem_limit_bytes=32 * MIB)
    hop = jax.ShapeDtypeStruct((rows + EXTRA, 2 * width), jnp.bfloat16)
    norm = own[-1]
    mine = jnp.concatenate(own[:-1], axis=0)
    weight = jnp.concatenate(weights, axis=1)
    sent = pl.pallas_call(
        send_kernel,
        out_shape=[hop] * (ctx - 1),
        in_specs=[vmem] * 2,
        out_specs=[vmem] * (ctx - 1),
        compiler_params=params,
    )(mine, norm)
    got = {at: swap(sent[at - 1], "ctx", at) for at in range(ctx - 1, 0, -1)}
    got = [got[at] for at in range(1, ctx)]
    half_low = jax.ShapeDtypeStruct((rows, part // 2), jnp.bfloat16)
    half = jax.ShapeDtypeStruct((rows, part // 2), jnp.float32)
    low = jax.ShapeDtypeStruct((rows, part), jnp.bfloat16)
    full = jax.ShapeDtypeStruct((rows, part), jnp.float32)
    grads, front, back = pl.pallas_call(
        functools.partial(near_kernel, scale, part),
        out_shape=[jax.ShapeDtypeStruct((rows, 3 * width), jnp.bfloat16), half_low, half_low],
        in_specs=[vmem] * (ctx + 2),
        out_specs=[vmem] * 3,
        compiler_params=params,
        cost_estimate=pl.CostEstimate(
            flops=14 * rows * rows * ctx * width + 6 * rows * width * part,
            bytes_accessed=4 * rows * ctx * width + 6 * part * width,
            transcendentals=rows * rows * ctx,
        ),
    )(mine, norm, weight, *got)
    front, back = swap(front, "head", 1), swap(back, "head", 1)
    two_front, two_back, near, total = pl.pallas_call(
        functools.partial(rest_kernel, part),
        out_shape=[half, half, low, full],
        in_specs=[vmem] * 2,
        out_specs=[vmem] * 4,
        compiler_params=params,
        cost_estimate=pl.CostEstimate(
            flops=18 * rows * width * part, bytes_accessed=18 * part * width, transcendentals=0
        ),
    )(grads, weight)
    front = swap((two_front + front.astype(jnp.float32)).astype(jnp.bfloat16), "head", 2)
    back = swap((two_back + back.astype(jnp.float32)).astype(jnp.bfloat16), "head", 2)
    near = swap(near, "head", 1)
    far_sum = jnp.concatenate([front, back], axis=1).astype(jnp.float32)
    return (total + near.astype(jnp.float32) + far_sum).astype(jnp.bfloat16)


def far_body(own, weights, scale):
    rows, width = own[0].shape
    depth = weights[0].shape[0]
    ctx = lax.axis_size("ctx")
    parts = lax.axis_size("head")
    spot = lax.axis_index("ctx").astype(jnp.int32).reshape(1)
    vmem = pl.BlockSpec(memory_space=pltpu.VMEM)
    smem = pl.BlockSpec(memory_space=pltpu.SMEM)
    hbm = pl.BlockSpec(memory_space=pl.ANY)
    packed = pl.pallas_call(
        pack_kernel,
        out_shape=jax.ShapeDtypeStruct((ctx, rows + EXTRA, 2 * width), jnp.bfloat16),
        in_specs=[smem] + [vmem] * 6,
        out_specs=vmem,
        compiler_params=pltpu.CompilerParams(vmem_limit_bytes=32 * MIB),
    )(spot, *own)
    got = lax.all_to_all(packed, "ctx", split_axis=0, concat_axis=0, tiled=True)
    total = ctx * rows
    group = math.gcd(ctx, 8)
    parted = pl.pallas_call(
        functools.partial(main_kernel, group, scale),
        out_shape=jax.ShapeDtypeStruct((parts, rows, depth // parts), jnp.bfloat16),
        in_specs=[smem] + [vmem] * 7 + [hbm] * 3,
        out_specs=vmem,
        scratch_shapes=[
            pltpu.VMEM((depth, 3 * width), jnp.bfloat16),
            pltpu.VMEM((rows, 3 * width), jnp.bfloat16),
            pltpu.SemaphoreType.DMA((3,)),
        ],
        compiler_params=pltpu.CompilerParams(vmem_limit_bytes=48 * MIB),
        cost_estimate=pl.CostEstimate(
            flops=14 * rows * total * width + 6 * rows * width * depth,
            bytes_accessed=6 * depth * width + 10 * total * width,
            transcendentals=2 * rows * total,
        ),
    )(spot, got, *own, *weights)
    swapped = lax.all_to_all(parted, "head", split_axis=0, concat_axis=0, tiled=True)
    return jnp.sum(swapped.astype(jnp.float32), axis=0).astype(jnp.bfloat16)


def body(
    queries,
    key_rows,
    value_rows,
    out_grad,
    attn_out,
    log_norm,
    query_weight,
    key_weight,
    value_weight,
):
    rows, width = queries.shape
    ctx, parts = lax.axis_size("ctx"), lax.axis_size("head")
    own = (queries, key_rows, value_rows, out_grad, attn_out, log_norm.reshape(1, rows))
    weights = (query_weight, key_weight, value_weight)
    near = ctx <= 8 and parts == 4 and ctx & (ctx - 1) == 0
    return (near_body if near else far_body)(own, weights, width ** (-0.5))


def solution(mesh):
    return jax.shard_map(
        body,
        mesh=mesh,
        in_specs=(P("ctx", "head"),) * 6 + (P(None, "head"),) * 3,
        out_specs=P("ctx", "head"),
        check_vma=False,
    )
```

```python
import functools
import math

import jax
import jax.numpy as jnp
from jax import lax
from jax.experimental import pallas as pl
from jax.experimental.pallas import tpu as pltpu
from jax.sharding import PartitionSpec as P

NT = (((1,), (1,)), ((), ()))
TN = (((0,), (0,)), ((), ()))
PIECES = 3
EXTRA = 16
MIB = 1024 * 1024


def dot_nt(left, right):
    return lax.dot_general(left, right, NT, preferred_element_type=jnp.float32)


def dot_tn(left, right):
    return lax.dot_general(left, right, TN, preferred_element_type=jnp.float32)


def dot_nn(left, right):
    return jnp.dot(left, right, preferred_element_type=jnp.float32)


def pieces_of(value):
    out = []
    rest = value
    for _ in range(PIECES):
        low = rest.astype(jnp.bfloat16).astype(jnp.float32)
        out.append(low)
        rest = rest - low
    return out


def diagonal(rows):
    row_at = lax.broadcasted_iota(jnp.int32, (rows, rows), 0)
    col_at = lax.broadcasted_iota(jnp.int32, (rows, rows), 1)
    return row_at == col_at


def delta_of(grad, attn):
    return jnp.sum(grad.astype(jnp.float32) * attn.astype(jnp.float32), axis=1, keepdims=True)


def pack_kernel(me_ref, q_ref, k_ref, v_ref, g_ref, a_ref, n_ref, out_ref):
    rows, width = q_ref.shape
    me = me_ref[0]
    delta = delta_of(g_ref[...], a_ref[...])
    delta = jnp.sum(jnp.where(diagonal(rows), delta, 0.0), axis=0, keepdims=True)
    row = lax.broadcasted_iota(jnp.int32, (EXTRA, rows), 0)
    extra = jnp.zeros((EXTRA, rows), jnp.float32)
    for at, piece in enumerate(pieces_of(n_ref[...]) + pieces_of(delta)):
        extra = jnp.where(row == at, piece, extra)
    extra = extra.astype(jnp.bfloat16)

    def for_later(at, carry):
        out_ref[at, :rows, :width] = k_ref[...]
        out_ref[at, :rows, width:] = v_ref[...]
        out_ref[at, rows:, :] = jnp.zeros((EXTRA, 2 * width), jnp.bfloat16)
        return carry

    def for_earlier(at, carry):
        out_ref[at, :rows, :width] = q_ref[...]
        out_ref[at, :rows, width:] = g_ref[...]
        out_ref[at, rows:, :width] = extra
        out_ref[at, rows:, width:] = jnp.zeros((EXTRA, width), jnp.bfloat16)
        return carry

    lax.fori_loop(0, me + 1, for_earlier, 0)
    lax.fori_loop(me + 1, out_ref.shape[0], for_later, 0)


def main_kernel(
    group,
    scale,
    me_ref,
    got_ref,
    q_ref,
    k_ref,
    v_ref,
    g_ref,
    a_ref,
    n_ref,
    wq_ref,
    wk_ref,
    wv_ref,
    out_ref,
    w_all,
    grads,
    sems,
):
    rows, width = q_ref.shape
    copies = [
        pltpu.make_async_copy(ref, w_all.at[:, at * width : (at + 1) * width], sems.at[at])
        for at, ref in enumerate((wq_ref, wk_ref, wv_ref))
    ]
    for copy in copies:
        copy.start()
    me = me_ref[0]
    exponent = scale * math.log2(math.e)
    query, key, value, grad = q_ref[...], k_ref[...], v_ref[...], g_ref[...]
    eye = diagonal(rows)
    norm = (1.0 / scale) * jnp.sum(jnp.where(eye, n_ref[...], 0.0), axis=1, keepdims=True)
    delta = delta_of(grad, a_ref[...])

    row_at = lax.broadcasted_iota(jnp.int32, (rows, rows), 0)
    col_at = lax.broadcasted_iota(jnp.int32, (rows, rows), 1)
    probs = jnp.where(col_at <= row_at, jnp.exp2(exponent * (dot_nt(query, key) - norm)), 0.0)
    score_low = (probs * (dot_nt(grad, value) - delta)).astype(jnp.bfloat16)
    query_sum = dot_nn(score_low, key)
    key_sum = dot_tn(score_low, query)
    value_sum = dot_tn(probs.astype(jnp.bfloat16), grad)

    first_side = jnp.concatenate([query, key], axis=0)
    second_side = jnp.concatenate([grad, value], axis=0)

    def step(at, sums):
        both_sum, value_sum = sums
        blocks = [at * group + i for i in range(group)]
        first = jnp.concatenate([got_ref[b, :rows, :width] for b in blocks], axis=0)
        second = jnp.concatenate([got_ref[b, :rows, width:] for b in blocks], axis=0)
        extra = jnp.concatenate([got_ref[b, rows:, :width] for b in blocks], axis=1)
        extra = extra.astype(jnp.float32)
        norms = (1.0 / scale) * jnp.sum(extra[:PIECES], axis=0, keepdims=True)
        deltas = jnp.sum(extra[PIECES : 2 * PIECES], axis=0, keepdims=True)
        block = at * group + lax.broadcasted_iota(jnp.int32, (rows, group * rows), 1) // rows
        earlier, later = block < me, block > me
        scores = dot_nt(first_side, first)
        scores = jnp.where(earlier, scores[:rows] - norm, scores[rows:] - norms)
        probs = jnp.exp2(exponent * jnp.where(block == me, 0.0, scores))
        prob_grad = dot_nt(second_side, second)
        prob_grad = jnp.where(earlier, prob_grad[:rows] - delta, prob_grad[rows:] - deltas)
        score_grad = probs * prob_grad
        sides = jnp.concatenate(
            [jnp.where(earlier, score_grad, 0.0), jnp.where(later, score_grad, 0.0)], axis=0
        ).astype(jnp.bfloat16)
        both_sum += dot_nn(sides, first)
        value_sum += dot_nn(jnp.where(later, probs, 0.0).astype(jnp.bfloat16), second)
        return both_sum, value_sum

    sums = (jnp.concatenate([query_sum, key_sum], axis=0), value_sum)
    count = got_ref.shape[0] // group
    if count == 1:
        sums = step(0, sums)
    else:
        sums = lax.fori_loop(0, count, step, sums)
    grads[:, :width] = (scale * sums[0][:rows]).astype(jnp.bfloat16)
    grads[:, width : 2 * width] = (scale * sums[0][rows:]).astype(jnp.bfloat16)
    grads[:, 2 * width :] = sums[1].astype(jnp.bfloat16)
    for copy in copies:
        copy.wait()
    parts, _, part = out_ref.shape
    cols = math.gcd(part, 512)
    for h in range(parts):
        for at in range(0, part, cols):
            weight = w_all[h * part + at : h * part + at + cols, :]
            out_ref[h, :, at : at + cols] = dot_nt(grads[...], weight).astype(jnp.bfloat16)


def send_kernel(q_in, k_in, v_in, g_in, a_in, n_ref, *refs):
    q_ref, k_ref, v_ref, g_ref, a_ref, sems = refs[-6:]
    hops = refs[:-6]
    me = lax.axis_index("ctx")
    rows, width = q_ref.shape
    loads = [
        pltpu.make_async_copy(src, dst, sems.at[at])
        for at, (src, dst) in enumerate(
            ((g_in, g_ref), (a_in, a_ref), (k_in, k_ref), (v_in, v_ref), (q_in, q_ref))
        )
    ]
    for load in loads:
        load.start()
    for load in loads:
        load.wait()
    delta = delta_of(g_ref[...], a_ref[...])
    delta = jnp.sum(jnp.where(diagonal(rows), delta, 0.0), axis=0, keepdims=True)
    row = lax.broadcasted_iota(jnp.int32, (EXTRA, rows), 0)
    extra = jnp.zeros((EXTRA, rows), jnp.float32)
    for at, part in enumerate(pieces_of(n_ref[...]) + pieces_of(delta)):
        extra = jnp.where(row == at, part, extra)
    extra = extra.astype(jnp.bfloat16)
    for bit, hop in enumerate(hops):
        later = (me & (1 << bit)) == 0

        @pl.when(later)
        def _():
            hop[:rows, :width] = k_ref[...]
            hop[:rows, width:] = v_ref[...]

        @pl.when(jnp.logical_not(later))
        def _():
            hop[:rows, :width] = q_ref[...]
            hop[:rows, width:] = g_ref[...]

        hop[rows:, :width] = extra
        hop[rows:, width:] = jnp.zeros((EXTRA, width), jnp.bfloat16)


def project(grads, w_ref, start, out_ref):
    part = out_ref.shape[1]
    cols = math.gcd(part, 512)
    for at in range(0, part, cols):
        weight = w_ref[pl.ds(pl.multiple_of(start + at, cols), cols), :]
        out_ref[:, at : at + cols] = dot_nt(grads[...], weight).astype(out_ref.dtype)


def near_kernel(scale, part, q_ref, k_ref, v_ref, g_ref, a_ref, n_ref, w_ref, *refs):
    grads, front, back = refs[-3:]
    got = refs[:-3]
    rows, width = q_ref.shape
    me, head = lax.axis_index("ctx"), lax.axis_index("head")
    exponent = scale * math.log2(math.e)
    query, key, value, grad = q_ref[...], k_ref[...], v_ref[...], g_ref[...]
    norm = (1.0 / scale) * jnp.sum(
        jnp.where(diagonal(rows), n_ref[...], 0.0), axis=1, keepdims=True
    )
    delta = delta_of(grad, a_ref[...])
    row_at = lax.broadcasted_iota(jnp.int32, (rows, rows), 0)
    col_at = lax.broadcasted_iota(jnp.int32, (rows, rows), 1)
    probs = jnp.where(col_at <= row_at, jnp.exp2(exponent * (dot_nt(query, key) - norm)), 0.0)
    score_low = (probs * (dot_nt(grad, value) - delta)).astype(jnp.bfloat16)
    query_sum = dot_nn(score_low, key)
    key_sum = dot_tn(score_low, query)
    value_sum = dot_tn(probs.astype(jnp.bfloat16), grad)

    first = jnp.concatenate([ref[:rows, :width] for ref in got], axis=0)
    second = jnp.concatenate([ref[:rows, width:] for ref in got], axis=0)
    extra = jnp.concatenate([ref[rows:, :width] for ref in got], axis=1).astype(jnp.float32)
    norms = (1.0 / scale) * jnp.sum(extra[:PIECES], axis=0, keepdims=True)
    deltas = jnp.sum(extra[PIECES : 2 * PIECES], axis=0, keepdims=True)
    lanes = lax.broadcasted_iota(jnp.int32, (rows, len(got) * rows), 1)
    earlier = ((lanes // rows + 1) ^ me) < me
    scores = dot_nt(jnp.concatenate([query, key], axis=0), first)
    scores = jnp.where(earlier, scores[:rows] - norm, scores[rows:] - norms)
    probs = jnp.exp2(exponent * scores)
    prob_grad = dot_nt(jnp.concatenate([grad, value], axis=0), second)
    prob_grad = jnp.where(earlier, prob_grad[:rows] - delta, prob_grad[rows:] - deltas)
    score_grad = probs * prob_grad
    sides = jnp.concatenate(
        [jnp.where(earlier, score_grad, 0.0), jnp.where(earlier, 0.0, score_grad)], axis=0
    ).astype(jnp.bfloat16)
    both_sum = dot_nn(sides, first)
    value_sum += dot_nn(jnp.where(earlier, 0.0, probs).astype(jnp.bfloat16), second)
    grads[:, :width] = (scale * (query_sum + both_sum[:rows])).astype(jnp.bfloat16)
    grads[:, width : 2 * width] = (scale * (key_sum + both_sum[rows:])).astype(jnp.bfloat16)
    grads[:, 2 * width :] = value_sum.astype(jnp.bfloat16)
    start = (head ^ 3) * part
    project(grads, w_ref, start, front)
    project(grads, w_ref, start + part // 2, back)


def far_kernel(part, grads, w_ref, front, back):
    start = (lax.axis_index("head") ^ 2) * part
    project(grads, w_ref, start, front)
    project(grads, w_ref, start + part // 2, back)


def close_kernel(part, grads, w_ref, near, mine):
    head = lax.axis_index("head")
    project(grads, w_ref, (head ^ 1) * part, near)
    project(grads, w_ref, head * part, mine)


def swap(value, axis, offset):
    size = lax.axis_size(axis)
    return lax.ppermute(value, axis, [(at, at ^ offset) for at in range(size)])


def near_body(own, weights, scale):
    rows, width = own[0].shape
    depth = weights[0].shape[0]
    ctx = lax.axis_size("ctx")
    part = depth // lax.axis_size("head")
    vmem = pl.BlockSpec(memory_space=pltpu.VMEM)
    hbm = pl.BlockSpec(memory_space=pl.ANY)
    params = pltpu.CompilerParams(vmem_limit_bytes=32 * MIB)
    hop = jax.ShapeDtypeStruct((rows + EXTRA, 2 * width), jnp.bfloat16)
    bits = (ctx - 1).bit_length()
    sent = pl.pallas_call(
        send_kernel,
        out_shape=[hop] * bits,
        in_specs=[hbm] * 5 + [vmem],
        out_specs=[vmem] * bits,
        scratch_shapes=[pltpu.VMEM((rows, width), jnp.bfloat16)] * 5
        + [pltpu.SemaphoreType.DMA((5,))],
        compiler_params=pltpu.CompilerParams(vmem_limit_bytes=60 * MIB),
    )(*own)
    got = {}
    for at in range(ctx - 1, 0, -1):
        got[at] = swap(sent[at.bit_length() - 1], "ctx", at)
    early = tuple(got[at] for at in range(ctx - 1, ctx // 2, -1))
    early, weights = lax.optimization_barrier((early, weights))
    got.update(zip(range(ctx - 1, ctx // 2, -1), early))
    weight = jnp.concatenate(weights, axis=1)
    got = [got[at] for at in range(1, ctx)]
    half_low = jax.ShapeDtypeStruct((rows, part // 2), jnp.bfloat16)
    half = jax.ShapeDtypeStruct((rows, part // 2), jnp.float32)
    low = jax.ShapeDtypeStruct((rows, part), jnp.bfloat16)
    full = jax.ShapeDtypeStruct((rows, part), jnp.float32)
    grads, front, back = pl.pallas_call(
        functools.partial(near_kernel, scale, part),
        out_shape=[jax.ShapeDtypeStruct((rows, 3 * width), jnp.bfloat16), half_low, half_low],
        in_specs=[vmem] * (ctx + 6),
        out_specs=[vmem] * 3,
        compiler_params=params,
        cost_estimate=pl.CostEstimate(
            flops=14 * rows * rows * ctx * width + 6 * rows * width * part,
            bytes_accessed=4 * rows * ctx * width + 6 * part * width,
            transcendentals=rows * rows * ctx,
        ),
    )(*own, weight, *got)
    front, back = swap(front, "head", 1), swap(back, "head", 1)
    def projected(kernel, outs, operands):
        count = sum(out.shape[1] for out in outs)
        return pl.pallas_call(
            functools.partial(kernel, part),
            out_shape=outs,
            in_specs=[vmem] * 2,
            out_specs=[vmem] * 2,
            compiler_params=params,
            cost_estimate=pl.CostEstimate(
                flops=6 * rows * width * count, bytes_accessed=6 * count * width, transcendentals=0
            ),
        )(*operands)

    two_front, two_back = projected(far_kernel, [half, half], (grads, weight))
    near, total = projected(close_kernel, [low, full], (grads, weight))
    near, back = lax.optimization_barrier((near, back))
    front = swap((two_front + front.astype(jnp.float32)).astype(jnp.bfloat16), "head", 2)
    back = swap((two_back + back.astype(jnp.float32)).astype(jnp.bfloat16), "head", 2)
    near = swap(near, "head", 1)
    far_sum = jnp.concatenate([front, back], axis=1).astype(jnp.float32)
    return (total + near.astype(jnp.float32) + far_sum).astype(jnp.bfloat16)


def far_body(own, weights, scale):
    rows, width = own[0].shape
    depth = weights[0].shape[0]
    ctx = lax.axis_size("ctx")
    parts = lax.axis_size("head")
    spot = lax.axis_index("ctx").astype(jnp.int32).reshape(1)
    vmem = pl.BlockSpec(memory_space=pltpu.VMEM)
    smem = pl.BlockSpec(memory_space=pltpu.SMEM)
    hbm = pl.BlockSpec(memory_space=pl.ANY)
    packed = pl.pallas_call(
        pack_kernel,
        out_shape=jax.ShapeDtypeStruct((ctx, rows + EXTRA, 2 * width), jnp.bfloat16),
        in_specs=[smem] + [vmem] * 6,
        out_specs=vmem,
        compiler_params=pltpu.CompilerParams(vmem_limit_bytes=32 * MIB),
    )(spot, *own)
    got = lax.all_to_all(packed, "ctx", split_axis=0, concat_axis=0, tiled=True)
    total = ctx * rows
    group = math.gcd(ctx, 8)
    parted = pl.pallas_call(
        functools.partial(main_kernel, group, scale),
        out_shape=jax.ShapeDtypeStruct((parts, rows, depth // parts), jnp.bfloat16),
        in_specs=[smem] + [vmem] * 7 + [hbm] * 3,
        out_specs=vmem,
        scratch_shapes=[
            pltpu.VMEM((depth, 3 * width), jnp.bfloat16),
            pltpu.VMEM((rows, 3 * width), jnp.bfloat16),
            pltpu.SemaphoreType.DMA((3,)),
        ],
        compiler_params=pltpu.CompilerParams(vmem_limit_bytes=48 * MIB),
        cost_estimate=pl.CostEstimate(
            flops=14 * rows * total * width + 6 * rows * width * depth,
            bytes_accessed=6 * depth * width + 10 * total * width,
            transcendentals=2 * rows * total,
        ),
    )(spot, got, *own, *weights)
    swapped = lax.all_to_all(parted, "head", split_axis=0, concat_axis=0, tiled=True)
    return jnp.sum(swapped.astype(jnp.float32), axis=0).astype(jnp.bfloat16)


def body(
    queries,
    key_rows,
    value_rows,
    out_grad,
    attn_out,
    log_norm,
    query_weight,
    key_weight,
    value_weight,
):
    rows, width = queries.shape
    ctx, parts = lax.axis_size("ctx"), lax.axis_size("head")
    own = (queries, key_rows, value_rows, out_grad, attn_out, log_norm.reshape(1, rows))
    weights = (query_weight, key_weight, value_weight)
    near = ctx <= 8 and parts == 4 and ctx & (ctx - 1) == 0
    return (near_body if near else far_body)(own, weights, width ** (-0.5))


def solution(mesh):
    return jax.shard_map(
        body,
        mesh=mesh,
        in_specs=(P("ctx", "head"),) * 6 + (P(None, "head"),) * 3,
        out_specs=P("ctx", "head"),
        check_vma=False,
    )
```

```python
import functools
import math

import jax
import jax.numpy as jnp
from jax import lax
from jax.experimental import pallas as pl
from jax.experimental.pallas import tpu as pltpu
from jax.sharding import PartitionSpec as P

NT = (((1,), (1,)), ((), ()))
TN = (((0,), (0,)), ((), ()))
PIECES = 3
EXTRA = 16
MIB = 1024 * 1024


def dot_nt(left, right):
    return lax.dot_general(left, right, NT, preferred_element_type=jnp.float32)


def dot_tn(left, right):
    return lax.dot_general(left, right, TN, preferred_element_type=jnp.float32)


def dot_nn(left, right):
    return jnp.dot(left, right, preferred_element_type=jnp.float32)


def pieces_of(value):
    out = []
    rest = value
    for _ in range(PIECES):
        low = rest.astype(jnp.bfloat16).astype(jnp.float32)
        out.append(low)
        rest = rest - low
    return out


def diagonal(rows):
    row_at = lax.broadcasted_iota(jnp.int32, (rows, rows), 0)
    col_at = lax.broadcasted_iota(jnp.int32, (rows, rows), 1)
    return row_at == col_at


def delta_of(grad, attn):
    return jnp.sum(grad.astype(jnp.float32) * attn.astype(jnp.float32), axis=1, keepdims=True)


def pack_kernel(me_ref, q_ref, k_ref, v_ref, g_ref, a_ref, n_ref, out_ref):
    rows, width = q_ref.shape
    me = me_ref[0]
    delta = delta_of(g_ref[...], a_ref[...])
    delta = jnp.sum(jnp.where(diagonal(rows), delta, 0.0), axis=0, keepdims=True)
    row = lax.broadcasted_iota(jnp.int32, (EXTRA, rows), 0)
    extra = jnp.zeros((EXTRA, rows), jnp.float32)
    for at, piece in enumerate(pieces_of(n_ref[...]) + pieces_of(delta)):
        extra = jnp.where(row == at, piece, extra)
    extra = extra.astype(jnp.bfloat16)

    def for_later(at, carry):
        out_ref[at, :rows, :width] = k_ref[...]
        out_ref[at, :rows, width:] = v_ref[...]
        out_ref[at, rows:, :] = jnp.zeros((EXTRA, 2 * width), jnp.bfloat16)
        return carry

    def for_earlier(at, carry):
        out_ref[at, :rows, :width] = q_ref[...]
        out_ref[at, :rows, width:] = g_ref[...]
        out_ref[at, rows:, :width] = extra
        out_ref[at, rows:, width:] = jnp.zeros((EXTRA, width), jnp.bfloat16)
        return carry

    lax.fori_loop(0, me + 1, for_earlier, 0)
    lax.fori_loop(me + 1, out_ref.shape[0], for_later, 0)


def main_kernel(
    group,
    scale,
    me_ref,
    got_ref,
    q_ref,
    k_ref,
    v_ref,
    g_ref,
    a_ref,
    n_ref,
    wq_ref,
    wk_ref,
    wv_ref,
    out_ref,
    w_all,
    grads,
    sems,
):
    rows, width = q_ref.shape
    copies = [
        pltpu.make_async_copy(ref, w_all.at[:, at * width : (at + 1) * width], sems.at[at])
        for at, ref in enumerate((wq_ref, wk_ref, wv_ref))
    ]
    for copy in copies:
        copy.start()
    me = me_ref[0]
    exponent = scale * math.log2(math.e)
    query, key, value, grad = q_ref[...], k_ref[...], v_ref[...], g_ref[...]
    eye = diagonal(rows)
    norm = (1.0 / scale) * jnp.sum(jnp.where(eye, n_ref[...], 0.0), axis=1, keepdims=True)
    delta = delta_of(grad, a_ref[...])

    row_at = lax.broadcasted_iota(jnp.int32, (rows, rows), 0)
    col_at = lax.broadcasted_iota(jnp.int32, (rows, rows), 1)
    probs = jnp.where(col_at <= row_at, jnp.exp2(exponent * (dot_nt(query, key) - norm)), 0.0)
    score_low = (probs * (dot_nt(grad, value) - delta)).astype(jnp.bfloat16)
    query_sum = dot_nn(score_low, key)
    key_sum = dot_tn(score_low, query)
    value_sum = dot_tn(probs.astype(jnp.bfloat16), grad)

    first_side = jnp.concatenate([query, key], axis=0)
    second_side = jnp.concatenate([grad, value], axis=0)

    def step(at, sums):
        both_sum, value_sum = sums
        blocks = [at * group + i for i in range(group)]
        first = jnp.concatenate([got_ref[b, :rows, :width] for b in blocks], axis=0)
        second = jnp.concatenate([got_ref[b, :rows, width:] for b in blocks], axis=0)
        extra = jnp.concatenate([got_ref[b, rows:, :width] for b in blocks], axis=1)
        extra = extra.astype(jnp.float32)
        norms = (1.0 / scale) * jnp.sum(extra[:PIECES], axis=0, keepdims=True)
        deltas = jnp.sum(extra[PIECES : 2 * PIECES], axis=0, keepdims=True)
        block = at * group + lax.broadcasted_iota(jnp.int32, (rows, group * rows), 1) // rows
        earlier, later = block < me, block > me
        scores = dot_nt(first_side, first)
        scores = jnp.where(earlier, scores[:rows] - norm, scores[rows:] - norms)
        probs = jnp.exp2(exponent * jnp.where(block == me, 0.0, scores))
        prob_grad = dot_nt(second_side, second)
        prob_grad = jnp.where(earlier, prob_grad[:rows] - delta, prob_grad[rows:] - deltas)
        score_grad = probs * prob_grad
        sides = jnp.concatenate(
            [jnp.where(earlier, score_grad, 0.0), jnp.where(later, score_grad, 0.0)], axis=0
        ).astype(jnp.bfloat16)
        both_sum += dot_nn(sides, first)
        value_sum += dot_nn(jnp.where(later, probs, 0.0).astype(jnp.bfloat16), second)
        return both_sum, value_sum

    sums = (jnp.concatenate([query_sum, key_sum], axis=0), value_sum)
    count = got_ref.shape[0] // group
    if count == 1:
        sums = step(0, sums)
    else:
        sums = lax.fori_loop(0, count, step, sums)
    grads[:, :width] = (scale * sums[0][:rows]).astype(jnp.bfloat16)
    grads[:, width : 2 * width] = (scale * sums[0][rows:]).astype(jnp.bfloat16)
    grads[:, 2 * width :] = sums[1].astype(jnp.bfloat16)
    for copy in copies:
        copy.wait()
    parts, _, part = out_ref.shape
    cols = math.gcd(part, 512)
    for h in range(parts):
        for at in range(0, part, cols):
            weight = w_all[h * part + at : h * part + at + cols, :]
            out_ref[h, :, at : at + cols] = dot_nt(grads[...], weight).astype(jnp.bfloat16)


def send_kernel(q_in, k_in, v_in, g_in, a_in, n_in, *refs):
    g_ref, a_ref, n_ref, extra_ref, in_sems, row_sems, extra_sems = refs[-7:]
    hops = refs[:-7]
    me = lax.axis_index("ctx")
    rows, width = g_ref.shape
    loads = [
        pltpu.make_async_copy(src, dst, in_sems.at[at])
        for at, (src, dst) in enumerate(((g_in, g_ref), (a_in, a_ref), (n_in, n_ref)))
    ]
    for load in loads:
        load.start()

    def moves(bit, first, second):
        return [
            pltpu.make_async_copy(
                src, hops[bit].at[:rows, at * width : (at + 1) * width], row_sems.at[2 * bit + at]
            )
            for at, src in enumerate((first, second))
        ]

    for bit in range(len(hops)):
        later = (me & (1 << bit)) == 0

        @pl.when(later)
        def _():
            for move in moves(bit, k_in, v_in):
                move.start()

        @pl.when(jnp.logical_not(later))
        def _():
            for move in moves(bit, q_in, g_in):
                move.start()

    for load in loads:
        load.wait()
    delta = delta_of(g_ref[...], a_ref[...])
    delta = jnp.sum(jnp.where(diagonal(rows), delta, 0.0), axis=0, keepdims=True)
    row = lax.broadcasted_iota(jnp.int32, (EXTRA, rows), 0)
    extra = jnp.zeros((EXTRA, rows), jnp.float32)
    for at, part in enumerate(pieces_of(n_ref[...]) + pieces_of(delta)):
        extra = jnp.where(row == at, part, extra)
    extra_ref[:, :width] = extra.astype(jnp.bfloat16)
    extra_ref[:, width:] = jnp.zeros((EXTRA, width), jnp.bfloat16)
    tails = [
        pltpu.make_async_copy(extra_ref, hop.at[rows:, :], extra_sems.at[bit])
        for bit, hop in enumerate(hops)
    ]
    for tail in tails:
        tail.start()
    for bit in range(len(hops)):
        for move in moves(bit, k_in, v_in):
            move.wait()
    for tail in tails:
        tail.wait()


def project(grads, w_ref, start, out_ref):
    part = out_ref.shape[1]
    cols = math.gcd(part, 512)
    for at in range(0, part, cols):
        span = pl.ds(pl.multiple_of(start + at, cols), cols)
        weight = jnp.concatenate([w_ref[i, span, :] for i in range(w_ref.shape[0])], axis=1)
        out_ref[:, at : at + cols] = dot_nt(grads[...], weight).astype(out_ref.dtype)


def near_kernel(scale, part, q_ref, k_ref, v_ref, g_ref, a_ref, n_ref, w_ref, *refs):
    grads, front = refs[-2:]
    got = refs[:-2]
    rows, width = q_ref.shape
    me, head = lax.axis_index("ctx"), lax.axis_index("head")
    exponent = scale * math.log2(math.e)
    query, key, value, grad = q_ref[...], k_ref[...], v_ref[...], g_ref[...]
    norm = (1.0 / scale) * jnp.sum(
        jnp.where(diagonal(rows), n_ref[...], 0.0), axis=1, keepdims=True
    )
    delta = delta_of(grad, a_ref[...])
    row_at = lax.broadcasted_iota(jnp.int32, (rows, rows), 0)
    col_at = lax.broadcasted_iota(jnp.int32, (rows, rows), 1)
    probs = jnp.where(col_at <= row_at, jnp.exp2(exponent * (dot_nt(query, key) - norm)), 0.0)
    score_low = (probs * (dot_nt(grad, value) - delta)).astype(jnp.bfloat16)
    query_sum = dot_nn(score_low, key)
    key_sum = dot_tn(score_low, query)
    value_sum = dot_tn(probs.astype(jnp.bfloat16), grad)

    first = jnp.concatenate([ref[:rows, :width] for ref in got], axis=0)
    second = jnp.concatenate([ref[:rows, width:] for ref in got], axis=0)
    extra = jnp.concatenate([ref[rows:, :width] for ref in got], axis=1).astype(jnp.float32)
    norms = (1.0 / scale) * jnp.sum(extra[:PIECES], axis=0, keepdims=True)
    deltas = jnp.sum(extra[PIECES : 2 * PIECES], axis=0, keepdims=True)
    lanes = lax.broadcasted_iota(jnp.int32, (rows, len(got) * rows), 1)
    earlier = ((lanes // rows + 1) ^ me) < me
    scores = dot_nt(jnp.concatenate([query, key], axis=0), first)
    scores = jnp.where(earlier, scores[:rows] - norm, scores[rows:] - norms)
    probs = jnp.exp2(exponent * scores)
    prob_grad = dot_nt(jnp.concatenate([grad, value], axis=0), second)
    prob_grad = jnp.where(earlier, prob_grad[:rows] - delta, prob_grad[rows:] - deltas)
    score_grad = probs * prob_grad
    sides = jnp.concatenate(
        [jnp.where(earlier, score_grad, 0.0), jnp.where(earlier, 0.0, score_grad)], axis=0
    ).astype(jnp.bfloat16)
    both_sum = dot_nn(sides, first)
    value_sum += dot_nn(jnp.where(earlier, 0.0, probs).astype(jnp.bfloat16), second)
    grads[:, :width] = (scale * (query_sum + both_sum[:rows])).astype(jnp.bfloat16)
    grads[:, width : 2 * width] = (scale * (key_sum + both_sum[rows:])).astype(jnp.bfloat16)
    grads[:, 2 * width :] = value_sum.astype(jnp.bfloat16)
    project(grads, w_ref, (head ^ 3) * part, front)


def far_kernel(part, grads, w_ref, last, front, back):
    head = lax.axis_index("head")
    project(grads, w_ref, (head ^ 3) * part + part // 2, last)
    start = (head ^ 2) * part
    project(grads, w_ref, start, front)
    project(grads, w_ref, start + part // 2, back)


def close_kernel(part, grads, w_ref, near, mine):
    head = lax.axis_index("head")
    project(grads, w_ref, (head ^ 1) * part, near)
    project(grads, w_ref, head * part, mine)


def swap(value, axis, offset):
    size = lax.axis_size(axis)
    return lax.ppermute(value, axis, [(at, at ^ offset) for at in range(size)])


def near_body(own, weights, scale):
    rows, width = own[0].shape
    depth = weights[0].shape[0]
    ctx = lax.axis_size("ctx")
    part = depth // lax.axis_size("head")
    vmem = pl.BlockSpec(memory_space=pltpu.VMEM)
    hbm = pl.BlockSpec(memory_space=pl.ANY)
    params = pltpu.CompilerParams(vmem_limit_bytes=32 * MIB)
    hop = jax.ShapeDtypeStruct((rows + EXTRA, 2 * width), jnp.bfloat16)
    bits = (ctx - 1).bit_length()
    sent = pl.pallas_call(
        send_kernel,
        out_shape=[hop] * bits,
        in_specs=[hbm] * 6,
        out_specs=[hbm] * bits,
        scratch_shapes=[pltpu.VMEM((rows, width), jnp.bfloat16)] * 2
        + [
            pltpu.VMEM((1, rows), jnp.float32),
            pltpu.VMEM((EXTRA, 2 * width), jnp.bfloat16),
            pltpu.SemaphoreType.DMA((3,)),
            pltpu.SemaphoreType.DMA((2 * bits,)),
            pltpu.SemaphoreType.DMA((bits,)),
        ],
        compiler_params=pltpu.CompilerParams(vmem_limit_bytes=60 * MIB),
    )(*own)
    got = {}
    for at in range(ctx - 1, 0, -1):
        got[at] = swap(sent[at.bit_length() - 1], "ctx", at)
    early = tuple(got[at] for at in range(ctx - 1, ctx // 2, -1))
    early, weights = lax.optimization_barrier((early, weights))
    got.update(zip(range(ctx - 1, ctx // 2, -1), early))
    weight = jnp.stack(weights)
    got = [got[at] for at in range(1, ctx)]
    half_low = jax.ShapeDtypeStruct((rows, part // 2), jnp.bfloat16)
    half = jax.ShapeDtypeStruct((rows, part // 2), jnp.float32)
    low = jax.ShapeDtypeStruct((rows, part), jnp.bfloat16)
    full = jax.ShapeDtypeStruct((rows, part), jnp.float32)
    grads, front = pl.pallas_call(
        functools.partial(near_kernel, scale, part),
        out_shape=[jax.ShapeDtypeStruct((rows, 3 * width), jnp.bfloat16), half_low],
        in_specs=[vmem] * (ctx + 6),
        out_specs=[vmem] * 2,
        compiler_params=params,
        cost_estimate=pl.CostEstimate(
            flops=14 * rows * rows * ctx * width + 6 * rows * width * part,
            bytes_accessed=4 * rows * ctx * width + 6 * part * width,
            transcendentals=rows * rows * ctx,
        ),
    )(*own, weight, *got)
    front = swap(front, "head", 1)
    def projected(kernel, outs, operands):
        count = sum(out.shape[1] for out in outs)
        return pl.pallas_call(
            functools.partial(kernel, part),
            out_shape=outs,
            in_specs=[vmem] * 2,
            out_specs=[vmem] * len(outs),
            compiler_params=params,
            cost_estimate=pl.CostEstimate(
                flops=6 * rows * width * count, bytes_accessed=6 * count * width, transcendentals=0
            ),
        )(*operands)

    back, two_front, two_back = projected(far_kernel, [half_low, half, half], (grads, weight))
    back = swap(back, "head", 1)
    near, total = projected(close_kernel, [low, full], (grads, weight))
    near, back = lax.optimization_barrier((near, back))
    front = swap((two_front + front.astype(jnp.float32)).astype(jnp.bfloat16), "head", 2)
    back = swap((two_back + back.astype(jnp.float32)).astype(jnp.bfloat16), "head", 2)
    near = swap(near, "head", 1)
    far_sum = jnp.concatenate([front, back], axis=1).astype(jnp.float32)
    return (total + near.astype(jnp.float32) + far_sum).astype(jnp.bfloat16)


def far_body(own, weights, scale):
    rows, width = own[0].shape
    depth = weights[0].shape[0]
    ctx = lax.axis_size("ctx")
    parts = lax.axis_size("head")
    spot = lax.axis_index("ctx").astype(jnp.int32).reshape(1)
    vmem = pl.BlockSpec(memory_space=pltpu.VMEM)
    smem = pl.BlockSpec(memory_space=pltpu.SMEM)
    hbm = pl.BlockSpec(memory_space=pl.ANY)
    packed = pl.pallas_call(
        pack_kernel,
        out_shape=jax.ShapeDtypeStruct((ctx, rows + EXTRA, 2 * width), jnp.bfloat16),
        in_specs=[smem] + [vmem] * 6,
        out_specs=vmem,
        compiler_params=pltpu.CompilerParams(vmem_limit_bytes=32 * MIB),
    )(spot, *own)
    got = lax.all_to_all(packed, "ctx", split_axis=0, concat_axis=0, tiled=True)
    total = ctx * rows
    group = math.gcd(ctx, 8)
    parted = pl.pallas_call(
        functools.partial(main_kernel, group, scale),
        out_shape=jax.ShapeDtypeStruct((parts, rows, depth // parts), jnp.bfloat16),
        in_specs=[smem] + [vmem] * 7 + [hbm] * 3,
        out_specs=vmem,
        scratch_shapes=[
            pltpu.VMEM((depth, 3 * width), jnp.bfloat16),
            pltpu.VMEM((rows, 3 * width), jnp.bfloat16),
            pltpu.SemaphoreType.DMA((3,)),
        ],
        compiler_params=pltpu.CompilerParams(vmem_limit_bytes=48 * MIB),
        cost_estimate=pl.CostEstimate(
            flops=14 * rows * total * width + 6 * rows * width * depth,
            bytes_accessed=6 * depth * width + 10 * total * width,
            transcendentals=2 * rows * total,
        ),
    )(spot, got, *own, *weights)
    swapped = lax.all_to_all(parted, "head", split_axis=0, concat_axis=0, tiled=True)
    return jnp.sum(swapped.astype(jnp.float32), axis=0).astype(jnp.bfloat16)


def body(
    queries,
    key_rows,
    value_rows,
    out_grad,
    attn_out,
    log_norm,
    query_weight,
    key_weight,
    value_weight,
):
    rows, width = queries.shape
    ctx, parts = lax.axis_size("ctx"), lax.axis_size("head")
    own = (queries, key_rows, value_rows, out_grad, attn_out, log_norm.reshape(1, rows))
    weights = (query_weight, key_weight, value_weight)
    near = ctx <= 8 and parts == 4 and ctx & (ctx - 1) == 0
    return (near_body if near else far_body)(own, weights, width ** (-0.5))


def solution(mesh):
    return jax.shard_map(
        body,
        mesh=mesh,
        in_specs=(P("ctx", "head"),) * 6 + (P(None, "head"),) * 3,
        out_specs=P("ctx", "head"),
        check_vma=False,
    )
```

```python
import functools
import math

import jax
import jax.numpy as jnp
from jax import lax
from jax.experimental import pallas as pl
from jax.experimental.pallas import tpu as pltpu
from jax.sharding import PartitionSpec as P

NT = (((1,), (1,)), ((), ()))
TN = (((0,), (0,)), ((), ()))
PIECES = 3
EXTRA = 16
MIB = 1024 * 1024


def dot_nt(left, right):
    return lax.dot_general(left, right, NT, preferred_element_type=jnp.float32)


def dot_tn(left, right):
    return lax.dot_general(left, right, TN, preferred_element_type=jnp.float32)


def dot_nn(left, right):
    return jnp.dot(left, right, preferred_element_type=jnp.float32)


def pieces_of(value):
    out = []
    rest = value
    for _ in range(PIECES):
        low = rest.astype(jnp.bfloat16).astype(jnp.float32)
        out.append(low)
        rest = rest - low
    return out


def diagonal(rows):
    row_at = lax.broadcasted_iota(jnp.int32, (rows, rows), 0)
    col_at = lax.broadcasted_iota(jnp.int32, (rows, rows), 1)
    return row_at == col_at


def delta_of(grad, attn):
    return jnp.sum(grad.astype(jnp.float32) * attn.astype(jnp.float32), axis=1, keepdims=True)


def pack_kernel(me_ref, q_ref, k_ref, v_ref, g_ref, a_ref, n_ref, out_ref):
    rows, width = q_ref.shape
    me = me_ref[0]
    delta = delta_of(g_ref[...], a_ref[...])
    delta = jnp.sum(jnp.where(diagonal(rows), delta, 0.0), axis=0, keepdims=True)
    row = lax.broadcasted_iota(jnp.int32, (EXTRA, rows), 0)
    extra = jnp.zeros((EXTRA, rows), jnp.float32)
    for at, piece in enumerate(pieces_of(n_ref[...]) + pieces_of(delta)):
        extra = jnp.where(row == at, piece, extra)
    extra = extra.astype(jnp.bfloat16)

    def for_later(at, carry):
        out_ref[at, :rows, :width] = k_ref[...]
        out_ref[at, :rows, width:] = v_ref[...]
        out_ref[at, rows:, :] = jnp.zeros((EXTRA, 2 * width), jnp.bfloat16)
        return carry

    def for_earlier(at, carry):
        out_ref[at, :rows, :width] = q_ref[...]
        out_ref[at, :rows, width:] = g_ref[...]
        out_ref[at, rows:, :width] = extra
        out_ref[at, rows:, width:] = jnp.zeros((EXTRA, width), jnp.bfloat16)
        return carry

    lax.fori_loop(0, me + 1, for_earlier, 0)
    lax.fori_loop(me + 1, out_ref.shape[0], for_later, 0)


def main_kernel(
    group,
    scale,
    me_ref,
    got_ref,
    q_ref,
    k_ref,
    v_ref,
    g_ref,
    a_ref,
    n_ref,
    wq_ref,
    wk_ref,
    wv_ref,
    out_ref,
    w_all,
    grads,
    sems,
):
    rows, width = q_ref.shape
    copies = [
        pltpu.make_async_copy(ref, w_all.at[:, at * width : (at + 1) * width], sems.at[at])
        for at, ref in enumerate((wq_ref, wk_ref, wv_ref))
    ]
    for copy in copies:
        copy.start()
    me = me_ref[0]
    exponent = scale * math.log2(math.e)
    query, key, value, grad = q_ref[...], k_ref[...], v_ref[...], g_ref[...]
    eye = diagonal(rows)
    norm = (1.0 / scale) * jnp.sum(jnp.where(eye, n_ref[...], 0.0), axis=1, keepdims=True)
    delta = delta_of(grad, a_ref[...])

    row_at = lax.broadcasted_iota(jnp.int32, (rows, rows), 0)
    col_at = lax.broadcasted_iota(jnp.int32, (rows, rows), 1)
    probs = jnp.where(col_at <= row_at, jnp.exp2(exponent * (dot_nt(query, key) - norm)), 0.0)
    score_low = (probs * (dot_nt(grad, value) - delta)).astype(jnp.bfloat16)
    query_sum = dot_nn(score_low, key)
    key_sum = dot_tn(score_low, query)
    value_sum = dot_tn(probs.astype(jnp.bfloat16), grad)

    first_side = jnp.concatenate([query, key], axis=0)
    second_side = jnp.concatenate([grad, value], axis=0)

    def step(at, sums):
        both_sum, value_sum = sums
        blocks = [at * group + i for i in range(group)]
        first = jnp.concatenate([got_ref[b, :rows, :width] for b in blocks], axis=0)
        second = jnp.concatenate([got_ref[b, :rows, width:] for b in blocks], axis=0)
        extra = jnp.concatenate([got_ref[b, rows:, :width] for b in blocks], axis=1)
        extra = extra.astype(jnp.float32)
        norms = (1.0 / scale) * jnp.sum(extra[:PIECES], axis=0, keepdims=True)
        deltas = jnp.sum(extra[PIECES : 2 * PIECES], axis=0, keepdims=True)
        block = at * group + lax.broadcasted_iota(jnp.int32, (rows, group * rows), 1) // rows
        earlier, later = block < me, block > me
        scores = dot_nt(first_side, first)
        scores = jnp.where(earlier, scores[:rows] - norm, scores[rows:] - norms)
        probs = jnp.exp2(exponent * jnp.where(block == me, 0.0, scores))
        prob_grad = dot_nt(second_side, second)
        prob_grad = jnp.where(earlier, prob_grad[:rows] - delta, prob_grad[rows:] - deltas)
        score_grad = probs * prob_grad
        sides = jnp.concatenate(
            [jnp.where(earlier, score_grad, 0.0), jnp.where(later, score_grad, 0.0)], axis=0
        ).astype(jnp.bfloat16)
        both_sum += dot_nn(sides, first)
        value_sum += dot_nn(jnp.where(later, probs, 0.0).astype(jnp.bfloat16), second)
        return both_sum, value_sum

    sums = (jnp.concatenate([query_sum, key_sum], axis=0), value_sum)
    count = got_ref.shape[0] // group
    if count == 1:
        sums = step(0, sums)
    else:
        sums = lax.fori_loop(0, count, step, sums)
    grads[:, :width] = (scale * sums[0][:rows]).astype(jnp.bfloat16)
    grads[:, width : 2 * width] = (scale * sums[0][rows:]).astype(jnp.bfloat16)
    grads[:, 2 * width :] = sums[1].astype(jnp.bfloat16)
    for copy in copies:
        copy.wait()
    parts, _, part = out_ref.shape
    cols = math.gcd(part, 512)
    for h in range(parts):
        for at in range(0, part, cols):
            weight = w_all[h * part + at : h * part + at + cols, :]
            out_ref[h, :, at : at + cols] = dot_nt(grads[...], weight).astype(jnp.bfloat16)


def send_kernel(q_in, k_in, v_in, g_in, a_in, n_in, *refs):
    q_ref, k_ref, v_ref, g_ref, a_ref, n_ref, extra_ref, in_sems, row_sems, extra_sems = refs[-10:]
    hops = refs[:-10]
    me = lax.axis_index("ctx")
    rows, width = g_ref.shape
    pairs = (
        (k_in, k_ref),
        (v_in, v_ref),
        (q_in, q_ref),
        (g_in, g_ref),
        (a_in, a_ref),
        (n_in, n_ref),
    )
    loads = [pltpu.make_async_copy(*pair, in_sems.at[at]) for at, pair in enumerate(pairs)]
    for load in loads:
        load.start()

    def moves(bit, first, second):
        return [
            pltpu.make_async_copy(
                src, hops[bit].at[:rows, at * width : (at + 1) * width], row_sems.at[2 * bit + at]
            )
            for at, src in enumerate((first, second))
        ]

    for load in loads:
        load.wait()
    for bit in range(len(hops)):
        later = (me & (1 << bit)) == 0

        @pl.when(later)
        def _():
            for move in moves(bit, k_ref, v_ref):
                move.start()

        @pl.when(jnp.logical_not(later))
        def _():
            for move in moves(bit, q_ref, g_ref):
                move.start()

    delta = delta_of(g_ref[...], a_ref[...])
    delta = jnp.sum(jnp.where(diagonal(rows), delta, 0.0), axis=0, keepdims=True)
    row = lax.broadcasted_iota(jnp.int32, (EXTRA, rows), 0)
    extra = jnp.zeros((EXTRA, rows), jnp.float32)
    for at, part in enumerate(pieces_of(n_ref[...]) + pieces_of(delta)):
        extra = jnp.where(row == at, part, extra)
    extra_ref[:, :width] = extra.astype(jnp.bfloat16)
    extra_ref[:, width:] = jnp.zeros((EXTRA, width), jnp.bfloat16)
    tails = [
        pltpu.make_async_copy(extra_ref, hop.at[rows:, :], extra_sems.at[bit])
        for bit, hop in enumerate(hops)
    ]
    for tail in tails:
        tail.start()
    for bit in range(len(hops)):
        for move in moves(bit, k_ref, v_ref):
            move.wait()
    for tail in tails:
        tail.wait()


def project(grads, w_refs, start, out_ref):
    part = out_ref.shape[1]
    cols = math.gcd(part, 512)
    for at in range(0, part, cols):
        span = pl.ds(pl.multiple_of(start + at, cols), cols)
        weight = jnp.concatenate([ref[span, :] for ref in w_refs], axis=1)
        out_ref[:, at : at + cols] = dot_nt(grads[...], weight).astype(out_ref.dtype)


def near_kernel(scale, q_ref, k_ref, v_ref, g_ref, a_ref, n_ref, w_ref, *refs):
    grads, front = refs[-2:]
    got = refs[:-2]
    rows, width = q_ref.shape
    me = lax.axis_index("ctx")
    exponent = scale * math.log2(math.e)
    query, key, value, grad = q_ref[...], k_ref[...], v_ref[...], g_ref[...]
    norm = (1.0 / scale) * jnp.sum(
        jnp.where(diagonal(rows), n_ref[...], 0.0), axis=1, keepdims=True
    )
    delta = delta_of(grad, a_ref[...])
    row_at = lax.broadcasted_iota(jnp.int32, (rows, rows), 0)
    col_at = lax.broadcasted_iota(jnp.int32, (rows, rows), 1)
    probs = jnp.where(col_at <= row_at, jnp.exp2(exponent * (dot_nt(query, key) - norm)), 0.0)
    score_low = (probs * (dot_nt(grad, value) - delta)).astype(jnp.bfloat16)
    query_sum = dot_nn(score_low, key)
    key_sum = dot_tn(score_low, query)
    value_sum = dot_tn(probs.astype(jnp.bfloat16), grad)

    first = jnp.concatenate([ref[:rows, :width] for ref in got], axis=0)
    second = jnp.concatenate([ref[:rows, width:] for ref in got], axis=0)
    extra = jnp.concatenate([ref[rows:, :width] for ref in got], axis=1).astype(jnp.float32)
    norms = (1.0 / scale) * jnp.sum(extra[:PIECES], axis=0, keepdims=True)
    deltas = jnp.sum(extra[PIECES : 2 * PIECES], axis=0, keepdims=True)
    lanes = lax.broadcasted_iota(jnp.int32, (rows, len(got) * rows), 1)
    earlier = ((lanes // rows + 1) ^ me) < me
    scores = dot_nt(jnp.concatenate([query, key], axis=0), first)
    scores = jnp.where(earlier, scores[:rows] - norm, scores[rows:] - norms)
    probs = jnp.exp2(exponent * scores)
    prob_grad = dot_nt(jnp.concatenate([grad, value], axis=0), second)
    prob_grad = jnp.where(earlier, prob_grad[:rows] - delta, prob_grad[rows:] - deltas)
    score_grad = probs * prob_grad
    sides = jnp.concatenate(
        [jnp.where(earlier, score_grad, 0.0), jnp.where(earlier, 0.0, score_grad)], axis=0
    ).astype(jnp.bfloat16)
    both_sum = dot_nn(sides, first)
    value_sum += dot_nn(jnp.where(earlier, 0.0, probs).astype(jnp.bfloat16), second)
    grads[:, :width] = (scale * (query_sum + both_sum[:rows])).astype(jnp.bfloat16)
    grads[:, width : 2 * width] = (scale * (key_sum + both_sum[rows:])).astype(jnp.bfloat16)
    grads[:, 2 * width :] = value_sum.astype(jnp.bfloat16)
    project(grads, [w_ref.at[at] for at in range(w_ref.shape[0])], 0, front)


def far_kernel(part, grads, wq_ref, wk_ref, wv_ref, last, front, back):
    w_refs = (wq_ref, wk_ref, wv_ref)
    head = lax.axis_index("head")
    project(grads, w_refs, (head ^ 3) * part + part // 2, last)
    start = (head ^ 2) * part
    project(grads, w_refs, start, front)
    project(grads, w_refs, start + part // 2, back)


def close_kernel(part, grads, wq_ref, wk_ref, wv_ref, near, mine):
    w_refs = (wq_ref, wk_ref, wv_ref)
    head = lax.axis_index("head")
    project(grads, w_refs, (head ^ 1) * part, near)
    project(grads, w_refs, head * part, mine)


def swap(value, axis, offset):
    size = lax.axis_size(axis)
    return lax.ppermute(value, axis, [(at, at ^ offset) for at in range(size)])


def near_body(own, weights, scale):
    rows, width = own[0].shape
    depth = weights[0].shape[0]
    ctx = lax.axis_size("ctx")
    part = depth // lax.axis_size("head")
    vmem = pl.BlockSpec(memory_space=pltpu.VMEM)
    hbm = pl.BlockSpec(memory_space=pl.ANY)
    params = pltpu.CompilerParams(vmem_limit_bytes=32 * MIB)
    hop = jax.ShapeDtypeStruct((rows + EXTRA, 2 * width), jnp.bfloat16)
    bits = (ctx - 1).bit_length()
    sent = pl.pallas_call(
        send_kernel,
        out_shape=[hop] * bits,
        in_specs=[hbm] * 6,
        out_specs=[hbm] * bits,
        scratch_shapes=[pltpu.VMEM((rows, width), jnp.bfloat16)] * 5
        + [
            pltpu.VMEM((1, rows), jnp.float32),
            pltpu.VMEM((EXTRA, 2 * width), jnp.bfloat16),
            pltpu.SemaphoreType.DMA((6,)),
            pltpu.SemaphoreType.DMA((2 * bits,)),
            pltpu.SemaphoreType.DMA((bits,)),
        ],
        compiler_params=pltpu.CompilerParams(vmem_limit_bytes=60 * MIB),
    )(*own)
    got = {}
    for at in range(ctx - 1, 0, -1):
        got[at] = swap(sent[at.bit_length() - 1], "ctx", at)
    early = tuple(got[at] for at in range(ctx - 1, ctx // 2, -1))
    early, first_weights = lax.optimization_barrier((early, weights))
    got.update(zip(range(ctx - 1, ctx // 2, -1), early))
    start = (lax.axis_index("head") ^ 3) * part
    weight = jnp.stack(
        [lax.dynamic_slice_in_dim(one, start, part // 2, 0) for one in first_weights]
    )
    got = [got[at] for at in range(1, ctx)]
    half_low = jax.ShapeDtypeStruct((rows, part // 2), jnp.bfloat16)
    half = jax.ShapeDtypeStruct((rows, part // 2), jnp.float32)
    low = jax.ShapeDtypeStruct((rows, part), jnp.bfloat16)
    full = jax.ShapeDtypeStruct((rows, part), jnp.float32)
    grads, front = pl.pallas_call(
        functools.partial(near_kernel, scale),
        out_shape=[jax.ShapeDtypeStruct((rows, 3 * width), jnp.bfloat16), half_low],
        in_specs=[vmem] * (ctx + 6),
        out_specs=[vmem] * 2,
        compiler_params=params,
        cost_estimate=pl.CostEstimate(
            flops=14 * rows * rows * ctx * width + 6 * rows * width * part,
            bytes_accessed=4 * rows * ctx * width + 6 * part * width,
            transcendentals=rows * rows * ctx,
        ),
    )(*own, weight, *got)
    front = swap(front, "head", 1)
    def projected(kernel, outs, operands):
        count = sum(out.shape[1] for out in outs)
        return pl.pallas_call(
            functools.partial(kernel, part),
            out_shape=outs,
            in_specs=[vmem] * (1 + len(weights)),
            out_specs=[vmem] * len(outs),
            compiler_params=params,
            cost_estimate=pl.CostEstimate(
                flops=6 * rows * width * count, bytes_accessed=6 * count * width, transcendentals=0
            ),
        )(*operands)

    back, two_front, two_back = projected(far_kernel, [half_low, half, half], (grads, *weights))
    back = swap(back, "head", 1)
    near, total = projected(close_kernel, [low, full], (grads, *weights))
    near, back = lax.optimization_barrier((near, back))
    front = swap((two_front + front.astype(jnp.float32)).astype(jnp.bfloat16), "head", 2)
    back = swap((two_back + back.astype(jnp.float32)).astype(jnp.bfloat16), "head", 2)
    near = swap(near, "head", 1)
    far_sum = jnp.concatenate([front, back], axis=1).astype(jnp.float32)
    return (total + near.astype(jnp.float32) + far_sum).astype(jnp.bfloat16)


def far_body(own, weights, scale):
    rows, width = own[0].shape
    depth = weights[0].shape[0]
    ctx = lax.axis_size("ctx")
    parts = lax.axis_size("head")
    spot = lax.axis_index("ctx").astype(jnp.int32).reshape(1)
    vmem = pl.BlockSpec(memory_space=pltpu.VMEM)
    smem = pl.BlockSpec(memory_space=pltpu.SMEM)
    hbm = pl.BlockSpec(memory_space=pl.ANY)
    packed = pl.pallas_call(
        pack_kernel,
        out_shape=jax.ShapeDtypeStruct((ctx, rows + EXTRA, 2 * width), jnp.bfloat16),
        in_specs=[smem] + [vmem] * 6,
        out_specs=vmem,
        compiler_params=pltpu.CompilerParams(vmem_limit_bytes=32 * MIB),
    )(spot, *own)
    got = lax.all_to_all(packed, "ctx", split_axis=0, concat_axis=0, tiled=True)
    total = ctx * rows
    group = math.gcd(ctx, 8)
    parted = pl.pallas_call(
        functools.partial(main_kernel, group, scale),
        out_shape=jax.ShapeDtypeStruct((parts, rows, depth // parts), jnp.bfloat16),
        in_specs=[smem] + [vmem] * 7 + [hbm] * 3,
        out_specs=vmem,
        scratch_shapes=[
            pltpu.VMEM((depth, 3 * width), jnp.bfloat16),
            pltpu.VMEM((rows, 3 * width), jnp.bfloat16),
            pltpu.SemaphoreType.DMA((3,)),
        ],
        compiler_params=pltpu.CompilerParams(vmem_limit_bytes=48 * MIB),
        cost_estimate=pl.CostEstimate(
            flops=14 * rows * total * width + 6 * rows * width * depth,
            bytes_accessed=6 * depth * width + 10 * total * width,
            transcendentals=2 * rows * total,
        ),
    )(spot, got, *own, *weights)
    swapped = lax.all_to_all(parted, "head", split_axis=0, concat_axis=0, tiled=True)
    return jnp.sum(swapped.astype(jnp.float32), axis=0).astype(jnp.bfloat16)


def body(
    queries,
    key_rows,
    value_rows,
    out_grad,
    attn_out,
    log_norm,
    query_weight,
    key_weight,
    value_weight,
):
    rows, width = queries.shape
    ctx, parts = lax.axis_size("ctx"), lax.axis_size("head")
    own = (queries, key_rows, value_rows, out_grad, attn_out, log_norm.reshape(1, rows))
    weights = (query_weight, key_weight, value_weight)
    near = ctx <= 8 and parts == 4 and ctx & (ctx - 1) == 0
    return (near_body if near else far_body)(own, weights, width ** (-0.5))


def solution(mesh):
    return jax.shard_map(
        body,
        mesh=mesh,
        in_specs=(P("ctx", "head"),) * 6 + (P(None, "head"),) * 3,
        out_specs=P("ctx", "head"),
        check_vma=False,
    )
```

```python
import functools
import math

import jax
import jax.numpy as jnp
from jax import lax
from jax.experimental import pallas as pl
from jax.experimental.pallas import tpu as pltpu
from jax.sharding import PartitionSpec as P

NT = (((1,), (1,)), ((), ()))
TN = (((0,), (0,)), ((), ()))
PIECES = 3
EXTRA = 16
MIB = 1024 * 1024


def dot_nt(left, right):
    return lax.dot_general(left, right, NT, preferred_element_type=jnp.float32)


def dot_tn(left, right):
    return lax.dot_general(left, right, TN, preferred_element_type=jnp.float32)


def dot_nn(left, right):
    return jnp.dot(left, right, preferred_element_type=jnp.float32)


def pieces_of(value):
    out = []
    rest = value
    for _ in range(PIECES):
        low = rest.astype(jnp.bfloat16).astype(jnp.float32)
        out.append(low)
        rest = rest - low
    return out


def diagonal(rows):
    row_at = lax.broadcasted_iota(jnp.int32, (rows, rows), 0)
    col_at = lax.broadcasted_iota(jnp.int32, (rows, rows), 1)
    return row_at == col_at


def delta_of(grad, attn):
    return jnp.sum(grad.astype(jnp.float32) * attn.astype(jnp.float32), axis=1, keepdims=True)


def pack_kernel(me_ref, q_ref, k_ref, v_ref, g_ref, a_ref, n_ref, out_ref):
    rows, width = q_ref.shape
    me = me_ref[0]
    delta = delta_of(g_ref[...], a_ref[...])
    delta = jnp.sum(jnp.where(diagonal(rows), delta, 0.0), axis=0, keepdims=True)
    row = lax.broadcasted_iota(jnp.int32, (EXTRA, rows), 0)
    extra = jnp.zeros((EXTRA, rows), jnp.float32)
    for at, piece in enumerate(pieces_of(n_ref[...]) + pieces_of(delta)):
        extra = jnp.where(row == at, piece, extra)
    extra = extra.astype(jnp.bfloat16)

    def for_later(at, carry):
        out_ref[at, :rows, :width] = k_ref[...]
        out_ref[at, :rows, width:] = v_ref[...]
        out_ref[at, rows:, :] = jnp.zeros((EXTRA, 2 * width), jnp.bfloat16)
        return carry

    def for_earlier(at, carry):
        out_ref[at, :rows, :width] = q_ref[...]
        out_ref[at, :rows, width:] = g_ref[...]
        out_ref[at, rows:, :width] = extra
        out_ref[at, rows:, width:] = jnp.zeros((EXTRA, width), jnp.bfloat16)
        return carry

    lax.fori_loop(0, me + 1, for_earlier, 0)
    lax.fori_loop(me + 1, out_ref.shape[0], for_later, 0)


def main_kernel(
    group,
    scale,
    me_ref,
    got_ref,
    q_ref,
    k_ref,
    v_ref,
    g_ref,
    a_ref,
    n_ref,
    wq_ref,
    wk_ref,
    wv_ref,
    out_ref,
    w_all,
    grads,
    sems,
):
    rows, width = q_ref.shape
    copies = [
        pltpu.make_async_copy(ref, w_all.at[:, at * width : (at + 1) * width], sems.at[at])
        for at, ref in enumerate((wq_ref, wk_ref, wv_ref))
    ]
    for copy in copies:
        copy.start()
    me = me_ref[0]
    exponent = scale * math.log2(math.e)
    query, key, value, grad = q_ref[...], k_ref[...], v_ref[...], g_ref[...]
    eye = diagonal(rows)
    norm = (1.0 / scale) * jnp.sum(jnp.where(eye, n_ref[...], 0.0), axis=1, keepdims=True)
    delta = delta_of(grad, a_ref[...])

    row_at = lax.broadcasted_iota(jnp.int32, (rows, rows), 0)
    col_at = lax.broadcasted_iota(jnp.int32, (rows, rows), 1)
    probs = jnp.where(col_at <= row_at, jnp.exp2(exponent * (dot_nt(query, key) - norm)), 0.0)
    score_low = (probs * (dot_nt(grad, value) - delta)).astype(jnp.bfloat16)
    query_sum = dot_nn(score_low, key)
    key_sum = dot_tn(score_low, query)
    value_sum = dot_tn(probs.astype(jnp.bfloat16), grad)

    first_side = jnp.concatenate([query, key], axis=0)
    second_side = jnp.concatenate([grad, value], axis=0)

    def step(at, sums):
        both_sum, value_sum = sums
        blocks = [at * group + i for i in range(group)]
        first = jnp.concatenate([got_ref[b, :rows, :width] for b in blocks], axis=0)
        second = jnp.concatenate([got_ref[b, :rows, width:] for b in blocks], axis=0)
        extra = jnp.concatenate([got_ref[b, rows:, :width] for b in blocks], axis=1)
        extra = extra.astype(jnp.float32)
        norms = (1.0 / scale) * jnp.sum(extra[:PIECES], axis=0, keepdims=True)
        deltas = jnp.sum(extra[PIECES : 2 * PIECES], axis=0, keepdims=True)
        block = at * group + lax.broadcasted_iota(jnp.int32, (rows, group * rows), 1) // rows
        earlier, later = block < me, block > me
        scores = dot_nt(first_side, first)
        scores = jnp.where(earlier, scores[:rows] - norm, scores[rows:] - norms)
        probs = jnp.exp2(exponent * jnp.where(block == me, 0.0, scores))
        prob_grad = dot_nt(second_side, second)
        prob_grad = jnp.where(earlier, prob_grad[:rows] - delta, prob_grad[rows:] - deltas)
        score_grad = probs * prob_grad
        sides = jnp.concatenate(
            [jnp.where(earlier, score_grad, 0.0), jnp.where(later, score_grad, 0.0)], axis=0
        ).astype(jnp.bfloat16)
        both_sum += dot_nn(sides, first)
        value_sum += dot_nn(jnp.where(later, probs, 0.0).astype(jnp.bfloat16), second)
        return both_sum, value_sum

    sums = (jnp.concatenate([query_sum, key_sum], axis=0), value_sum)
    count = got_ref.shape[0] // group
    if count == 1:
        sums = step(0, sums)
    else:
        sums = lax.fori_loop(0, count, step, sums)
    grads[:, :width] = (scale * sums[0][:rows]).astype(jnp.bfloat16)
    grads[:, width : 2 * width] = (scale * sums[0][rows:]).astype(jnp.bfloat16)
    grads[:, 2 * width :] = sums[1].astype(jnp.bfloat16)
    for copy in copies:
        copy.wait()
    parts, _, part = out_ref.shape
    cols = math.gcd(part, 512)
    for h in range(parts):
        for at in range(0, part, cols):
            weight = w_all[h * part + at : h * part + at + cols, :]
            out_ref[h, :, at : at + cols] = dot_nt(grads[...], weight).astype(jnp.bfloat16)


def send_kernel(q_in, k_in, v_in, g_in, a_in, n_in, *refs):
    q_ref, k_ref, v_ref, g_ref, a_ref, n_ref, extra_ref, in_sems, row_sems, extra_sems = refs[-10:]
    hops = refs[:-10]
    me = lax.axis_index("ctx")
    rows, width = g_ref.shape
    pairs = (
        (k_in, k_ref),
        (v_in, v_ref),
        (q_in, q_ref),
        (g_in, g_ref),
        (a_in, a_ref),
        (n_in, n_ref),
    )
    loads = [pltpu.make_async_copy(*pair, in_sems.at[at]) for at, pair in enumerate(pairs)]
    for load in loads:
        load.start()

    def moves(bit, first, second):
        return [
            pltpu.make_async_copy(
                src, hops[bit].at[:rows, at * width : (at + 1) * width], row_sems.at[2 * bit + at]
            )
            for at, src in enumerate((first, second))
        ]

    for load in loads:
        load.wait()
    for bit in range(len(hops)):
        later = (me & (1 << bit)) == 0

        @pl.when(later)
        def _():
            for move in moves(bit, k_ref, v_ref):
                move.start()

        @pl.when(jnp.logical_not(later))
        def _():
            for move in moves(bit, q_ref, g_ref):
                move.start()

    delta = delta_of(g_ref[...], a_ref[...])
    delta = jnp.sum(jnp.where(diagonal(rows), delta, 0.0), axis=0, keepdims=True)
    row = lax.broadcasted_iota(jnp.int32, (EXTRA, rows), 0)
    extra = jnp.zeros((EXTRA, rows), jnp.float32)
    for at, part in enumerate(pieces_of(n_ref[...]) + pieces_of(delta)):
        extra = jnp.where(row == at, part, extra)
    extra_ref[:, :width] = extra.astype(jnp.bfloat16)
    extra_ref[:, width:] = jnp.zeros((EXTRA, width), jnp.bfloat16)
    tails = [
        pltpu.make_async_copy(extra_ref, hop.at[rows:, :], extra_sems.at[bit])
        for bit, hop in enumerate(hops)
    ]
    for tail in tails:
        tail.start()
    for bit in range(len(hops)):
        for move in moves(bit, k_ref, v_ref):
            move.wait()
    for tail in tails:
        tail.wait()


def project(grads, w_refs, start, out_ref):
    part = out_ref.shape[1]
    cols = math.gcd(part, 512)
    for at in range(0, part, cols):
        span = pl.ds(pl.multiple_of(start + at, cols), cols)
        weight = jnp.concatenate([ref[span, :] for ref in w_refs], axis=1)
        out_ref[:, at : at + cols] = dot_nt(grads[...], weight).astype(out_ref.dtype)


def near_kernel(scale, q_ref, k_ref, v_ref, g_ref, a_ref, n_ref, w_ref, *refs):
    grads, front = refs[-2:]
    got = refs[:-2]
    rows, width = q_ref.shape
    me = lax.axis_index("ctx")
    exponent = scale * math.log2(math.e)
    query, key, value, grad = q_ref[...], k_ref[...], v_ref[...], g_ref[...]
    norm = (1.0 / scale) * jnp.sum(
        jnp.where(diagonal(rows), n_ref[...], 0.0), axis=1, keepdims=True
    )
    delta = delta_of(grad, a_ref[...])
    row_at = lax.broadcasted_iota(jnp.int32, (rows, rows), 0)
    col_at = lax.broadcasted_iota(jnp.int32, (rows, rows), 1)
    probs = jnp.where(col_at <= row_at, jnp.exp2(exponent * (dot_nt(query, key) - norm)), 0.0)
    score_low = (probs * (dot_nt(grad, value) - delta)).astype(jnp.bfloat16)
    query_sum = dot_nn(score_low, key)
    key_sum = dot_tn(score_low, query)
    value_sum = dot_tn(probs.astype(jnp.bfloat16), grad)

    first = jnp.concatenate([ref[:rows, :width] for ref in got], axis=0)
    second = jnp.concatenate([ref[:rows, width:] for ref in got], axis=0)
    extra = jnp.concatenate([ref[rows:, :width] for ref in got], axis=1).astype(jnp.float32)
    norms = (1.0 / scale) * jnp.sum(extra[:PIECES], axis=0, keepdims=True)
    deltas = jnp.sum(extra[PIECES : 2 * PIECES], axis=0, keepdims=True)
    lanes = lax.broadcasted_iota(jnp.int32, (rows, len(got) * rows), 1)
    earlier = ((lanes // rows + 1) ^ me) < me
    scores = dot_nt(jnp.concatenate([query, key], axis=0), first)
    scores = jnp.where(earlier, scores[:rows] - norm, scores[rows:] - norms)
    probs = jnp.exp2(exponent * scores)
    prob_grad = dot_nt(jnp.concatenate([grad, value], axis=0), second)
    prob_grad = jnp.where(earlier, prob_grad[:rows] - delta, prob_grad[rows:] - deltas)
    score_grad = probs * prob_grad
    sides = jnp.concatenate(
        [jnp.where(earlier, score_grad, 0.0), jnp.where(earlier, 0.0, score_grad)], axis=0
    ).astype(jnp.bfloat16)
    both_sum = dot_nn(sides, first)
    value_sum += dot_nn(jnp.where(earlier, 0.0, probs).astype(jnp.bfloat16), second)
    grads[:, :width] = (scale * (query_sum + both_sum[:rows])).astype(jnp.bfloat16)
    grads[:, width : 2 * width] = (scale * (key_sum + both_sum[rows:])).astype(jnp.bfloat16)
    grads[:, 2 * width :] = value_sum.astype(jnp.bfloat16)
    project(grads, [w_ref.at[at] for at in range(w_ref.shape[0])], 0, front)


def far_kernel(part, grads, wq_ref, wk_ref, wv_ref, last, front, back):
    w_refs = (wq_ref, wk_ref, wv_ref)
    head = lax.axis_index("head")
    project(grads, w_refs, (head ^ 3) * part + part // 2, last)
    start = (head ^ 2) * part
    project(grads, w_refs, start, front)
    project(grads, w_refs, start + part // 2, back)


def close_kernel(part, grads, wq_ref, wk_ref, wv_ref, near, mine):
    w_refs = (wq_ref, wk_ref, wv_ref)
    head = lax.axis_index("head")
    project(grads, w_refs, (head ^ 1) * part, near)
    project(grads, w_refs, head * part, mine)


def swap(value, axis, offset):
    size = lax.axis_size(axis)
    return lax.ppermute(value, axis, [(at, at ^ offset) for at in range(size)])


def near_body(own, weights, scale):
    rows, width = own[0].shape
    depth = weights[0].shape[0]
    ctx = lax.axis_size("ctx")
    part = depth // lax.axis_size("head")
    vmem = pl.BlockSpec(memory_space=pltpu.VMEM)
    hbm = pl.BlockSpec(memory_space=pl.ANY)
    params = pltpu.CompilerParams(vmem_limit_bytes=32 * MIB)
    hop = jax.ShapeDtypeStruct((rows + EXTRA, 2 * width), jnp.bfloat16)
    bits = (ctx - 1).bit_length()
    sent = pl.pallas_call(
        send_kernel,
        out_shape=[hop] * bits,
        in_specs=[hbm] * 6,
        out_specs=[hbm] * bits,
        scratch_shapes=[pltpu.VMEM((rows, width), jnp.bfloat16)] * 5
        + [
            pltpu.VMEM((1, rows), jnp.float32),
            pltpu.VMEM((EXTRA, 2 * width), jnp.bfloat16),
            pltpu.SemaphoreType.DMA((6,)),
            pltpu.SemaphoreType.DMA((2 * bits,)),
            pltpu.SemaphoreType.DMA((bits,)),
        ],
        compiler_params=pltpu.CompilerParams(vmem_limit_bytes=60 * MIB),
    )(*own)
    got = {}
    for at in range(ctx - 1, 0, -1):
        got[at] = swap(sent[at.bit_length() - 1], "ctx", at)
    soon = [at for at in (1, 2, 6) if at < ctx]
    early = tuple(got[at] for at in soon)
    early, first_weights = lax.optimization_barrier((early, weights))
    got.update(zip(soon, early))
    start = (lax.axis_index("head") ^ 3) * part
    weight = jnp.stack(
        [lax.dynamic_slice_in_dim(one, start, part // 2, 0) for one in first_weights]
    )
    got = [got[at] for at in range(1, ctx)]
    half_low = jax.ShapeDtypeStruct((rows, part // 2), jnp.bfloat16)
    half = jax.ShapeDtypeStruct((rows, part // 2), jnp.float32)
    low = jax.ShapeDtypeStruct((rows, part), jnp.bfloat16)
    full = jax.ShapeDtypeStruct((rows, part), jnp.float32)
    grads, front = pl.pallas_call(
        functools.partial(near_kernel, scale),
        out_shape=[jax.ShapeDtypeStruct((rows, 3 * width), jnp.bfloat16), half_low],
        in_specs=[vmem] * (ctx + 6),
        out_specs=[vmem] * 2,
        compiler_params=params,
        cost_estimate=pl.CostEstimate(
            flops=14 * rows * rows * ctx * width + 6 * rows * width * part,
            bytes_accessed=4 * rows * ctx * width + 6 * part * width,
            transcendentals=rows * rows * ctx,
        ),
    )(*own, weight, *got)
    front = swap(front, "head", 1)
    def projected(kernel, outs, operands):
        count = sum(out.shape[1] for out in outs)
        return pl.pallas_call(
            functools.partial(kernel, part),
            out_shape=outs,
            in_specs=[vmem] * (1 + len(weights)),
            out_specs=[vmem] * len(outs),
            compiler_params=params,
            cost_estimate=pl.CostEstimate(
                flops=6 * rows * width * count, bytes_accessed=6 * count * width, transcendentals=0
            ),
        )(*operands)

    back, two_front, two_back = projected(far_kernel, [half_low, half, half], (grads, *weights))
    back = swap(back, "head", 1)
    near, total = projected(close_kernel, [low, full], (grads, *weights))
    near, back = lax.optimization_barrier((near, back))
    front = swap((two_front + front.astype(jnp.float32)).astype(jnp.bfloat16), "head", 2)
    back = swap((two_back + back.astype(jnp.float32)).astype(jnp.bfloat16), "head", 2)
    near = swap(near, "head", 1)
    far_sum = jnp.concatenate([front, back], axis=1).astype(jnp.float32)
    return (total + near.astype(jnp.float32) + far_sum).astype(jnp.bfloat16)


def far_body(own, weights, scale):
    rows, width = own[0].shape
    depth = weights[0].shape[0]
    ctx = lax.axis_size("ctx")
    parts = lax.axis_size("head")
    spot = lax.axis_index("ctx").astype(jnp.int32).reshape(1)
    vmem = pl.BlockSpec(memory_space=pltpu.VMEM)
    smem = pl.BlockSpec(memory_space=pltpu.SMEM)
    hbm = pl.BlockSpec(memory_space=pl.ANY)
    packed = pl.pallas_call(
        pack_kernel,
        out_shape=jax.ShapeDtypeStruct((ctx, rows + EXTRA, 2 * width), jnp.bfloat16),
        in_specs=[smem] + [vmem] * 6,
        out_specs=vmem,
        compiler_params=pltpu.CompilerParams(vmem_limit_bytes=32 * MIB),
    )(spot, *own)
    got = lax.all_to_all(packed, "ctx", split_axis=0, concat_axis=0, tiled=True)
    total = ctx * rows
    group = math.gcd(ctx, 8)
    parted = pl.pallas_call(
        functools.partial(main_kernel, group, scale),
        out_shape=jax.ShapeDtypeStruct((parts, rows, depth // parts), jnp.bfloat16),
        in_specs=[smem] + [vmem] * 7 + [hbm] * 3,
        out_specs=vmem,
        scratch_shapes=[
            pltpu.VMEM((depth, 3 * width), jnp.bfloat16),
            pltpu.VMEM((rows, 3 * width), jnp.bfloat16),
            pltpu.SemaphoreType.DMA((3,)),
        ],
        compiler_params=pltpu.CompilerParams(vmem_limit_bytes=48 * MIB),
        cost_estimate=pl.CostEstimate(
            flops=14 * rows * total * width + 6 * rows * width * depth,
            bytes_accessed=6 * depth * width + 10 * total * width,
            transcendentals=2 * rows * total,
        ),
    )(spot, got, *own, *weights)
    swapped = lax.all_to_all(parted, "head", split_axis=0, concat_axis=0, tiled=True)
    return jnp.sum(swapped.astype(jnp.float32), axis=0).astype(jnp.bfloat16)


def body(
    queries,
    key_rows,
    value_rows,
    out_grad,
    attn_out,
    log_norm,
    query_weight,
    key_weight,
    value_weight,
):
    rows, width = queries.shape
    ctx, parts = lax.axis_size("ctx"), lax.axis_size("head")
    own = (queries, key_rows, value_rows, out_grad, attn_out, log_norm.reshape(1, rows))
    weights = (query_weight, key_weight, value_weight)
    near = ctx <= 8 and parts == 4 and ctx & (ctx - 1) == 0
    return (near_body if near else far_body)(own, weights, width ** (-0.5))


def solution(mesh):
    return jax.shard_map(
        body,
        mesh=mesh,
        in_specs=(P("ctx", "head"),) * 6 + (P(None, "head"),) * 3,
        out_specs=P("ctx", "head"),
        check_vma=False,
    )
```

```python
import functools
import math

import jax
import jax.numpy as jnp
from jax import lax
from jax.experimental import pallas as pl
from jax.experimental.pallas import tpu as pltpu
from jax.sharding import PartitionSpec as P

NT = (((1,), (1,)), ((), ()))
TN = (((0,), (0,)), ((), ()))
PIECES = 3
EXTRA = 16
MIB = 1024 * 1024


def dot_nt(left, right):
    return lax.dot_general(left, right, NT, preferred_element_type=jnp.float32)


def dot_tn(left, right):
    return lax.dot_general(left, right, TN, preferred_element_type=jnp.float32)


def dot_nn(left, right):
    return jnp.dot(left, right, preferred_element_type=jnp.float32)


def pieces_of(value):
    out = []
    rest = value
    for _ in range(PIECES):
        low = rest.astype(jnp.bfloat16).astype(jnp.float32)
        out.append(low)
        rest = rest - low
    return out


def diagonal(rows):
    row_at = lax.broadcasted_iota(jnp.int32, (rows, rows), 0)
    col_at = lax.broadcasted_iota(jnp.int32, (rows, rows), 1)
    return row_at == col_at


def delta_of(grad, attn):
    return jnp.sum(grad.astype(jnp.float32) * attn.astype(jnp.float32), axis=1, keepdims=True)


def pack_kernel(me_ref, q_ref, k_ref, v_ref, g_ref, a_ref, n_ref, out_ref):
    rows, width = q_ref.shape
    me = me_ref[0]
    delta = delta_of(g_ref[...], a_ref[...])
    delta = jnp.sum(jnp.where(diagonal(rows), delta, 0.0), axis=0, keepdims=True)
    row = lax.broadcasted_iota(jnp.int32, (EXTRA, rows), 0)
    extra = jnp.zeros((EXTRA, rows), jnp.float32)
    for at, piece in enumerate(pieces_of(n_ref[...]) + pieces_of(delta)):
        extra = jnp.where(row == at, piece, extra)
    extra = extra.astype(jnp.bfloat16)

    def for_later(at, carry):
        out_ref[at, :rows, :width] = k_ref[...]
        out_ref[at, :rows, width:] = v_ref[...]
        out_ref[at, rows:, :] = jnp.zeros((EXTRA, 2 * width), jnp.bfloat16)
        return carry

    def for_earlier(at, carry):
        out_ref[at, :rows, :width] = q_ref[...]
        out_ref[at, :rows, width:] = g_ref[...]
        out_ref[at, rows:, :width] = extra
        out_ref[at, rows:, width:] = jnp.zeros((EXTRA, width), jnp.bfloat16)
        return carry

    lax.fori_loop(0, me + 1, for_earlier, 0)
    lax.fori_loop(me + 1, out_ref.shape[0], for_later, 0)


def main_kernel(
    group,
    scale,
    me_ref,
    got_ref,
    q_ref,
    k_ref,
    v_ref,
    g_ref,
    a_ref,
    n_ref,
    wq_ref,
    wk_ref,
    wv_ref,
    out_ref,
    w_all,
    grads,
    sems,
):
    rows, width = q_ref.shape
    copies = [
        pltpu.make_async_copy(ref, w_all.at[:, at * width : (at + 1) * width], sems.at[at])
        for at, ref in enumerate((wq_ref, wk_ref, wv_ref))
    ]
    for copy in copies:
        copy.start()
    me = me_ref[0]
    exponent = scale * math.log2(math.e)
    query, key, value, grad = q_ref[...], k_ref[...], v_ref[...], g_ref[...]
    eye = diagonal(rows)
    norm = (1.0 / scale) * jnp.sum(jnp.where(eye, n_ref[...], 0.0), axis=1, keepdims=True)
    delta = delta_of(grad, a_ref[...])

    row_at = lax.broadcasted_iota(jnp.int32, (rows, rows), 0)
    col_at = lax.broadcasted_iota(jnp.int32, (rows, rows), 1)
    probs = jnp.where(col_at <= row_at, jnp.exp2(exponent * (dot_nt(query, key) - norm)), 0.0)
    score_low = (probs * (dot_nt(grad, value) - delta)).astype(jnp.bfloat16)
    query_sum = dot_nn(score_low, key)
    key_sum = dot_tn(score_low, query)
    value_sum = dot_tn(probs.astype(jnp.bfloat16), grad)

    first_side = jnp.concatenate([query, key], axis=0)
    second_side = jnp.concatenate([grad, value], axis=0)

    def step(at, sums):
        both_sum, value_sum = sums
        blocks = [at * group + i for i in range(group)]
        first = jnp.concatenate([got_ref[b, :rows, :width] for b in blocks], axis=0)
        second = jnp.concatenate([got_ref[b, :rows, width:] for b in blocks], axis=0)
        extra = jnp.concatenate([got_ref[b, rows:, :width] for b in blocks], axis=1)
        extra = extra.astype(jnp.float32)
        norms = (1.0 / scale) * jnp.sum(extra[:PIECES], axis=0, keepdims=True)
        deltas = jnp.sum(extra[PIECES : 2 * PIECES], axis=0, keepdims=True)
        block = at * group + lax.broadcasted_iota(jnp.int32, (rows, group * rows), 1) // rows
        earlier, later = block < me, block > me
        scores = dot_nt(first_side, first)
        scores = jnp.where(earlier, scores[:rows] - norm, scores[rows:] - norms)
        probs = jnp.exp2(exponent * jnp.where(block == me, 0.0, scores))
        prob_grad = dot_nt(second_side, second)
        prob_grad = jnp.where(earlier, prob_grad[:rows] - delta, prob_grad[rows:] - deltas)
        score_grad = probs * prob_grad
        sides = jnp.concatenate(
            [jnp.where(earlier, score_grad, 0.0), jnp.where(later, score_grad, 0.0)], axis=0
        ).astype(jnp.bfloat16)
        both_sum += dot_nn(sides, first)
        value_sum += dot_nn(jnp.where(later, probs, 0.0).astype(jnp.bfloat16), second)
        return both_sum, value_sum

    sums = (jnp.concatenate([query_sum, key_sum], axis=0), value_sum)
    count = got_ref.shape[0] // group
    if count == 1:
        sums = step(0, sums)
    else:
        sums = lax.fori_loop(0, count, step, sums)
    grads[:, :width] = (scale * sums[0][:rows]).astype(jnp.bfloat16)
    grads[:, width : 2 * width] = (scale * sums[0][rows:]).astype(jnp.bfloat16)
    grads[:, 2 * width :] = sums[1].astype(jnp.bfloat16)
    for copy in copies:
        copy.wait()
    parts, _, part = out_ref.shape
    cols = math.gcd(part, 512)
    for h in range(parts):
        for at in range(0, part, cols):
            weight = w_all[h * part + at : h * part + at + cols, :]
            out_ref[h, :, at : at + cols] = dot_nt(grads[...], weight).astype(jnp.bfloat16)


def send_kernel(q_in, k_in, v_in, g_in, a_in, n_in, *refs):
    q_ref, k_ref, v_ref, g_ref, a_ref, n_ref, extra_ref, in_sems, row_sems, extra_sems = refs[-10:]
    hops = refs[:-10]
    me = lax.axis_index("ctx")
    rows, width = g_ref.shape
    pairs = (
        (k_in, k_ref),
        (v_in, v_ref),
        (q_in, q_ref),
        (g_in, g_ref),
        (a_in, a_ref),
        (n_in, n_ref),
    )
    loads = [pltpu.make_async_copy(*pair, in_sems.at[at]) for at, pair in enumerate(pairs)]
    for load in loads:
        load.start()

    def moves(bit, first, second):
        return [
            pltpu.make_async_copy(
                src, hops[bit].at[:rows, at * width : (at + 1) * width], row_sems.at[2 * bit + at]
            )
            for at, src in enumerate((first, second))
        ]

    for load in loads:
        load.wait()
    for bit in range(len(hops)):
        later = (me & (1 << bit)) == 0

        @pl.when(later)
        def _():
            for move in moves(bit, k_ref, v_ref):
                move.start()

        @pl.when(jnp.logical_not(later))
        def _():
            for move in moves(bit, q_ref, g_ref):
                move.start()

    delta = delta_of(g_ref[...], a_ref[...])
    delta = jnp.sum(jnp.where(diagonal(rows), delta, 0.0), axis=0, keepdims=True)
    row = lax.broadcasted_iota(jnp.int32, (EXTRA, rows), 0)
    extra = jnp.zeros((EXTRA, rows), jnp.float32)
    for at, part in enumerate(pieces_of(n_ref[...]) + pieces_of(delta)):
        extra = jnp.where(row == at, part, extra)
    extra_ref[:, :width] = extra.astype(jnp.bfloat16)
    extra_ref[:, width:] = jnp.zeros((EXTRA, width), jnp.bfloat16)
    tails = [
        pltpu.make_async_copy(extra_ref, hop.at[rows:, :], extra_sems.at[bit])
        for bit, hop in enumerate(hops)
    ]
    for tail in tails:
        tail.start()
    for bit in range(len(hops)):
        for move in moves(bit, k_ref, v_ref):
            move.wait()
    for tail in tails:
        tail.wait()


def project(grads, w_refs, start, out_ref):
    part = out_ref.shape[1]
    cols = math.gcd(part, 512)
    for at in range(0, part, cols):
        span = pl.ds(pl.multiple_of(start + at, cols), cols)
        weight = jnp.concatenate([ref[span, :] for ref in w_refs], axis=1)
        out_ref[:, at : at + cols] = dot_nt(grads[...], weight).astype(out_ref.dtype)


def near_kernel(scale, q_ref, k_ref, v_ref, g_ref, a_ref, n_ref, w_ref, *refs):
    grads, front = refs[-2:]
    got = refs[:-2]
    rows, width = q_ref.shape
    me = lax.axis_index("ctx")
    exponent = scale * math.log2(math.e)
    query, key, value, grad = q_ref[...], k_ref[...], v_ref[...], g_ref[...]
    norm = (1.0 / scale) * jnp.sum(
        jnp.where(diagonal(rows), n_ref[...], 0.0), axis=1, keepdims=True
    )
    delta = delta_of(grad, a_ref[...])
    row_at = lax.broadcasted_iota(jnp.int32, (rows, rows), 0)
    col_at = lax.broadcasted_iota(jnp.int32, (rows, rows), 1)
    probs = jnp.where(col_at <= row_at, jnp.exp2(exponent * (dot_nt(query, key) - norm)), 0.0)
    score_low = (probs * (dot_nt(grad, value) - delta)).astype(jnp.bfloat16)
    query_sum = dot_nn(score_low, key)
    key_sum = dot_tn(score_low, query)
    value_sum = dot_tn(probs.astype(jnp.bfloat16), grad)

    first = jnp.concatenate([ref[:rows, :width] for ref in got], axis=0)
    second = jnp.concatenate([ref[:rows, width:] for ref in got], axis=0)
    extra = jnp.concatenate([ref[rows:, :width] for ref in got], axis=1).astype(jnp.float32)
    norms = (1.0 / scale) * jnp.sum(extra[:PIECES], axis=0, keepdims=True)
    deltas = jnp.sum(extra[PIECES : 2 * PIECES], axis=0, keepdims=True)
    lanes = lax.broadcasted_iota(jnp.int32, (rows, len(got) * rows), 1)
    earlier = ((lanes // rows + 1) ^ me) < me
    scores = dot_nt(jnp.concatenate([query, key], axis=0), first)
    scores = jnp.where(earlier, scores[:rows] - norm, scores[rows:] - norms)
    probs = jnp.exp2(exponent * scores)
    prob_grad = dot_nt(jnp.concatenate([grad, value], axis=0), second)
    prob_grad = jnp.where(earlier, prob_grad[:rows] - delta, prob_grad[rows:] - deltas)
    score_grad = probs * prob_grad
    sides = jnp.concatenate(
        [jnp.where(earlier, score_grad, 0.0), jnp.where(earlier, 0.0, score_grad)], axis=0
    ).astype(jnp.bfloat16)
    both_sum = dot_nn(sides, first)
    value_sum += dot_nn(jnp.where(earlier, 0.0, probs).astype(jnp.bfloat16), second)
    grads[:, :width] = (scale * (query_sum + both_sum[:rows])).astype(jnp.bfloat16)
    grads[:, width : 2 * width] = (scale * (key_sum + both_sum[rows:])).astype(jnp.bfloat16)
    grads[:, 2 * width :] = value_sum.astype(jnp.bfloat16)
    project(grads, [w_ref.at[at] for at in range(w_ref.shape[0])], 0, front)


def far_kernel(part, grads, wq_ref, wk_ref, wv_ref, last, front, back):
    w_refs = (wq_ref, wk_ref, wv_ref)
    head = lax.axis_index("head")
    project(grads, w_refs, (head ^ 3) * part + part // 2, last)
    start = (head ^ 2) * part
    project(grads, w_refs, start, front)
    project(grads, w_refs, start + part // 2, back)


def close_kernel(part, grads, wq_ref, wk_ref, wv_ref, near, mine):
    w_refs = (wq_ref, wk_ref, wv_ref)
    head = lax.axis_index("head")
    project(grads, w_refs, (head ^ 1) * part, near)
    project(grads, w_refs, head * part, mine)


def swap(value, axis, offset):
    size = lax.axis_size(axis)
    return lax.ppermute(value, axis, [(at, at ^ offset) for at in range(size)])


def near_body(own, weights, scale):
    rows, width = own[0].shape
    depth = weights[0].shape[0]
    ctx = lax.axis_size("ctx")
    part = depth // lax.axis_size("head")
    vmem = pl.BlockSpec(memory_space=pltpu.VMEM)
    hbm = pl.BlockSpec(memory_space=pl.ANY)
    params = pltpu.CompilerParams(vmem_limit_bytes=32 * MIB)
    hop = jax.ShapeDtypeStruct((rows + EXTRA, 2 * width), jnp.bfloat16)
    bits = (ctx - 1).bit_length()
    sent = pl.pallas_call(
        send_kernel,
        out_shape=[hop] * bits,
        in_specs=[hbm] * 6,
        out_specs=[hbm] * bits,
        scratch_shapes=[pltpu.VMEM((rows, width), jnp.bfloat16)] * 5
        + [
            pltpu.VMEM((1, rows), jnp.float32),
            pltpu.VMEM((EXTRA, 2 * width), jnp.bfloat16),
            pltpu.SemaphoreType.DMA((6,)),
            pltpu.SemaphoreType.DMA((2 * bits,)),
            pltpu.SemaphoreType.DMA((bits,)),
        ],
        compiler_params=pltpu.CompilerParams(vmem_limit_bytes=60 * MIB),
    )(*own)
    got = {}
    for at in range(ctx - 1, 0, -1):
        got[at] = swap(sent[at.bit_length() - 1], "ctx", at)
    soon = [at for at in (1, 6, 4, 7, 5) if at < ctx]
    early = tuple(got[at] for at in soon)
    early, first_weights = lax.optimization_barrier((early, weights))
    got.update(zip(soon, early))
    start = (lax.axis_index("head") ^ 3) * part
    weight = jnp.stack(
        [lax.dynamic_slice_in_dim(one, start, part // 2, 0) for one in first_weights]
    )
    got = [got[at] for at in range(1, ctx)]
    half_low = jax.ShapeDtypeStruct((rows, part // 2), jnp.bfloat16)
    half = jax.ShapeDtypeStruct((rows, part // 2), jnp.float32)
    low = jax.ShapeDtypeStruct((rows, part), jnp.bfloat16)
    full = jax.ShapeDtypeStruct((rows, part), jnp.float32)
    grads, front = pl.pallas_call(
        functools.partial(near_kernel, scale),
        out_shape=[jax.ShapeDtypeStruct((rows, 3 * width), jnp.bfloat16), half_low],
        in_specs=[vmem] * (ctx + 6),
        out_specs=[vmem] * 2,
        compiler_params=params,
        cost_estimate=pl.CostEstimate(
            flops=14 * rows * rows * ctx * width + 6 * rows * width * part,
            bytes_accessed=4 * rows * ctx * width + 6 * part * width,
            transcendentals=rows * rows * ctx,
        ),
    )(*own, weight, *got)
    front = swap(front, "head", 1)
    def projected(kernel, outs, operands):
        count = sum(out.shape[1] for out in outs)
        return pl.pallas_call(
            functools.partial(kernel, part),
            out_shape=outs,
            in_specs=[vmem] * (1 + len(weights)),
            out_specs=[vmem] * len(outs),
            compiler_params=params,
            cost_estimate=pl.CostEstimate(
                flops=6 * rows * width * count, bytes_accessed=6 * count * width, transcendentals=0
            ),
        )(*operands)

    back, two_front, two_back = projected(far_kernel, [half_low, half, half], (grads, *weights))
    back = swap(back, "head", 1)
    near, total = projected(close_kernel, [low, full], (grads, *weights))
    near, back = lax.optimization_barrier((near, back))
    front = swap((two_front + front.astype(jnp.float32)).astype(jnp.bfloat16), "head", 2)
    back = swap((two_back + back.astype(jnp.float32)).astype(jnp.bfloat16), "head", 2)
    near = swap(near, "head", 1)
    far_sum = jnp.concatenate([front, back], axis=1).astype(jnp.float32)
    return (total + near.astype(jnp.float32) + far_sum).astype(jnp.bfloat16)


def far_body(own, weights, scale):
    rows, width = own[0].shape
    depth = weights[0].shape[0]
    ctx = lax.axis_size("ctx")
    parts = lax.axis_size("head")
    spot = lax.axis_index("ctx").astype(jnp.int32).reshape(1)
    vmem = pl.BlockSpec(memory_space=pltpu.VMEM)
    smem = pl.BlockSpec(memory_space=pltpu.SMEM)
    hbm = pl.BlockSpec(memory_space=pl.ANY)
    packed = pl.pallas_call(
        pack_kernel,
        out_shape=jax.ShapeDtypeStruct((ctx, rows + EXTRA, 2 * width), jnp.bfloat16),
        in_specs=[smem] + [vmem] * 6,
        out_specs=vmem,
        compiler_params=pltpu.CompilerParams(vmem_limit_bytes=32 * MIB),
    )(spot, *own)
    got = lax.all_to_all(packed, "ctx", split_axis=0, concat_axis=0, tiled=True)
    total = ctx * rows
    group = math.gcd(ctx, 8)
    parted = pl.pallas_call(
        functools.partial(main_kernel, group, scale),
        out_shape=jax.ShapeDtypeStruct((parts, rows, depth // parts), jnp.bfloat16),
        in_specs=[smem] + [vmem] * 7 + [hbm] * 3,
        out_specs=vmem,
        scratch_shapes=[
            pltpu.VMEM((depth, 3 * width), jnp.bfloat16),
            pltpu.VMEM((rows, 3 * width), jnp.bfloat16),
            pltpu.SemaphoreType.DMA((3,)),
        ],
        compiler_params=pltpu.CompilerParams(vmem_limit_bytes=48 * MIB),
        cost_estimate=pl.CostEstimate(
            flops=14 * rows * total * width + 6 * rows * width * depth,
            bytes_accessed=6 * depth * width + 10 * total * width,
            transcendentals=2 * rows * total,
        ),
    )(spot, got, *own, *weights)
    swapped = lax.all_to_all(parted, "head", split_axis=0, concat_axis=0, tiled=True)
    return jnp.sum(swapped.astype(jnp.float32), axis=0).astype(jnp.bfloat16)


def body(
    queries,
    key_rows,
    value_rows,
    out_grad,
    attn_out,
    log_norm,
    query_weight,
    key_weight,
    value_weight,
):
    rows, width = queries.shape
    ctx, parts = lax.axis_size("ctx"), lax.axis_size("head")
    own = (queries, key_rows, value_rows, out_grad, attn_out, log_norm.reshape(1, rows))
    weights = (query_weight, key_weight, value_weight)
    near = ctx <= 8 and parts == 4 and ctx & (ctx - 1) == 0
    return (near_body if near else far_body)(own, weights, width ** (-0.5))


def solution(mesh):
    return jax.shard_map(
        body,
        mesh=mesh,
        in_specs=(P("ctx", "head"),) * 6 + (P(None, "head"),) * 3,
        out_specs=P("ctx", "head"),
        check_vma=False,
    )
```

```python
import functools
import math

import jax
import jax.numpy as jnp
from jax import lax
from jax.experimental import pallas as pl
from jax.experimental.pallas import tpu as pltpu
from jax.sharding import PartitionSpec as P

NT = (((1,), (1,)), ((), ()))
TN = (((0,), (0,)), ((), ()))
PIECES = 3
EXTRA = 16
MIB = 1024 * 1024


def dot_nt(left, right):
    return lax.dot_general(left, right, NT, preferred_element_type=jnp.float32)


def dot_tn(left, right):
    return lax.dot_general(left, right, TN, preferred_element_type=jnp.float32)


def dot_nn(left, right):
    return jnp.dot(left, right, preferred_element_type=jnp.float32)


def pieces_of(value):
    out = []
    rest = value
    for _ in range(PIECES):
        low = rest.astype(jnp.bfloat16).astype(jnp.float32)
        out.append(low)
        rest = rest - low
    return out


def diagonal(rows):
    row_at = lax.broadcasted_iota(jnp.int32, (rows, rows), 0)
    col_at = lax.broadcasted_iota(jnp.int32, (rows, rows), 1)
    return row_at == col_at


def delta_of(grad, attn):
    return jnp.sum(grad.astype(jnp.float32) * attn.astype(jnp.float32), axis=1, keepdims=True)


def pack_kernel(me_ref, q_ref, k_ref, v_ref, g_ref, a_ref, n_ref, out_ref):
    rows, width = q_ref.shape
    me = me_ref[0]
    delta = delta_of(g_ref[...], a_ref[...])
    delta = jnp.sum(jnp.where(diagonal(rows), delta, 0.0), axis=0, keepdims=True)
    row = lax.broadcasted_iota(jnp.int32, (EXTRA, rows), 0)
    extra = jnp.zeros((EXTRA, rows), jnp.float32)
    for at, piece in enumerate(pieces_of(n_ref[...]) + pieces_of(delta)):
        extra = jnp.where(row == at, piece, extra)
    extra = extra.astype(jnp.bfloat16)

    def for_later(at, carry):
        out_ref[at, :rows, :width] = k_ref[...]
        out_ref[at, :rows, width:] = v_ref[...]
        out_ref[at, rows:, :] = jnp.zeros((EXTRA, 2 * width), jnp.bfloat16)
        return carry

    def for_earlier(at, carry):
        out_ref[at, :rows, :width] = q_ref[...]
        out_ref[at, :rows, width:] = g_ref[...]
        out_ref[at, rows:, :width] = extra
        out_ref[at, rows:, width:] = jnp.zeros((EXTRA, width), jnp.bfloat16)
        return carry

    lax.fori_loop(0, me + 1, for_earlier, 0)
    lax.fori_loop(me + 1, out_ref.shape[0], for_later, 0)


def main_kernel(
    group,
    scale,
    me_ref,
    got_ref,
    q_ref,
    k_ref,
    v_ref,
    g_ref,
    a_ref,
    n_ref,
    wq_ref,
    wk_ref,
    wv_ref,
    out_ref,
    w_all,
    grads,
    sems,
):
    rows, width = q_ref.shape
    copies = [
        pltpu.make_async_copy(ref, w_all.at[:, at * width : (at + 1) * width], sems.at[at])
        for at, ref in enumerate((wq_ref, wk_ref, wv_ref))
    ]
    for copy in copies:
        copy.start()
    me = me_ref[0]
    exponent = scale * math.log2(math.e)
    query, key, value, grad = q_ref[...], k_ref[...], v_ref[...], g_ref[...]
    eye = diagonal(rows)
    norm = (1.0 / scale) * jnp.sum(jnp.where(eye, n_ref[...], 0.0), axis=1, keepdims=True)
    delta = delta_of(grad, a_ref[...])

    row_at = lax.broadcasted_iota(jnp.int32, (rows, rows), 0)
    col_at = lax.broadcasted_iota(jnp.int32, (rows, rows), 1)
    probs = jnp.where(col_at <= row_at, jnp.exp2(exponent * (dot_nt(query, key) - norm)), 0.0)
    score_low = (probs * (dot_nt(grad, value) - delta)).astype(jnp.bfloat16)
    query_sum = dot_nn(score_low, key)
    key_sum = dot_tn(score_low, query)
    value_sum = dot_tn(probs.astype(jnp.bfloat16), grad)

    first_side = jnp.concatenate([query, key], axis=0)
    second_side = jnp.concatenate([grad, value], axis=0)

    def step(at, sums):
        both_sum, value_sum = sums
        blocks = [at * group + i for i in range(group)]
        first = jnp.concatenate([got_ref[b, :rows, :width] for b in blocks], axis=0)
        second = jnp.concatenate([got_ref[b, :rows, width:] for b in blocks], axis=0)
        extra = jnp.concatenate([got_ref[b, rows:, :width] for b in blocks], axis=1)
        extra = extra.astype(jnp.float32)
        norms = (1.0 / scale) * jnp.sum(extra[:PIECES], axis=0, keepdims=True)
        deltas = jnp.sum(extra[PIECES : 2 * PIECES], axis=0, keepdims=True)
        block = at * group + lax.broadcasted_iota(jnp.int32, (rows, group * rows), 1) // rows
        earlier, later = block < me, block > me
        scores = dot_nt(first_side, first)
        scores = jnp.where(earlier, scores[:rows] - norm, scores[rows:] - norms)
        probs = jnp.exp2(exponent * jnp.where(block == me, 0.0, scores))
        prob_grad = dot_nt(second_side, second)
        prob_grad = jnp.where(earlier, prob_grad[:rows] - delta, prob_grad[rows:] - deltas)
        score_grad = probs * prob_grad
        sides = jnp.concatenate(
            [jnp.where(earlier, score_grad, 0.0), jnp.where(later, score_grad, 0.0)], axis=0
        ).astype(jnp.bfloat16)
        both_sum += dot_nn(sides, first)
        value_sum += dot_nn(jnp.where(later, probs, 0.0).astype(jnp.bfloat16), second)
        return both_sum, value_sum

    sums = (jnp.concatenate([query_sum, key_sum], axis=0), value_sum)
    count = got_ref.shape[0] // group
    if count == 1:
        sums = step(0, sums)
    else:
        sums = lax.fori_loop(0, count, step, sums)
    grads[:, :width] = (scale * sums[0][:rows]).astype(jnp.bfloat16)
    grads[:, width : 2 * width] = (scale * sums[0][rows:]).astype(jnp.bfloat16)
    grads[:, 2 * width :] = sums[1].astype(jnp.bfloat16)
    for copy in copies:
        copy.wait()
    parts, _, part = out_ref.shape
    cols = math.gcd(part, 512)
    for h in range(parts):
        for at in range(0, part, cols):
            weight = w_all[h * part + at : h * part + at + cols, :]
            out_ref[h, :, at : at + cols] = dot_nt(grads[...], weight).astype(jnp.bfloat16)


def send_kernel(q_in, k_in, v_in, g_in, a_in, n_in, *refs):
    q_ref, k_ref, v_ref, g_ref, a_ref, n_ref, extra_ref, in_sems, row_sems, extra_sems = refs[-10:]
    hops = refs[:-10]
    me = lax.axis_index("ctx")
    rows, width = g_ref.shape
    pairs = (
        (k_in, k_ref),
        (v_in, v_ref),
        (q_in, q_ref),
        (g_in, g_ref),
        (a_in, a_ref),
        (n_in, n_ref),
    )
    loads = [pltpu.make_async_copy(*pair, in_sems.at[at]) for at, pair in enumerate(pairs)]
    for load in loads:
        load.start()

    def moves(bit, first, second):
        return [
            pltpu.make_async_copy(
                src, hops[bit].at[:rows, at * width : (at + 1) * width], row_sems.at[2 * bit + at]
            )
            for at, src in enumerate((first, second))
        ]

    for load in loads:
        load.wait()
    for bit in range(len(hops)):
        later = (me & (1 << bit)) == 0

        @pl.when(later)
        def _():
            for move in moves(bit, k_ref, v_ref):
                move.start()

        @pl.when(jnp.logical_not(later))
        def _():
            for move in moves(bit, q_ref, g_ref):
                move.start()

    delta = delta_of(g_ref[...], a_ref[...])
    delta = jnp.sum(jnp.where(diagonal(rows), delta, 0.0), axis=0, keepdims=True)
    row = lax.broadcasted_iota(jnp.int32, (EXTRA, rows), 0)
    extra = jnp.zeros((EXTRA, rows), jnp.float32)
    for at, part in enumerate(pieces_of(n_ref[...]) + pieces_of(delta)):
        extra = jnp.where(row == at, part, extra)
    extra_ref[:, :width] = extra.astype(jnp.bfloat16)
    extra_ref[:, width:] = jnp.zeros((EXTRA, width), jnp.bfloat16)
    tails = [
        pltpu.make_async_copy(extra_ref, hop.at[rows:, :], extra_sems.at[bit])
        for bit, hop in enumerate(hops)
    ]
    for tail in tails:
        tail.start()
    for bit in range(len(hops)):
        for move in moves(bit, k_ref, v_ref):
            move.wait()
    for tail in tails:
        tail.wait()


def project(grads, w_refs, start, out_ref):
    part = out_ref.shape[1]
    cols = math.gcd(part, 512)
    for at in range(0, part, cols):
        span = pl.ds(pl.multiple_of(start + at, cols), cols)
        weight = jnp.concatenate([ref[span, :] for ref in w_refs], axis=1)
        out_ref[:, at : at + cols] = dot_nt(grads[...], weight).astype(out_ref.dtype)


def near_kernel(scale, part, q_ref, k_ref, v_ref, g_ref, a_ref, n_ref, wq_ref, wk_ref, wv_ref, *refs):
    grads, front = refs[-2:]
    got = refs[:-2]
    rows, width = q_ref.shape
    me = lax.axis_index("ctx")
    exponent = scale * math.log2(math.e)
    query, key, value, grad = q_ref[...], k_ref[...], v_ref[...], g_ref[...]
    norm = jnp.sum(jnp.where(diagonal(rows), n_ref[...], 0.0), axis=1, keepdims=True)
    delta = delta_of(grad, a_ref[...])
    row_at = lax.broadcasted_iota(jnp.int32, (rows, rows), 0)
    col_at = lax.broadcasted_iota(jnp.int32, (rows, rows), 1)
    probs = jnp.where(col_at <= row_at, jnp.exp2(exponent * (dot_nt(query, key) - norm)), 0.0)
    score_low = (probs * (dot_nt(grad, value) - delta)).astype(jnp.bfloat16)
    query_sum = dot_nn(score_low, key)
    key_sum = dot_tn(score_low, query)
    value_sum = dot_tn(probs.astype(jnp.bfloat16), grad)

    first = jnp.concatenate([ref[:rows, :width] for ref in got], axis=0)
    second = jnp.concatenate([ref[:rows, width:] for ref in got], axis=0)
    extra = jnp.concatenate([ref[rows:, :width] for ref in got], axis=1).astype(jnp.float32)
    norms = (1.0 / scale) * jnp.sum(extra[:PIECES], axis=0, keepdims=True)
    deltas = jnp.sum(extra[PIECES : 2 * PIECES], axis=0, keepdims=True)
    lanes = lax.broadcasted_iota(jnp.int32, (rows, len(got) * rows), 1)
    earlier = ((lanes // rows + 1) ^ me) < me
    scores = dot_nt(jnp.concatenate([query, key], axis=0), first)
    scores = jnp.where(earlier, scores[:rows] - norm, scores[rows:] - norms)
    probs = jnp.exp2(exponent * scores)
    prob_grad = dot_nt(jnp.concatenate([grad, value], axis=0), second)
    prob_grad = jnp.where(earlier, prob_grad[:rows] - delta, prob_grad[rows:] - deltas)
    score_grad = probs * prob_grad
    sides = jnp.concatenate(
        [jnp.where(earlier, score_grad, 0.0), jnp.where(earlier, 0.0, score_grad)], axis=0
    ).astype(jnp.bfloat16)
    both_sum = dot_nn(sides, first)
    value_sum += dot_nn(jnp.where(earlier, 0.0, probs).astype(jnp.bfloat16), second)
    grads[:, :width] = (scale * (query_sum + both_sum[:rows])).astype(jnp.bfloat16)
    grads[:, width : 2 * width] = (scale * (key_sum + both_sum[rows:])).astype(jnp.bfloat16)
    grads[:, 2 * width :] = value_sum.astype(jnp.bfloat16)
    start = (lax.axis_index("head") ^ 3) * part
    project(grads, (wq_ref, wk_ref, wv_ref), start, front)


def far_kernel(part, grads, wq_ref, wk_ref, wv_ref, last, front, back):
    w_refs = (wq_ref, wk_ref, wv_ref)
    head = lax.axis_index("head")
    project(grads, w_refs, (head ^ 3) * part + part // 2, last)
    start = (head ^ 2) * part
    project(grads, w_refs, start, front)
    project(grads, w_refs, start + part // 2, back)


def close_kernel(part, grads, wq_ref, wk_ref, wv_ref, near, mine):
    w_refs = (wq_ref, wk_ref, wv_ref)
    head = lax.axis_index("head")
    project(grads, w_refs, (head ^ 1) * part, near)
    project(grads, w_refs, head * part, mine)


def swap(value, axis, offset):
    size = lax.axis_size(axis)
    return lax.ppermute(value, axis, [(at, at ^ offset) for at in range(size)])


def near_body(own, weights, scale):
    rows, width = own[0].shape
    depth = weights[0].shape[0]
    ctx = lax.axis_size("ctx")
    part = depth // lax.axis_size("head")
    vmem = pl.BlockSpec(memory_space=pltpu.VMEM)
    hbm = pl.BlockSpec(memory_space=pl.ANY)
    params = pltpu.CompilerParams(vmem_limit_bytes=32 * MIB)
    hop = jax.ShapeDtypeStruct((rows + EXTRA, 2 * width), jnp.bfloat16)
    bits = (ctx - 1).bit_length()
    sent = pl.pallas_call(
        send_kernel,
        out_shape=[hop] * bits,
        in_specs=[hbm] * 6,
        out_specs=[hbm] * bits,
        scratch_shapes=[pltpu.VMEM((rows, width), jnp.bfloat16)] * 5
        + [
            pltpu.VMEM((1, rows), jnp.float32),
            pltpu.VMEM((EXTRA, 2 * width), jnp.bfloat16),
            pltpu.SemaphoreType.DMA((6,)),
            pltpu.SemaphoreType.DMA((2 * bits,)),
            pltpu.SemaphoreType.DMA((bits,)),
        ],
        compiler_params=pltpu.CompilerParams(vmem_limit_bytes=56 * MIB),
        cost_estimate=pl.CostEstimate(
            flops=5000000000, bytes_accessed=20 * rows * width, transcendentals=0
        ),
    )(*own)
    got = {}
    for at in range(ctx - 1, 0, -1):
        got[at] = swap(sent[at.bit_length() - 1], "ctx", at)
    soon = [at for at in (1,6,4,7,5) if at < ctx]
    early, norm = lax.optimization_barrier((tuple(got[at] for at in soon), own[-1]))
    got.update(zip(soon, early))
    own = own[:-1] + (norm * (1.0 / scale),)
    got = [got[at] for at in range(1, ctx)]
    half_low = jax.ShapeDtypeStruct((rows, part // 2), jnp.bfloat16)
    half = jax.ShapeDtypeStruct((rows, part // 2), jnp.float32)
    low = jax.ShapeDtypeStruct((rows, part), jnp.bfloat16)
    full = jax.ShapeDtypeStruct((rows, part), jnp.float32)
    grads, front = pl.pallas_call(
        functools.partial(near_kernel, scale, part),
        out_shape=[jax.ShapeDtypeStruct((rows, 3 * width), jnp.bfloat16), half_low],
        in_specs=[vmem] * (ctx + 8),
        out_specs=[vmem] * 2,
        compiler_params=params,
        cost_estimate=pl.CostEstimate(
            flops=14 * rows * rows * ctx * width + 6 * rows * width * part,
            bytes_accessed=4 * rows * ctx * width + 6 * part * width,
            transcendentals=rows * rows * ctx,
        ),
    )(*own, *weights, *got)
    front = swap(front, "head", 1)
    def projected(kernel, outs, operands):
        count = sum(out.shape[1] for out in outs)
        return pl.pallas_call(
            functools.partial(kernel, part),
            out_shape=outs,
            in_specs=[vmem] * (1 + len(weights)),
            out_specs=[vmem] * len(outs),
            compiler_params=params,
            cost_estimate=pl.CostEstimate(
                flops=6 * rows * width * count, bytes_accessed=6 * count * width, transcendentals=0
            ),
        )(*operands)

    back, two_front, two_back = projected(far_kernel, [half_low, half, half], (grads, *weights))
    back = swap(back, "head", 1)
    near, total = projected(close_kernel, [low, full], (grads, *weights))
    near, back = lax.optimization_barrier((near, back))
    front = swap((two_front + front.astype(jnp.float32)).astype(jnp.bfloat16), "head", 2)
    back = swap((two_back + back.astype(jnp.float32)).astype(jnp.bfloat16), "head", 2)
    near = swap(near, "head", 1)
    far_sum = jnp.concatenate([front, back], axis=1).astype(jnp.float32)
    return (total + near.astype(jnp.float32) + far_sum).astype(jnp.bfloat16)


def far_body(own, weights, scale):
    rows, width = own[0].shape
    depth = weights[0].shape[0]
    ctx = lax.axis_size("ctx")
    parts = lax.axis_size("head")
    spot = lax.axis_index("ctx").astype(jnp.int32).reshape(1)
    vmem = pl.BlockSpec(memory_space=pltpu.VMEM)
    smem = pl.BlockSpec(memory_space=pltpu.SMEM)
    hbm = pl.BlockSpec(memory_space=pl.ANY)
    packed = pl.pallas_call(
        pack_kernel,
        out_shape=jax.ShapeDtypeStruct((ctx, rows + EXTRA, 2 * width), jnp.bfloat16),
        in_specs=[smem] + [vmem] * 6,
        out_specs=vmem,
        compiler_params=pltpu.CompilerParams(vmem_limit_bytes=32 * MIB),
    )(spot, *own)
    got = lax.all_to_all(packed, "ctx", split_axis=0, concat_axis=0, tiled=True)
    total = ctx * rows
    group = math.gcd(ctx, 8)
    parted = pl.pallas_call(
        functools.partial(main_kernel, group, scale),
        out_shape=jax.ShapeDtypeStruct((parts, rows, depth // parts), jnp.bfloat16),
        in_specs=[smem] + [vmem] * 7 + [hbm] * 3,
        out_specs=vmem,
        scratch_shapes=[
            pltpu.VMEM((depth, 3 * width), jnp.bfloat16),
            pltpu.VMEM((rows, 3 * width), jnp.bfloat16),
            pltpu.SemaphoreType.DMA((3,)),
        ],
        compiler_params=pltpu.CompilerParams(vmem_limit_bytes=48 * MIB),
        cost_estimate=pl.CostEstimate(
            flops=14 * rows * total * width + 6 * rows * width * depth,
            bytes_accessed=6 * depth * width + 10 * total * width,
            transcendentals=2 * rows * total,
        ),
    )(spot, got, *own, *weights)
    swapped = lax.all_to_all(parted, "head", split_axis=0, concat_axis=0, tiled=True)
    return jnp.sum(swapped.astype(jnp.float32), axis=0).astype(jnp.bfloat16)


def body(
    queries,
    key_rows,
    value_rows,
    out_grad,
    attn_out,
    log_norm,
    query_weight,
    key_weight,
    value_weight,
):
    rows, width = queries.shape
    ctx, parts = lax.axis_size("ctx"), lax.axis_size("head")
    own = (queries, key_rows, value_rows, out_grad, attn_out, log_norm.reshape(1, rows))
    weights = (query_weight, key_weight, value_weight)
    near = ctx <= 8 and parts == 4 and ctx & (ctx - 1) == 0
    return (near_body if near else far_body)(own, weights, width ** (-0.5))


def solution(mesh):
    return jax.shard_map(
        body,
        mesh=mesh,
        in_specs=(P("ctx", "head"),) * 6 + (P(None, "head"),) * 3,
        out_specs=P("ctx", "head"),
        check_vma=False,
    )
```

```python
import functools
import math

import jax
import jax.numpy as jnp
from jax import lax
from jax.experimental import pallas as pl
from jax.experimental.pallas import tpu as pltpu
from jax.sharding import PartitionSpec as P

NT = (((1,), (1,)), ((), ()))
TN = (((0,), (0,)), ((), ()))
PIECES = 3
EXTRA = 16
MIB = 1024 * 1024


def dot_nt(left, right):
    return lax.dot_general(left, right, NT, preferred_element_type=jnp.float32)


def dot_tn(left, right):
    return lax.dot_general(left, right, TN, preferred_element_type=jnp.float32)


def dot_nn(left, right):
    return jnp.dot(left, right, preferred_element_type=jnp.float32)


def pieces_of(value):
    out = []
    rest = value
    for _ in range(PIECES):
        low = rest.astype(jnp.bfloat16).astype(jnp.float32)
        out.append(low)
        rest = rest - low
    return out


def diagonal(rows):
    row_at = lax.broadcasted_iota(jnp.int32, (rows, rows), 0)
    col_at = lax.broadcasted_iota(jnp.int32, (rows, rows), 1)
    return row_at == col_at


def delta_of(grad, attn):
    return jnp.sum(grad.astype(jnp.float32) * attn.astype(jnp.float32), axis=1, keepdims=True)


def pack_kernel(me_ref, q_ref, k_ref, v_ref, g_ref, a_ref, n_ref, out_ref):
    rows, width = q_ref.shape
    me = me_ref[0]
    delta = delta_of(g_ref[...], a_ref[...])
    delta = jnp.sum(jnp.where(diagonal(rows), delta, 0.0), axis=0, keepdims=True)
    row = lax.broadcasted_iota(jnp.int32, (EXTRA, rows), 0)
    extra = jnp.zeros((EXTRA, rows), jnp.float32)
    for at, piece in enumerate(pieces_of(n_ref[...]) + pieces_of(delta)):
        extra = jnp.where(row == at, piece, extra)
    extra = extra.astype(jnp.bfloat16)

    def for_later(at, carry):
        out_ref[at, :rows, :width] = k_ref[...]
        out_ref[at, :rows, width:] = v_ref[...]
        out_ref[at, rows:, :] = jnp.zeros((EXTRA, 2 * width), jnp.bfloat16)
        return carry

    def for_earlier(at, carry):
        out_ref[at, :rows, :width] = q_ref[...]
        out_ref[at, :rows, width:] = g_ref[...]
        out_ref[at, rows:, :width] = extra
        out_ref[at, rows:, width:] = jnp.zeros((EXTRA, width), jnp.bfloat16)
        return carry

    lax.fori_loop(0, me + 1, for_earlier, 0)
    lax.fori_loop(me + 1, out_ref.shape[0], for_later, 0)


def main_kernel(
    group,
    scale,
    me_ref,
    got_ref,
    q_ref,
    k_ref,
    v_ref,
    g_ref,
    a_ref,
    n_ref,
    wq_ref,
    wk_ref,
    wv_ref,
    out_ref,
    w_all,
    grads,
    sems,
):
    rows, width = q_ref.shape
    copies = [
        pltpu.make_async_copy(ref, w_all.at[:, at * width : (at + 1) * width], sems.at[at])
        for at, ref in enumerate((wq_ref, wk_ref, wv_ref))
    ]
    for copy in copies:
        copy.start()
    me = me_ref[0]
    exponent = scale * math.log2(math.e)
    query, key, value, grad = q_ref[...], k_ref[...], v_ref[...], g_ref[...]
    eye = diagonal(rows)
    norm = (1.0 / scale) * jnp.sum(jnp.where(eye, n_ref[...], 0.0), axis=1, keepdims=True)
    delta = delta_of(grad, a_ref[...])

    row_at = lax.broadcasted_iota(jnp.int32, (rows, rows), 0)
    col_at = lax.broadcasted_iota(jnp.int32, (rows, rows), 1)
    probs = jnp.where(col_at <= row_at, jnp.exp2(exponent * (dot_nt(query, key) - norm)), 0.0)
    score_low = (probs * (dot_nt(grad, value) - delta)).astype(jnp.bfloat16)
    query_sum = dot_nn(score_low, key)
    key_sum = dot_tn(score_low, query)
    value_sum = dot_tn(probs.astype(jnp.bfloat16), grad)

    first_side = jnp.concatenate([query, key], axis=0)
    second_side = jnp.concatenate([grad, value], axis=0)

    def step(at, sums):
        both_sum, value_sum = sums
        blocks = [at * group + i for i in range(group)]
        first = jnp.concatenate([got_ref[b, :rows, :width] for b in blocks], axis=0)
        second = jnp.concatenate([got_ref[b, :rows, width:] for b in blocks], axis=0)
        extra = jnp.concatenate([got_ref[b, rows:, :width] for b in blocks], axis=1)
        extra = extra.astype(jnp.float32)
        norms = (1.0 / scale) * jnp.sum(extra[:PIECES], axis=0, keepdims=True)
        deltas = jnp.sum(extra[PIECES : 2 * PIECES], axis=0, keepdims=True)
        block = at * group + lax.broadcasted_iota(jnp.int32, (rows, group * rows), 1) // rows
        earlier, later = block < me, block > me
        scores = dot_nt(first_side, first)
        scores = jnp.where(earlier, scores[:rows] - norm, scores[rows:] - norms)
        probs = jnp.exp2(exponent * jnp.where(block == me, 0.0, scores))
        prob_grad = dot_nt(second_side, second)
        prob_grad = jnp.where(earlier, prob_grad[:rows] - delta, prob_grad[rows:] - deltas)
        score_grad = probs * prob_grad
        sides = jnp.concatenate(
            [jnp.where(earlier, score_grad, 0.0), jnp.where(later, score_grad, 0.0)], axis=0
        ).astype(jnp.bfloat16)
        both_sum += dot_nn(sides, first)
        value_sum += dot_nn(jnp.where(later, probs, 0.0).astype(jnp.bfloat16), second)
        return both_sum, value_sum

    sums = (jnp.concatenate([query_sum, key_sum], axis=0), value_sum)
    count = got_ref.shape[0] // group
    if count == 1:
        sums = step(0, sums)
    else:
        sums = lax.fori_loop(0, count, step, sums)
    grads[:, :width] = (scale * sums[0][:rows]).astype(jnp.bfloat16)
    grads[:, width : 2 * width] = (scale * sums[0][rows:]).astype(jnp.bfloat16)
    grads[:, 2 * width :] = sums[1].astype(jnp.bfloat16)
    for copy in copies:
        copy.wait()
    parts, _, part = out_ref.shape
    cols = math.gcd(part, 512)
    for h in range(parts):
        for at in range(0, part, cols):
            weight = w_all[h * part + at : h * part + at + cols, :]
            out_ref[h, :, at : at + cols] = dot_nt(grads[...], weight).astype(jnp.bfloat16)


def send_kernel(q_in, k_in, v_in, g_in, a_in, n_in, *refs):
    q_ref, k_ref, v_ref, g_ref, a_ref, n_ref, extra_ref, in_sems, row_sems, extra_sems = refs[-10:]
    hops = refs[:-10]
    me = lax.axis_index("ctx")
    rows, width = g_ref.shape
    pairs = (
        (k_in, k_ref),
        (v_in, v_ref),
        (q_in, q_ref),
        (g_in, g_ref),
        (a_in, a_ref),
        (n_in, n_ref),
    )
    loads = [pltpu.make_async_copy(*pair, in_sems.at[at]) for at, pair in enumerate(pairs)]
    for load in loads:
        load.start()

    def moves(bit, first, second):
        return [
            pltpu.make_async_copy(
                src, hops[bit].at[:rows, at * width : (at + 1) * width], row_sems.at[2 * bit + at]
            )
            for at, src in enumerate((first, second))
        ]

    for load in loads:
        load.wait()
    for bit in range(len(hops)):
        later = (me & (1 << bit)) == 0

        @pl.when(later)
        def _():
            for move in moves(bit, k_ref, v_ref):
                move.start()

        @pl.when(jnp.logical_not(later))
        def _():
            for move in moves(bit, q_ref, g_ref):
                move.start()

    delta = delta_of(g_ref[...], a_ref[...])
    delta = jnp.sum(jnp.where(diagonal(rows), delta, 0.0), axis=0, keepdims=True)
    row = lax.broadcasted_iota(jnp.int32, (EXTRA, rows), 0)
    extra = jnp.zeros((EXTRA, rows), jnp.float32)
    for at, part in enumerate(pieces_of(n_ref[...]) + pieces_of(delta)):
        extra = jnp.where(row == at, part, extra)
    extra_ref[:, :width] = extra.astype(jnp.bfloat16)
    extra_ref[:, width:] = jnp.zeros((EXTRA, width), jnp.bfloat16)
    tails = [
        pltpu.make_async_copy(extra_ref, hop.at[rows:, :], extra_sems.at[bit])
        for bit, hop in enumerate(hops)
    ]
    for tail in tails:
        tail.start()
    for bit in range(len(hops)):
        for move in moves(bit, k_ref, v_ref):
            move.wait()
    for tail in tails:
        tail.wait()


def project(grads, w_refs, start, out_ref):
    part = out_ref.shape[1]
    cols = math.gcd(part, 512)
    for at in range(0, part, cols):
        span = pl.ds(pl.multiple_of(start + at, cols), cols)
        weight = jnp.concatenate([ref[span, :] for ref in w_refs], axis=1)
        out_ref[:, at : at + cols] = dot_nt(grads[...], weight).astype(out_ref.dtype)


def near_kernel(scale, part, q_ref, k_ref, v_ref, g_ref, a_ref, n_ref, wq_ref, wk_ref, wv_ref, *refs):
    grads, front = refs[-2:]
    got = refs[:-2]
    rows, width = q_ref.shape
    me = lax.axis_index("ctx")
    exponent = scale * math.log2(math.e)
    query, key, value, grad = q_ref[...], k_ref[...], v_ref[...], g_ref[...]
    norm = jnp.sum(jnp.where(diagonal(rows), n_ref[...], 0.0), axis=1, keepdims=True)
    delta = delta_of(grad, a_ref[...])
    row_at = lax.broadcasted_iota(jnp.int32, (rows, rows), 0)
    col_at = lax.broadcasted_iota(jnp.int32, (rows, rows), 1)
    probs = jnp.where(col_at <= row_at, jnp.exp2(exponent * (dot_nt(query, key) - norm)), 0.0)
    score_low = (probs * (dot_nt(grad, value) - delta)).astype(jnp.bfloat16)
    query_sum = dot_nn(score_low, key)
    key_sum = dot_tn(score_low, query)
    value_sum = dot_tn(probs.astype(jnp.bfloat16), grad)

    first = jnp.concatenate([ref[:rows, :width] for ref in got], axis=0)
    second = jnp.concatenate([ref[:rows, width:] for ref in got], axis=0)
    extra = jnp.concatenate([ref[rows:, :width] for ref in got], axis=1).astype(jnp.float32)
    norms = (1.0 / scale) * jnp.sum(extra[:PIECES], axis=0, keepdims=True)
    deltas = jnp.sum(extra[PIECES : 2 * PIECES], axis=0, keepdims=True)
    lanes = lax.broadcasted_iota(jnp.int32, (rows, len(got) * rows), 1)
    earlier = ((lanes // rows + 1) ^ me) < me
    scores = dot_nt(jnp.concatenate([query, key], axis=0), first)
    scores = jnp.where(earlier, scores[:rows] - norm, scores[rows:] - norms)
    probs = jnp.exp2(exponent * scores)
    prob_grad = dot_nt(jnp.concatenate([grad, value], axis=0), second)
    prob_grad = jnp.where(earlier, prob_grad[:rows] - delta, prob_grad[rows:] - deltas)
    score_grad = probs * prob_grad
    sides = jnp.concatenate(
        [jnp.where(earlier, score_grad, 0.0), jnp.where(earlier, 0.0, score_grad)], axis=0
    ).astype(jnp.bfloat16)
    both_sum = dot_nn(sides, first)
    value_sum += dot_nn(jnp.where(earlier, 0.0, probs).astype(jnp.bfloat16), second)
    grads[:, :width] = (scale * (query_sum + both_sum[:rows])).astype(jnp.bfloat16)
    grads[:, width : 2 * width] = (scale * (key_sum + both_sum[rows:])).astype(jnp.bfloat16)
    grads[:, 2 * width :] = value_sum.astype(jnp.bfloat16)
    start = (lax.axis_index("head") ^ 3) * part
    project(grads, (wq_ref, wk_ref, wv_ref), start, front)


def far_kernel(part, grads, wq_ref, wk_ref, wv_ref, front, back):
    w_refs = (wq_ref, wk_ref, wv_ref)
    head = lax.axis_index("head")
    start = (head ^ 2) * part
    project(grads, w_refs, start, front)
    project(grads, w_refs, start + part // 2, back)


def close_kernel(part, grads, wq_ref, wk_ref, wv_ref, last, near, mine):
    w_refs = (wq_ref, wk_ref, wv_ref)
    head = lax.axis_index("head")
    project(grads, w_refs, (head ^ 3) * part + part // 2, last)
    project(grads, w_refs, (head ^ 1) * part, near)
    project(grads, w_refs, head * part, mine)


def swap(value, axis, offset):
    size = lax.axis_size(axis)
    return lax.ppermute(value, axis, [(at, at ^ offset) for at in range(size)])


def near_body(own, weights, scale):
    rows, width = own[0].shape
    depth = weights[0].shape[0]
    ctx = lax.axis_size("ctx")
    part = depth // lax.axis_size("head")
    vmem = pl.BlockSpec(memory_space=pltpu.VMEM)
    hbm = pl.BlockSpec(memory_space=pl.ANY)
    params = pltpu.CompilerParams(vmem_limit_bytes=32 * MIB)
    hop = jax.ShapeDtypeStruct((rows + EXTRA, 2 * width), jnp.bfloat16)
    bits = (ctx - 1).bit_length()
    sent = pl.pallas_call(
        send_kernel,
        out_shape=[hop] * bits,
        in_specs=[hbm] * 6,
        out_specs=[hbm] * bits,
        scratch_shapes=[pltpu.VMEM((rows, width), jnp.bfloat16)] * 5
        + [
            pltpu.VMEM((1, rows), jnp.float32),
            pltpu.VMEM((EXTRA, 2 * width), jnp.bfloat16),
            pltpu.SemaphoreType.DMA((6,)),
            pltpu.SemaphoreType.DMA((2 * bits,)),
            pltpu.SemaphoreType.DMA((bits,)),
        ],
        compiler_params=pltpu.CompilerParams(vmem_limit_bytes=56 * MIB),
        cost_estimate=pl.CostEstimate(
            flops=5000000000, bytes_accessed=20 * rows * width, transcendentals=0
        ),
    )(*own)
    got = {}
    for at in range(ctx - 1, 0, -1):
        got[at] = swap(sent[at.bit_length() - 1], "ctx", at)
    soon = [at for at in (7,6,5) if at < ctx]
    early, norm = lax.optimization_barrier((tuple(got[at] for at in soon), own[-1]))
    got.update(zip(soon, early))
    own = own[:-1] + (norm * (1.0 / scale),)
    got = [got[at] for at in range(1, ctx)]
    half_low = jax.ShapeDtypeStruct((rows, part // 2), jnp.bfloat16)
    half = jax.ShapeDtypeStruct((rows, part // 2), jnp.float32)
    low = jax.ShapeDtypeStruct((rows, part), jnp.bfloat16)
    full = jax.ShapeDtypeStruct((rows, part), jnp.float32)
    grads, front = pl.pallas_call(
        functools.partial(near_kernel, scale, part),
        out_shape=[jax.ShapeDtypeStruct((rows, 3 * width), jnp.bfloat16), half_low],
        in_specs=[vmem] * (ctx + 8),
        out_specs=[vmem] * 2,
        compiler_params=params,
        cost_estimate=pl.CostEstimate(
            flops=14 * rows * rows * ctx * width + 6 * rows * width * part,
            bytes_accessed=4 * rows * ctx * width + 6 * part * width,
            transcendentals=rows * rows * ctx,
        ),
    )(*own, *weights, *got)
    front = swap(front, "head", 1)
    def projected(kernel, outs, operands):
        count = sum(out.shape[1] for out in outs)
        return pl.pallas_call(
            functools.partial(kernel, part),
            out_shape=outs,
            in_specs=[vmem] * (1 + len(weights)),
            out_specs=[vmem] * len(outs),
            compiler_params=params,
            cost_estimate=pl.CostEstimate(
                flops=6 * rows * width * count, bytes_accessed=6 * count * width, transcendentals=0
            ),
        )(*operands)

    two_front, two_back = projected(far_kernel, [half, half], (grads, *weights))
    grads, two_front = lax.optimization_barrier((grads, two_front))
    back, near, total = projected(close_kernel, [half_low, low, full], (grads, *weights))
    back = swap(back, "head", 1)
    near, back = lax.optimization_barrier((near, back))
    front = swap((two_front + front.astype(jnp.float32)).astype(jnp.bfloat16), "head", 2)
    back = swap((two_back + back.astype(jnp.float32)).astype(jnp.bfloat16), "head", 2)
    near = swap(near, "head", 1)
    far_sum = jnp.concatenate([front, back], axis=1).astype(jnp.float32)
    return (total + near.astype(jnp.float32) + far_sum).astype(jnp.bfloat16)


def far_body(own, weights, scale):
    rows, width = own[0].shape
    depth = weights[0].shape[0]
    ctx = lax.axis_size("ctx")
    parts = lax.axis_size("head")
    spot = lax.axis_index("ctx").astype(jnp.int32).reshape(1)
    vmem = pl.BlockSpec(memory_space=pltpu.VMEM)
    smem = pl.BlockSpec(memory_space=pltpu.SMEM)
    hbm = pl.BlockSpec(memory_space=pl.ANY)
    packed = pl.pallas_call(
        pack_kernel,
        out_shape=jax.ShapeDtypeStruct((ctx, rows + EXTRA, 2 * width), jnp.bfloat16),
        in_specs=[smem] + [vmem] * 6,
        out_specs=vmem,
        compiler_params=pltpu.CompilerParams(vmem_limit_bytes=32 * MIB),
    )(spot, *own)
    got = lax.all_to_all(packed, "ctx", split_axis=0, concat_axis=0, tiled=True)
    total = ctx * rows
    group = math.gcd(ctx, 8)
    parted = pl.pallas_call(
        functools.partial(main_kernel, group, scale),
        out_shape=jax.ShapeDtypeStruct((parts, rows, depth // parts), jnp.bfloat16),
        in_specs=[smem] + [vmem] * 7 + [hbm] * 3,
        out_specs=vmem,
        scratch_shapes=[
            pltpu.VMEM((depth, 3 * width), jnp.bfloat16),
            pltpu.VMEM((rows, 3 * width), jnp.bfloat16),
            pltpu.SemaphoreType.DMA((3,)),
        ],
        compiler_params=pltpu.CompilerParams(vmem_limit_bytes=48 * MIB),
        cost_estimate=pl.CostEstimate(
            flops=14 * rows * total * width + 6 * rows * width * depth,
            bytes_accessed=6 * depth * width + 10 * total * width,
            transcendentals=2 * rows * total,
        ),
    )(spot, got, *own, *weights)
    swapped = lax.all_to_all(parted, "head", split_axis=0, concat_axis=0, tiled=True)
    return jnp.sum(swapped.astype(jnp.float32), axis=0).astype(jnp.bfloat16)


def body(
    queries,
    key_rows,
    value_rows,
    out_grad,
    attn_out,
    log_norm,
    query_weight,
    key_weight,
    value_weight,
):
    rows, width = queries.shape
    ctx, parts = lax.axis_size("ctx"), lax.axis_size("head")
    own = (queries, key_rows, value_rows, out_grad, attn_out, log_norm.reshape(1, rows))
    weights = (query_weight, key_weight, value_weight)
    near = ctx <= 8 and parts == 4 and ctx & (ctx - 1) == 0
    return (near_body if near else far_body)(own, weights, width ** (-0.5))


def solution(mesh):
    return jax.shard_map(
        body,
        mesh=mesh,
        in_specs=(P("ctx", "head"),) * 6 + (P(None, "head"),) * 3,
        out_specs=P("ctx", "head"),
        check_vma=False,
    )
```

```python
import functools
import math

import jax
import jax.numpy as jnp
from jax import lax
from jax.experimental import pallas as pl
from jax.experimental.pallas import tpu as pltpu
from jax.sharding import PartitionSpec as P

NT = (((1,), (1,)), ((), ()))
TN = (((0,), (0,)), ((), ()))
PIECES = 3
EXTRA = 16
MIB = 1024 * 1024


def dot_nt(left, right):
    return lax.dot_general(left, right, NT, preferred_element_type=jnp.float32)


def dot_tn(left, right):
    return lax.dot_general(left, right, TN, preferred_element_type=jnp.float32)


def dot_nn(left, right):
    return jnp.dot(left, right, preferred_element_type=jnp.float32)


def pieces_of(value):
    out = []
    rest = value
    for _ in range(PIECES):
        low = rest.astype(jnp.bfloat16).astype(jnp.float32)
        out.append(low)
        rest = rest - low
    return out


def diagonal(rows):
    row_at = lax.broadcasted_iota(jnp.int32, (rows, rows), 0)
    col_at = lax.broadcasted_iota(jnp.int32, (rows, rows), 1)
    return row_at == col_at


def delta_of(grad, attn):
    return jnp.sum(grad.astype(jnp.float32) * attn.astype(jnp.float32), axis=1, keepdims=True)


def pack_kernel(me_ref, q_ref, k_ref, v_ref, g_ref, a_ref, n_ref, out_ref):
    rows, width = q_ref.shape
    me = me_ref[0]
    delta = delta_of(g_ref[...], a_ref[...])
    delta = jnp.sum(jnp.where(diagonal(rows), delta, 0.0), axis=0, keepdims=True)
    row = lax.broadcasted_iota(jnp.int32, (EXTRA, rows), 0)
    extra = jnp.zeros((EXTRA, rows), jnp.float32)
    for at, piece in enumerate(pieces_of(n_ref[...]) + pieces_of(delta)):
        extra = jnp.where(row == at, piece, extra)
    extra = extra.astype(jnp.bfloat16)

    def for_later(at, carry):
        out_ref[at, :rows, :width] = k_ref[...]
        out_ref[at, :rows, width:] = v_ref[...]
        out_ref[at, rows:, :] = jnp.zeros((EXTRA, 2 * width), jnp.bfloat16)
        return carry

    def for_earlier(at, carry):
        out_ref[at, :rows, :width] = q_ref[...]
        out_ref[at, :rows, width:] = g_ref[...]
        out_ref[at, rows:, :width] = extra
        out_ref[at, rows:, width:] = jnp.zeros((EXTRA, width), jnp.bfloat16)
        return carry

    lax.fori_loop(0, me + 1, for_earlier, 0)
    lax.fori_loop(me + 1, out_ref.shape[0], for_later, 0)


def main_kernel(
    group,
    scale,
    me_ref,
    got_ref,
    q_ref,
    k_ref,
    v_ref,
    g_ref,
    a_ref,
    n_ref,
    wq_ref,
    wk_ref,
    wv_ref,
    out_ref,
    w_all,
    grads,
    sems,
):
    rows, width = q_ref.shape
    copies = [
        pltpu.make_async_copy(ref, w_all.at[:, at * width : (at + 1) * width], sems.at[at])
        for at, ref in enumerate((wq_ref, wk_ref, wv_ref))
    ]
    for copy in copies:
        copy.start()
    me = me_ref[0]
    exponent = scale * math.log2(math.e)
    query, key, value, grad = q_ref[...], k_ref[...], v_ref[...], g_ref[...]
    eye = diagonal(rows)
    norm = (1.0 / scale) * jnp.sum(jnp.where(eye, n_ref[...], 0.0), axis=1, keepdims=True)
    delta = delta_of(grad, a_ref[...])

    row_at = lax.broadcasted_iota(jnp.int32, (rows, rows), 0)
    col_at = lax.broadcasted_iota(jnp.int32, (rows, rows), 1)
    probs = jnp.where(col_at <= row_at, jnp.exp2(exponent * (dot_nt(query, key) - norm)), 0.0)
    score_low = (probs * (dot_nt(grad, value) - delta)).astype(jnp.bfloat16)
    query_sum = dot_nn(score_low, key)
    key_sum = dot_tn(score_low, query)
    value_sum = dot_tn(probs.astype(jnp.bfloat16), grad)

    first_side = jnp.concatenate([query, key], axis=0)
    second_side = jnp.concatenate([grad, value], axis=0)

    def step(at, sums):
        both_sum, value_sum = sums
        blocks = [at * group + i for i in range(group)]
        first = jnp.concatenate([got_ref[b, :rows, :width] for b in blocks], axis=0)
        second = jnp.concatenate([got_ref[b, :rows, width:] for b in blocks], axis=0)
        extra = jnp.concatenate([got_ref[b, rows:, :width] for b in blocks], axis=1)
        extra = extra.astype(jnp.float32)
        norms = (1.0 / scale) * jnp.sum(extra[:PIECES], axis=0, keepdims=True)
        deltas = jnp.sum(extra[PIECES : 2 * PIECES], axis=0, keepdims=True)
        block = at * group + lax.broadcasted_iota(jnp.int32, (rows, group * rows), 1) // rows
        earlier, later = block < me, block > me
        scores = dot_nt(first_side, first)
        scores = jnp.where(earlier, scores[:rows] - norm, scores[rows:] - norms)
        probs = jnp.exp2(exponent * jnp.where(block == me, 0.0, scores))
        prob_grad = dot_nt(second_side, second)
        prob_grad = jnp.where(earlier, prob_grad[:rows] - delta, prob_grad[rows:] - deltas)
        score_grad = probs * prob_grad
        sides = jnp.concatenate(
            [jnp.where(earlier, score_grad, 0.0), jnp.where(later, score_grad, 0.0)], axis=0
        ).astype(jnp.bfloat16)
        both_sum += dot_nn(sides, first)
        value_sum += dot_nn(jnp.where(later, probs, 0.0).astype(jnp.bfloat16), second)
        return both_sum, value_sum

    sums = (jnp.concatenate([query_sum, key_sum], axis=0), value_sum)
    count = got_ref.shape[0] // group
    if count == 1:
        sums = step(0, sums)
    else:
        sums = lax.fori_loop(0, count, step, sums)
    grads[:, :width] = (scale * sums[0][:rows]).astype(jnp.bfloat16)
    grads[:, width : 2 * width] = (scale * sums[0][rows:]).astype(jnp.bfloat16)
    grads[:, 2 * width :] = sums[1].astype(jnp.bfloat16)
    for copy in copies:
        copy.wait()
    parts, _, part = out_ref.shape
    cols = math.gcd(part, 512)
    for h in range(parts):
        for at in range(0, part, cols):
            weight = w_all[h * part + at : h * part + at + cols, :]
            out_ref[h, :, at : at + cols] = dot_nt(grads[...], weight).astype(jnp.bfloat16)


def send_kernel(q_in, k_in, v_in, g_in, a_in, n_in, *refs):
    q_ref, k_ref, v_ref, g_ref, a_ref, n_ref, extra_ref, in_sems, row_sems, extra_sems = refs[-10:]
    hops = refs[:-10]
    me = lax.axis_index("ctx")
    rows, width = g_ref.shape
    pairs = (
        (k_in, k_ref),
        (v_in, v_ref),
        (q_in, q_ref),
        (g_in, g_ref),
        (a_in, a_ref),
        (n_in, n_ref),
    )
    loads = [pltpu.make_async_copy(*pair, in_sems.at[at]) for at, pair in enumerate(pairs)]
    for load in loads:
        load.start()

    def moves(bit, first, second):
        return [
            pltpu.make_async_copy(
                src, hops[bit].at[:rows, at * width : (at + 1) * width], row_sems.at[2 * bit + at]
            )
            for at, src in enumerate((first, second))
        ]

    for load in loads:
        load.wait()
    for bit in range(len(hops)):
        later = (me & (1 << bit)) == 0

        @pl.when(later)
        def _():
            for move in moves(bit, k_ref, v_ref):
                move.start()

        @pl.when(jnp.logical_not(later))
        def _():
            for move in moves(bit, q_ref, g_ref):
                move.start()

    delta = delta_of(g_ref[...], a_ref[...])
    delta = jnp.sum(jnp.where(diagonal(rows), delta, 0.0), axis=0, keepdims=True)
    row = lax.broadcasted_iota(jnp.int32, (EXTRA, rows), 0)
    extra = jnp.zeros((EXTRA, rows), jnp.float32)
    for at, part in enumerate(pieces_of(n_ref[...]) + pieces_of(delta)):
        extra = jnp.where(row == at, part, extra)
    extra_ref[:, :width] = extra.astype(jnp.bfloat16)
    extra_ref[:, width:] = jnp.zeros((EXTRA, width), jnp.bfloat16)
    tails = [
        pltpu.make_async_copy(extra_ref, hop.at[rows:, :], extra_sems.at[bit])
        for bit, hop in enumerate(hops)
    ]
    for tail in tails:
        tail.start()
    for bit in range(len(hops)):
        for move in moves(bit, k_ref, v_ref):
            move.wait()
    for tail in tails:
        tail.wait()


def project(grads, w_refs, start, out_ref):
    part = out_ref.shape[1]
    cols = math.gcd(part, 512)
    for at in range(0, part, cols):
        span = pl.ds(pl.multiple_of(start + at, cols), cols)
        weight = jnp.concatenate([ref[span, :] for ref in w_refs], axis=1)
        out_ref[:, at : at + cols] = dot_nt(grads[...], weight).astype(out_ref.dtype)


def near_kernel(scale, part, q_ref, k_ref, v_ref, g_ref, a_ref, n_ref, wq_ref, wk_ref, wv_ref, *refs):
    grads, front = refs[-2:]
    got = refs[:-2]
    rows, width = q_ref.shape
    me = lax.axis_index("ctx")
    exponent = scale * math.log2(math.e)
    query, key, value, grad = q_ref[...], k_ref[...], v_ref[...], g_ref[...]
    norm = jnp.sum(jnp.where(diagonal(rows), n_ref[...], 0.0), axis=1, keepdims=True)
    delta = delta_of(grad, a_ref[...])
    row_at = lax.broadcasted_iota(jnp.int32, (rows, rows), 0)
    col_at = lax.broadcasted_iota(jnp.int32, (rows, rows), 1)
    probs = jnp.where(col_at <= row_at, jnp.exp2(exponent * (dot_nt(query, key) - norm)), 0.0)
    score_low = (probs * (dot_nt(grad, value) - delta)).astype(jnp.bfloat16)
    query_sum = dot_nn(score_low, key)
    key_sum = dot_tn(score_low, query)
    value_sum = dot_tn(probs.astype(jnp.bfloat16), grad)

    first = jnp.concatenate([ref[:rows, :width] for ref in got], axis=0)
    second = jnp.concatenate([ref[:rows, width:] for ref in got], axis=0)
    extra = jnp.concatenate([ref[rows:, :width] for ref in got], axis=1).astype(jnp.float32)
    norms = (1.0 / scale) * jnp.sum(extra[:PIECES], axis=0, keepdims=True)
    deltas = jnp.sum(extra[PIECES : 2 * PIECES], axis=0, keepdims=True)
    lanes = lax.broadcasted_iota(jnp.int32, (rows, len(got) * rows), 1)
    earlier = ((lanes // rows + 1) ^ me) < me
    scores = dot_nt(jnp.concatenate([query, key], axis=0), first)
    scores = jnp.where(earlier, scores[:rows] - norm, scores[rows:] - norms)
    probs = jnp.exp2(exponent * scores)
    prob_grad = dot_nt(jnp.concatenate([grad, value], axis=0), second)
    prob_grad = jnp.where(earlier, prob_grad[:rows] - delta, prob_grad[rows:] - deltas)
    score_grad = probs * prob_grad
    sides = jnp.concatenate(
        [jnp.where(earlier, score_grad, 0.0), jnp.where(earlier, 0.0, score_grad)], axis=0
    ).astype(jnp.bfloat16)
    both_sum = dot_nn(sides, first)
    value_sum += dot_nn(jnp.where(earlier, 0.0, probs).astype(jnp.bfloat16), second)
    grads[:, :width] = (scale * (query_sum + both_sum[:rows])).astype(jnp.bfloat16)
    grads[:, width : 2 * width] = (scale * (key_sum + both_sum[rows:])).astype(jnp.bfloat16)
    grads[:, 2 * width :] = value_sum.astype(jnp.bfloat16)
    start = (lax.axis_index("head") ^ 3) * part
    project(grads, (wq_ref, wk_ref, wv_ref), start, front)


def far_kernel(part, grads, wq_ref, wk_ref, wv_ref, front, back):
    w_refs = (wq_ref, wk_ref, wv_ref)
    head = lax.axis_index("head")
    start = (head ^ 2) * part
    project(grads, w_refs, start, front)
    project(grads, w_refs, start + part // 2, back)


def close_kernel(part, grads, wq_ref, wk_ref, wv_ref, last, near, mine):
    w_refs = (wq_ref, wk_ref, wv_ref)
    head = lax.axis_index("head")
    project(grads, w_refs, (head ^ 3) * part + part // 2, last)
    project(grads, w_refs, (head ^ 1) * part, near)
    project(grads, w_refs, head * part, mine)


def swap(value, axis, offset):
    size = lax.axis_size(axis)
    return lax.ppermute(value, axis, [(at, at ^ offset) for at in range(size)])


def near_body(own, weights, scale):
    rows, width = own[0].shape
    depth = weights[0].shape[0]
    ctx = lax.axis_size("ctx")
    part = depth // lax.axis_size("head")
    vmem = pl.BlockSpec(memory_space=pltpu.VMEM)
    hbm = pl.BlockSpec(memory_space=pl.ANY)
    params = pltpu.CompilerParams(vmem_limit_bytes=32 * MIB)
    hop = jax.ShapeDtypeStruct((rows + EXTRA, 2 * width), jnp.bfloat16)
    bits = (ctx - 1).bit_length()
    sent = pl.pallas_call(
        send_kernel,
        out_shape=[hop] * bits,
        in_specs=[hbm] * 6,
        out_specs=[hbm] * bits,
        scratch_shapes=[pltpu.VMEM((rows, width), jnp.bfloat16)] * 5
        + [
            pltpu.VMEM((1, rows), jnp.float32),
            pltpu.VMEM((EXTRA, 2 * width), jnp.bfloat16),
            pltpu.SemaphoreType.DMA((6,)),
            pltpu.SemaphoreType.DMA((2 * bits,)),
            pltpu.SemaphoreType.DMA((bits,)),
        ],
        compiler_params=pltpu.CompilerParams(vmem_limit_bytes=56 * MIB),
        cost_estimate=pl.CostEstimate(
            flops=5000000000, bytes_accessed=20 * rows * width, transcendentals=0
        ),
    )(*own)
    got = {at: swap(sent[at.bit_length() - 1], "ctx", at) for at in (1, *range(2, ctx, 2))}
    soon = [at for at in (6,) if at < ctx]
    early, norm = lax.optimization_barrier((tuple(got[at] for at in soon), own[-1]))
    got.update(zip(soon, early))
    own = own[:-1] + (norm * (1.0 / scale),)
    for at in range(2, ctx, 2):
        got[at + 1] = swap(got[at], "ctx", 1)
    got = [got[at] for at in range(1, ctx)]
    half_low = jax.ShapeDtypeStruct((rows, part // 2), jnp.bfloat16)
    half = jax.ShapeDtypeStruct((rows, part // 2), jnp.float32)
    low = jax.ShapeDtypeStruct((rows, part), jnp.bfloat16)
    full = jax.ShapeDtypeStruct((rows, part), jnp.float32)
    grads, front = pl.pallas_call(
        functools.partial(near_kernel, scale, part),
        out_shape=[jax.ShapeDtypeStruct((rows, 3 * width), jnp.bfloat16), half_low],
        in_specs=[vmem] * (ctx + 8),
        out_specs=[vmem] * 2,
        compiler_params=params,
        cost_estimate=pl.CostEstimate(
            flops=14 * rows * rows * ctx * width + 6 * rows * width * part,
            bytes_accessed=4 * rows * ctx * width + 6 * part * width,
            transcendentals=rows * rows * ctx,
        ),
    )(*own, *weights, *got)
    front = swap(front, "head", 1)
    def projected(kernel, outs, operands):
        count = sum(out.shape[1] for out in outs)
        return pl.pallas_call(
            functools.partial(kernel, part),
            out_shape=outs,
            in_specs=[vmem] * (1 + len(weights)),
            out_specs=[vmem] * len(outs),
            compiler_params=params,
            cost_estimate=pl.CostEstimate(
                flops=6 * rows * width * count, bytes_accessed=6 * count * width, transcendentals=0
            ),
        )(*operands)

    two_front, two_back = projected(far_kernel, [half, half], (grads, *weights))
    grads, two_front = lax.optimization_barrier((grads, two_front))
    back, near, total = projected(close_kernel, [half_low, low, full], (grads, *weights))
    back = swap(back, "head", 1)
    near, back = lax.optimization_barrier((near, back))
    front = swap((two_front + front.astype(jnp.float32)).astype(jnp.bfloat16), "head", 2)
    back = swap((two_back + back.astype(jnp.float32)).astype(jnp.bfloat16), "head", 2)
    near = swap(near, "head", 1)
    far_sum = jnp.concatenate([front, back], axis=1).astype(jnp.float32)
    return (total + near.astype(jnp.float32) + far_sum).astype(jnp.bfloat16)


def far_body(own, weights, scale):
    rows, width = own[0].shape
    depth = weights[0].shape[0]
    ctx = lax.axis_size("ctx")
    parts = lax.axis_size("head")
    spot = lax.axis_index("ctx").astype(jnp.int32).reshape(1)
    vmem = pl.BlockSpec(memory_space=pltpu.VMEM)
    smem = pl.BlockSpec(memory_space=pltpu.SMEM)
    hbm = pl.BlockSpec(memory_space=pl.ANY)
    packed = pl.pallas_call(
        pack_kernel,
        out_shape=jax.ShapeDtypeStruct((ctx, rows + EXTRA, 2 * width), jnp.bfloat16),
        in_specs=[smem] + [vmem] * 6,
        out_specs=vmem,
        compiler_params=pltpu.CompilerParams(vmem_limit_bytes=32 * MIB),
    )(spot, *own)
    got = lax.all_to_all(packed, "ctx", split_axis=0, concat_axis=0, tiled=True)
    total = ctx * rows
    group = math.gcd(ctx, 8)
    parted = pl.pallas_call(
        functools.partial(main_kernel, group, scale),
        out_shape=jax.ShapeDtypeStruct((parts, rows, depth // parts), jnp.bfloat16),
        in_specs=[smem] + [vmem] * 7 + [hbm] * 3,
        out_specs=vmem,
        scratch_shapes=[
            pltpu.VMEM((depth, 3 * width), jnp.bfloat16),
            pltpu.VMEM((rows, 3 * width), jnp.bfloat16),
            pltpu.SemaphoreType.DMA((3,)),
        ],
        compiler_params=pltpu.CompilerParams(vmem_limit_bytes=48 * MIB),
        cost_estimate=pl.CostEstimate(
            flops=14 * rows * total * width + 6 * rows * width * depth,
            bytes_accessed=6 * depth * width + 10 * total * width,
            transcendentals=2 * rows * total,
        ),
    )(spot, got, *own, *weights)
    swapped = lax.all_to_all(parted, "head", split_axis=0, concat_axis=0, tiled=True)
    return jnp.sum(swapped.astype(jnp.float32), axis=0).astype(jnp.bfloat16)


def body(
    queries,
    key_rows,
    value_rows,
    out_grad,
    attn_out,
    log_norm,
    query_weight,
    key_weight,
    value_weight,
):
    rows, width = queries.shape
    ctx, parts = lax.axis_size("ctx"), lax.axis_size("head")
    own = (queries, key_rows, value_rows, out_grad, attn_out, log_norm.reshape(1, rows))
    weights = (query_weight, key_weight, value_weight)
    near = ctx <= 8 and parts == 4 and ctx & (ctx - 1) == 0
    return (near_body if near else far_body)(own, weights, width ** (-0.5))


def solution(mesh):
    return jax.shard_map(
        body,
        mesh=mesh,
        in_specs=(P("ctx", "head"),) * 6 + (P(None, "head"),) * 3,
        out_specs=P("ctx", "head"),
        check_vma=False,
    )
```

```python
import functools
import math

import jax
import jax.numpy as jnp
from jax import lax
from jax.experimental import pallas as pl
from jax.experimental.pallas import tpu as pltpu
from jax.sharding import PartitionSpec as P

NT = (((1,), (1,)), ((), ()))
TN = (((0,), (0,)), ((), ()))
PIECES = 3
EXTRA = 16
MIB = 1024 * 1024


def dot_nt(left, right):
    return lax.dot_general(left, right, NT, preferred_element_type=jnp.float32)


def dot_tn(left, right):
    return lax.dot_general(left, right, TN, preferred_element_type=jnp.float32)


def dot_nn(left, right):
    return jnp.dot(left, right, preferred_element_type=jnp.float32)


def pieces_of(value):
    out = []
    rest = value
    for _ in range(PIECES):
        low = rest.astype(jnp.bfloat16).astype(jnp.float32)
        out.append(low)
        rest = rest - low
    return out


def diagonal(rows):
    row_at = lax.broadcasted_iota(jnp.int32, (rows, rows), 0)
    col_at = lax.broadcasted_iota(jnp.int32, (rows, rows), 1)
    return row_at == col_at


def delta_of(grad, attn):
    return jnp.sum(grad.astype(jnp.float32) * attn.astype(jnp.float32), axis=1, keepdims=True)


def pack_kernel(me_ref, q_ref, k_ref, v_ref, g_ref, a_ref, n_ref, out_ref):
    rows, width = q_ref.shape
    me = me_ref[0]
    delta = delta_of(g_ref[...], a_ref[...])
    delta = jnp.sum(jnp.where(diagonal(rows), delta, 0.0), axis=0, keepdims=True)
    row = lax.broadcasted_iota(jnp.int32, (EXTRA, rows), 0)
    extra = jnp.zeros((EXTRA, rows), jnp.float32)
    for at, piece in enumerate(pieces_of(n_ref[...]) + pieces_of(delta)):
        extra = jnp.where(row == at, piece, extra)
    extra = extra.astype(jnp.bfloat16)

    def for_later(at, carry):
        out_ref[at, :rows, :width] = k_ref[...]
        out_ref[at, :rows, width:] = v_ref[...]
        out_ref[at, rows:, :] = jnp.zeros((EXTRA, 2 * width), jnp.bfloat16)
        return carry

    def for_earlier(at, carry):
        out_ref[at, :rows, :width] = q_ref[...]
        out_ref[at, :rows, width:] = g_ref[...]
        out_ref[at, rows:, :width] = extra
        out_ref[at, rows:, width:] = jnp.zeros((EXTRA, width), jnp.bfloat16)
        return carry

    lax.fori_loop(0, me + 1, for_earlier, 0)
    lax.fori_loop(me + 1, out_ref.shape[0], for_later, 0)


def main_kernel(
    group,
    scale,
    me_ref,
    got_ref,
    q_ref,
    k_ref,
    v_ref,
    g_ref,
    a_ref,
    n_ref,
    wq_ref,
    wk_ref,
    wv_ref,
    out_ref,
    w_all,
    grads,
    sems,
):
    rows, width = q_ref.shape
    copies = [
        pltpu.make_async_copy(ref, w_all.at[:, at * width : (at + 1) * width], sems.at[at])
        for at, ref in enumerate((wq_ref, wk_ref, wv_ref))
    ]
    for copy in copies:
        copy.start()
    me = me_ref[0]
    exponent = scale * math.log2(math.e)
    query, key, value, grad = q_ref[...], k_ref[...], v_ref[...], g_ref[...]
    eye = diagonal(rows)
    norm = (1.0 / scale) * jnp.sum(jnp.where(eye, n_ref[...], 0.0), axis=1, keepdims=True)
    delta = delta_of(grad, a_ref[...])

    row_at = lax.broadcasted_iota(jnp.int32, (rows, rows), 0)
    col_at = lax.broadcasted_iota(jnp.int32, (rows, rows), 1)
    probs = jnp.where(col_at <= row_at, jnp.exp2(exponent * (dot_nt(query, key) - norm)), 0.0)
    score_low = (probs * (dot_nt(grad, value) - delta)).astype(jnp.bfloat16)
    query_sum = dot_nn(score_low, key)
    key_sum = dot_tn(score_low, query)
    value_sum = dot_tn(probs.astype(jnp.bfloat16), grad)

    first_side = jnp.concatenate([query, key], axis=0)
    second_side = jnp.concatenate([grad, value], axis=0)

    def step(at, sums):
        both_sum, value_sum = sums
        blocks = [at * group + i for i in range(group)]
        first = jnp.concatenate([got_ref[b, :rows, :width] for b in blocks], axis=0)
        second = jnp.concatenate([got_ref[b, :rows, width:] for b in blocks], axis=0)
        extra = jnp.concatenate([got_ref[b, rows:, :width] for b in blocks], axis=1)
        extra = extra.astype(jnp.float32)
        norms = (1.0 / scale) * jnp.sum(extra[:PIECES], axis=0, keepdims=True)
        deltas = jnp.sum(extra[PIECES : 2 * PIECES], axis=0, keepdims=True)
        block = at * group + lax.broadcasted_iota(jnp.int32, (rows, group * rows), 1) // rows
        earlier, later = block < me, block > me
        scores = dot_nt(first_side, first)
        scores = jnp.where(earlier, scores[:rows] - norm, scores[rows:] - norms)
        probs = jnp.exp2(exponent * jnp.where(block == me, 0.0, scores))
        prob_grad = dot_nt(second_side, second)
        prob_grad = jnp.where(earlier, prob_grad[:rows] - delta, prob_grad[rows:] - deltas)
        score_grad = probs * prob_grad
        sides = jnp.concatenate(
            [jnp.where(earlier, score_grad, 0.0), jnp.where(later, score_grad, 0.0)], axis=0
        ).astype(jnp.bfloat16)
        both_sum += dot_nn(sides, first)
        value_sum += dot_nn(jnp.where(later, probs, 0.0).astype(jnp.bfloat16), second)
        return both_sum, value_sum

    sums = (jnp.concatenate([query_sum, key_sum], axis=0), value_sum)
    count = got_ref.shape[0] // group
    if count == 1:
        sums = step(0, sums)
    else:
        sums = lax.fori_loop(0, count, step, sums)
    grads[:, :width] = (scale * sums[0][:rows]).astype(jnp.bfloat16)
    grads[:, width : 2 * width] = (scale * sums[0][rows:]).astype(jnp.bfloat16)
    grads[:, 2 * width :] = sums[1].astype(jnp.bfloat16)
    for copy in copies:
        copy.wait()
    parts, _, part = out_ref.shape
    cols = math.gcd(part, 512)
    for h in range(parts):
        for at in range(0, part, cols):
            weight = w_all[h * part + at : h * part + at + cols, :]
            out_ref[h, :, at : at + cols] = dot_nt(grads[...], weight).astype(jnp.bfloat16)


def send_kernel(q_in, k_in, v_in, g_in, a_in, n_in, *refs):
    q_ref, k_ref, v_ref, g_ref, a_ref, n_ref, extra_ref, in_sems, row_sems, extra_sems = refs[-10:]
    hops = refs[:-10]
    me = lax.axis_index("ctx")
    rows, width = g_ref.shape
    pairs = (
        (k_in, k_ref),
        (v_in, v_ref),
        (q_in, q_ref),
        (g_in, g_ref),
        (a_in, a_ref),
        (n_in, n_ref),
    )
    loads = [pltpu.make_async_copy(*pair, in_sems.at[at]) for at, pair in enumerate(pairs)]
    for load in loads:
        load.start()

    def moves(bit, first, second):
        return [
            pltpu.make_async_copy(
                src, hops[bit].at[:rows, at * width : (at + 1) * width], row_sems.at[2 * bit + at]
            )
            for at, src in enumerate((first, second))
        ]

    for load in loads:
        load.wait()
    for bit in range(len(hops)):
        later = (me & (1 << bit)) == 0

        @pl.when(later)
        def _():
            for move in moves(bit, k_ref, v_ref):
                move.start()

        @pl.when(jnp.logical_not(later))
        def _():
            for move in moves(bit, q_ref, g_ref):
                move.start()

    delta = delta_of(g_ref[...], a_ref[...])
    delta = jnp.sum(jnp.where(diagonal(rows), delta, 0.0), axis=0, keepdims=True)
    row = lax.broadcasted_iota(jnp.int32, (EXTRA, rows), 0)
    extra = jnp.zeros((EXTRA, rows), jnp.float32)
    for at, part in enumerate(pieces_of(n_ref[...]) + pieces_of(delta)):
        extra = jnp.where(row == at, part, extra)
    extra_ref[:, :width] = extra.astype(jnp.bfloat16)
    extra_ref[:, width:] = jnp.zeros((EXTRA, width), jnp.bfloat16)
    tails = [
        pltpu.make_async_copy(extra_ref, hop.at[rows:, :], extra_sems.at[bit])
        for bit, hop in enumerate(hops)
    ]
    for tail in tails:
        tail.start()
    for bit in range(len(hops)):
        for move in moves(bit, k_ref, v_ref):
            move.wait()
    for tail in tails:
        tail.wait()


def project(grads, w_refs, start, out_ref):
    part = out_ref.shape[1]
    cols = part if part < 512 else math.gcd(part, 512)
    for at in range(0, part, cols):
        span = pl.ds(pl.multiple_of(start + at, 128), cols)
        weight = jnp.concatenate([ref[span, :] for ref in w_refs], axis=1)
        out_ref[:, at : at + cols] = dot_nt(grads[...], weight).astype(out_ref.dtype)


def near_kernel(scale, part, q_ref, k_ref, v_ref, g_ref, a_ref, n_ref, wq_ref, wk_ref, wv_ref, *refs):
    grads, front = refs[-2:]
    got = refs[:-2]
    rows, width = q_ref.shape
    me = lax.axis_index("ctx")
    exponent = scale * math.log2(math.e)
    query, key, value, grad = q_ref[...], k_ref[...], v_ref[...], g_ref[...]
    norm = jnp.sum(jnp.where(diagonal(rows), n_ref[...], 0.0), axis=1, keepdims=True)
    delta = delta_of(grad, a_ref[...])
    row_at = lax.broadcasted_iota(jnp.int32, (rows, rows), 0)
    col_at = lax.broadcasted_iota(jnp.int32, (rows, rows), 1)
    probs = jnp.where(col_at <= row_at, jnp.exp2(exponent * (dot_nt(query, key) - norm)), 0.0)
    score_low = (probs * (dot_nt(grad, value) - delta)).astype(jnp.bfloat16)
    query_sum = dot_nn(score_low, key)
    key_sum = dot_tn(score_low, query)
    value_sum = dot_tn(probs.astype(jnp.bfloat16), grad)

    first = jnp.concatenate([ref[:rows, :width] for ref in got], axis=0)
    second = jnp.concatenate([ref[:rows, width:] for ref in got], axis=0)
    extra = jnp.concatenate([ref[rows:, :width] for ref in got], axis=1).astype(jnp.float32)
    norms = (1.0 / scale) * jnp.sum(extra[:PIECES], axis=0, keepdims=True)
    deltas = jnp.sum(extra[PIECES : 2 * PIECES], axis=0, keepdims=True)
    lanes = lax.broadcasted_iota(jnp.int32, (rows, len(got) * rows), 1)
    earlier = ((lanes // rows + 1) ^ me) < me
    scores = dot_nt(jnp.concatenate([query, key], axis=0), first)
    scores = jnp.where(earlier, scores[:rows] - norm, scores[rows:] - norms)
    probs = jnp.exp2(exponent * scores)
    prob_grad = dot_nt(jnp.concatenate([grad, value], axis=0), second)
    prob_grad = jnp.where(earlier, prob_grad[:rows] - delta, prob_grad[rows:] - deltas)
    score_grad = probs * prob_grad
    sides = jnp.concatenate(
        [jnp.where(earlier, score_grad, 0.0), jnp.where(earlier, 0.0, score_grad)], axis=0
    ).astype(jnp.bfloat16)
    both_sum = dot_nn(sides, first)
    value_sum += dot_nn(jnp.where(earlier, 0.0, probs).astype(jnp.bfloat16), second)
    grads[:, :width] = (scale * (query_sum + both_sum[:rows])).astype(jnp.bfloat16)
    grads[:, width : 2 * width] = (scale * (key_sum + both_sum[rows:])).astype(jnp.bfloat16)
    grads[:, 2 * width :] = value_sum.astype(jnp.bfloat16)
    start = (lax.axis_index("head") ^ 3) * part
    project(grads, (wq_ref, wk_ref, wv_ref), start, front)


def far_kernel(part, grads, wq_ref, wk_ref, wv_ref, front, back, third, second):
    w_refs = (wq_ref, wk_ref, wv_ref)
    head = lax.axis_index("head")
    start = (head ^ 2) * part
    size = front.shape[1]
    project(grads, w_refs, (head ^ 3) * part + 2 * size, third)
    project(grads, w_refs, start + 2 * size, second)
    project(grads, w_refs, start, front)
    project(grads, w_refs, start + size, back)


def close_kernel(part, grads, wq_ref, wk_ref, wv_ref, last, near, mine):
    w_refs = (wq_ref, wk_ref, wv_ref)
    head = lax.axis_index("head")
    project(grads, w_refs, (head ^ 3) * part + last.shape[1], last)
    project(grads, w_refs, (head ^ 1) * part, near)
    project(grads, w_refs, head * part, mine)


def swap(value, axis, offset):
    size = lax.axis_size(axis)
    return lax.ppermute(value, axis, [(at, at ^ offset) for at in range(size)])


def near_body(own, weights, scale):
    rows, width = own[0].shape
    depth = weights[0].shape[0]
    ctx = lax.axis_size("ctx")
    part = depth // lax.axis_size("head")
    vmem = pl.BlockSpec(memory_space=pltpu.VMEM)
    hbm = pl.BlockSpec(memory_space=pl.ANY)
    params = pltpu.CompilerParams(vmem_limit_bytes=32 * MIB)
    hop = jax.ShapeDtypeStruct((rows + EXTRA, 2 * width), jnp.bfloat16)
    bits = (ctx - 1).bit_length()
    sent = pl.pallas_call(
        send_kernel,
        out_shape=[hop] * bits,
        in_specs=[hbm] * 6,
        out_specs=[hbm] * bits,
        scratch_shapes=[pltpu.VMEM((rows, width), jnp.bfloat16)] * 5
        + [
            pltpu.VMEM((1, rows), jnp.float32),
            pltpu.VMEM((EXTRA, 2 * width), jnp.bfloat16),
            pltpu.SemaphoreType.DMA((6,)),
            pltpu.SemaphoreType.DMA((2 * bits,)),
            pltpu.SemaphoreType.DMA((bits,)),
        ],
        compiler_params=pltpu.CompilerParams(vmem_limit_bytes=56 * MIB),
        cost_estimate=pl.CostEstimate(
            flops=5000000000, bytes_accessed=20 * rows * width, transcendentals=0
        ),
    )(*own)
    got = {at: swap(sent[at.bit_length() - 1], "ctx", at) for at in (1, *range(2, ctx, 2))}
    soon = [at for at in (6,) if at < ctx]
    early, norm = lax.optimization_barrier((tuple(got[at] for at in soon), own[-1]))
    got.update(zip(soon, early))
    own = own[:-1] + (norm * (1.0 / scale),)
    for at in range(2, ctx, 2):
        got[at + 1] = swap(got[at], "ctx", 1)
    got = [got[at] for at in range(1, ctx)]
    straight = part // 4
    size = (part - straight) // 2
    half_low = jax.ShapeDtypeStruct((rows, size), jnp.bfloat16)
    half = jax.ShapeDtypeStruct((rows, size), jnp.float32)
    piece = jax.ShapeDtypeStruct((rows, straight), jnp.bfloat16)
    low = jax.ShapeDtypeStruct((rows, part), jnp.bfloat16)
    full = jax.ShapeDtypeStruct((rows, part), jnp.float32)
    grads, front = pl.pallas_call(
        functools.partial(near_kernel, scale, part),
        out_shape=[jax.ShapeDtypeStruct((rows, 3 * width), jnp.bfloat16), half_low],
        in_specs=[vmem] * (ctx + 8),
        out_specs=[vmem] * 2,
        compiler_params=params,
        cost_estimate=pl.CostEstimate(
            flops=14 * rows * rows * ctx * width + 6 * rows * width * part,
            bytes_accessed=4 * rows * ctx * width + 6 * part * width,
            transcendentals=rows * rows * ctx,
        ),
    )(*own, *weights, *got)
    front = swap(front, "head", 1)
    def projected(kernel, outs, operands):
        count = sum(out.shape[1] for out in outs)
        return pl.pallas_call(
            functools.partial(kernel, part),
            out_shape=outs,
            in_specs=[vmem] * (1 + len(weights)),
            out_specs=[vmem] * len(outs),
            compiler_params=params,
            cost_estimate=pl.CostEstimate(
                flops=6 * rows * width * count, bytes_accessed=6 * count * width, transcendentals=0
            ),
        )(*operands)

    two_front, two_back, third, second = projected(
        far_kernel, [half, half, piece, piece], (grads, *weights)
    )
    third, second = swap(third, "head", 3), swap(second, "head", 2)
    grads, two_front = lax.optimization_barrier((grads, two_front))
    back, near, total = projected(close_kernel, [half_low, low, full], (grads, *weights))
    back = swap(back, "head", 1)
    near, back = lax.optimization_barrier((near, back))
    front = swap((two_front + front.astype(jnp.float32)).astype(jnp.bfloat16), "head", 2)
    back = swap((two_back + back.astype(jnp.float32)).astype(jnp.bfloat16), "head", 2)
    near = swap(near, "head", 1)
    direct = second.astype(jnp.float32) + third.astype(jnp.float32)
    far_sum = jnp.concatenate([front, back], axis=1).astype(jnp.float32)
    far_sum = jnp.concatenate([far_sum, direct], axis=1)
    return (total + near.astype(jnp.float32) + far_sum).astype(jnp.bfloat16)


def far_body(own, weights, scale):
    rows, width = own[0].shape
    depth = weights[0].shape[0]
    ctx = lax.axis_size("ctx")
    parts = lax.axis_size("head")
    spot = lax.axis_index("ctx").astype(jnp.int32).reshape(1)
    vmem = pl.BlockSpec(memory_space=pltpu.VMEM)
    smem = pl.BlockSpec(memory_space=pltpu.SMEM)
    hbm = pl.BlockSpec(memory_space=pl.ANY)
    packed = pl.pallas_call(
        pack_kernel,
        out_shape=jax.ShapeDtypeStruct((ctx, rows + EXTRA, 2 * width), jnp.bfloat16),
        in_specs=[smem] + [vmem] * 6,
        out_specs=vmem,
        compiler_params=pltpu.CompilerParams(vmem_limit_bytes=32 * MIB),
    )(spot, *own)
    got = lax.all_to_all(packed, "ctx", split_axis=0, concat_axis=0, tiled=True)
    total = ctx * rows
    group = math.gcd(ctx, 8)
    parted = pl.pallas_call(
        functools.partial(main_kernel, group, scale),
        out_shape=jax.ShapeDtypeStruct((parts, rows, depth // parts), jnp.bfloat16),
        in_specs=[smem] + [vmem] * 7 + [hbm] * 3,
        out_specs=vmem,
        scratch_shapes=[
            pltpu.VMEM((depth, 3 * width), jnp.bfloat16),
            pltpu.VMEM((rows, 3 * width), jnp.bfloat16),
            pltpu.SemaphoreType.DMA((3,)),
        ],
        compiler_params=pltpu.CompilerParams(vmem_limit_bytes=48 * MIB),
        cost_estimate=pl.CostEstimate(
            flops=14 * rows * total * width + 6 * rows * width * depth,
            bytes_accessed=6 * depth * width + 10 * total * width,
            transcendentals=2 * rows * total,
        ),
    )(spot, got, *own, *weights)
    swapped = lax.all_to_all(parted, "head", split_axis=0, concat_axis=0, tiled=True)
    return jnp.sum(swapped.astype(jnp.float32), axis=0).astype(jnp.bfloat16)


def body(
    queries,
    key_rows,
    value_rows,
    out_grad,
    attn_out,
    log_norm,
    query_weight,
    key_weight,
    value_weight,
):
    rows, width = queries.shape
    ctx, parts = lax.axis_size("ctx"), lax.axis_size("head")
    own = (queries, key_rows, value_rows, out_grad, attn_out, log_norm.reshape(1, rows))
    weights = (query_weight, key_weight, value_weight)
    near = ctx <= 8 and parts == 4 and ctx & (ctx - 1) == 0
    return (near_body if near else far_body)(own, weights, width ** (-0.5))


def solution(mesh):
    return jax.shard_map(
        body,
        mesh=mesh,
        in_specs=(P("ctx", "head"),) * 6 + (P(None, "head"),) * 3,
        out_specs=P("ctx", "head"),
        check_vma=False,
    )
```

```python
import functools
import math

import jax
import jax.numpy as jnp
from jax import lax
from jax.experimental import pallas as pl
from jax.experimental.pallas import tpu as pltpu
from jax.sharding import PartitionSpec as P

NT = (((1,), (1,)), ((), ()))
TN = (((0,), (0,)), ((), ()))
PIECES = 3
EXTRA = 16
MIB = 1024 * 1024


def dot_nt(left, right):
    return lax.dot_general(left, right, NT, preferred_element_type=jnp.float32)


def dot_tn(left, right):
    return lax.dot_general(left, right, TN, preferred_element_type=jnp.float32)


def dot_nn(left, right):
    return jnp.dot(left, right, preferred_element_type=jnp.float32)


def pieces_of(value):
    out = []
    rest = value
    for _ in range(PIECES):
        low = rest.astype(jnp.bfloat16).astype(jnp.float32)
        out.append(low)
        rest = rest - low
    return out


def diagonal(rows):
    row_at = lax.broadcasted_iota(jnp.int32, (rows, rows), 0)
    col_at = lax.broadcasted_iota(jnp.int32, (rows, rows), 1)
    return row_at == col_at


def delta_of(grad, attn):
    return jnp.sum(grad.astype(jnp.float32) * attn.astype(jnp.float32), axis=1, keepdims=True)


def pack_kernel(me_ref, q_ref, k_ref, v_ref, g_ref, a_ref, n_ref, out_ref):
    rows, width = q_ref.shape
    me = me_ref[0]
    delta = delta_of(g_ref[...], a_ref[...])
    delta = jnp.sum(jnp.where(diagonal(rows), delta, 0.0), axis=0, keepdims=True)
    row = lax.broadcasted_iota(jnp.int32, (EXTRA, rows), 0)
    extra = jnp.zeros((EXTRA, rows), jnp.float32)
    for at, piece in enumerate(pieces_of(n_ref[...]) + pieces_of(delta)):
        extra = jnp.where(row == at, piece, extra)
    extra = extra.astype(jnp.bfloat16)

    def for_later(at, carry):
        out_ref[at, :rows, :width] = k_ref[...]
        out_ref[at, :rows, width:] = v_ref[...]
        out_ref[at, rows:, :] = jnp.zeros((EXTRA, 2 * width), jnp.bfloat16)
        return carry

    def for_earlier(at, carry):
        out_ref[at, :rows, :width] = q_ref[...]
        out_ref[at, :rows, width:] = g_ref[...]
        out_ref[at, rows:, :width] = extra
        out_ref[at, rows:, width:] = jnp.zeros((EXTRA, width), jnp.bfloat16)
        return carry

    lax.fori_loop(0, me + 1, for_earlier, 0)
    lax.fori_loop(me + 1, out_ref.shape[0], for_later, 0)


def main_kernel(
    group,
    scale,
    me_ref,
    got_ref,
    q_ref,
    k_ref,
    v_ref,
    g_ref,
    a_ref,
    n_ref,
    wq_ref,
    wk_ref,
    wv_ref,
    out_ref,
    w_all,
    grads,
    sems,
):
    rows, width = q_ref.shape
    copies = [
        pltpu.make_async_copy(ref, w_all.at[:, at * width : (at + 1) * width], sems.at[at])
        for at, ref in enumerate((wq_ref, wk_ref, wv_ref))
    ]
    for copy in copies:
        copy.start()
    me = me_ref[0]
    exponent = scale * math.log2(math.e)
    query, key, value, grad = q_ref[...], k_ref[...], v_ref[...], g_ref[...]
    eye = diagonal(rows)
    norm = (1.0 / scale) * jnp.sum(jnp.where(eye, n_ref[...], 0.0), axis=1, keepdims=True)
    delta = delta_of(grad, a_ref[...])

    row_at = lax.broadcasted_iota(jnp.int32, (rows, rows), 0)
    col_at = lax.broadcasted_iota(jnp.int32, (rows, rows), 1)
    probs = jnp.where(col_at <= row_at, jnp.exp2(exponent * (dot_nt(query, key) - norm)), 0.0)
    score_low = (probs * (dot_nt(grad, value) - delta)).astype(jnp.bfloat16)
    query_sum = dot_nn(score_low, key)
    key_sum = dot_tn(score_low, query)
    value_sum = dot_tn(probs.astype(jnp.bfloat16), grad)

    first_side = jnp.concatenate([query, key], axis=0)
    second_side = jnp.concatenate([grad, value], axis=0)

    def step(at, sums):
        both_sum, value_sum = sums
        blocks = [at * group + i for i in range(group)]
        first = jnp.concatenate([got_ref[b, :rows, :width] for b in blocks], axis=0)
        second = jnp.concatenate([got_ref[b, :rows, width:] for b in blocks], axis=0)
        extra = jnp.concatenate([got_ref[b, rows:, :width] for b in blocks], axis=1)
        extra = extra.astype(jnp.float32)
        norms = (1.0 / scale) * jnp.sum(extra[:PIECES], axis=0, keepdims=True)
        deltas = jnp.sum(extra[PIECES : 2 * PIECES], axis=0, keepdims=True)
        block = at * group + lax.broadcasted_iota(jnp.int32, (rows, group * rows), 1) // rows
        earlier, later = block < me, block > me
        scores = dot_nt(first_side, first)
        scores = jnp.where(earlier, scores[:rows] - norm, scores[rows:] - norms)
        probs = jnp.exp2(exponent * jnp.where(block == me, 0.0, scores))
        prob_grad = dot_nt(second_side, second)
        prob_grad = jnp.where(earlier, prob_grad[:rows] - delta, prob_grad[rows:] - deltas)
        score_grad = probs * prob_grad
        sides = jnp.concatenate(
            [jnp.where(earlier, score_grad, 0.0), jnp.where(later, score_grad, 0.0)], axis=0
        ).astype(jnp.bfloat16)
        both_sum += dot_nn(sides, first)
        value_sum += dot_nn(jnp.where(later, probs, 0.0).astype(jnp.bfloat16), second)
        return both_sum, value_sum

    sums = (jnp.concatenate([query_sum, key_sum], axis=0), value_sum)
    count = got_ref.shape[0] // group
    if count == 1:
        sums = step(0, sums)
    else:
        sums = lax.fori_loop(0, count, step, sums)
    grads[:, :width] = (scale * sums[0][:rows]).astype(jnp.bfloat16)
    grads[:, width : 2 * width] = (scale * sums[0][rows:]).astype(jnp.bfloat16)
    grads[:, 2 * width :] = sums[1].astype(jnp.bfloat16)
    for copy in copies:
        copy.wait()
    parts, _, part = out_ref.shape
    cols = math.gcd(part, 512)
    for h in range(parts):
        for at in range(0, part, cols):
            weight = w_all[h * part + at : h * part + at + cols, :]
            out_ref[h, :, at : at + cols] = dot_nt(grads[...], weight).astype(jnp.bfloat16)


def send_kernel(q_in, k_in, v_in, g_in, a_in, n_in, *refs):
    q_ref, k_ref, v_ref, g_ref, a_ref, n_ref, extra_ref, in_sems, row_sems, extra_sems = refs[-10:]
    hops = refs[:-10]
    me = lax.axis_index("ctx")
    rows, width = g_ref.shape
    pairs = (
        (k_in, k_ref),
        (v_in, v_ref),
        (q_in, q_ref),
        (g_in, g_ref),
        (a_in, a_ref),
        (n_in, n_ref),
    )
    loads = [pltpu.make_async_copy(*pair, in_sems.at[at]) for at, pair in enumerate(pairs)]
    for load in loads:
        load.start()

    def moves(bit, first, second):
        return [
            pltpu.make_async_copy(
                src, hops[bit].at[:rows, at * width : (at + 1) * width], row_sems.at[2 * bit + at]
            )
            for at, src in enumerate((first, second))
        ]

    for load in loads:
        load.wait()
    for bit in range(len(hops)):
        later = (me & (1 << bit)) == 0

        @pl.when(later)
        def _():
            for move in moves(bit, k_ref, v_ref):
                move.start()

        @pl.when(jnp.logical_not(later))
        def _():
            for move in moves(bit, q_ref, g_ref):
                move.start()

    delta = delta_of(g_ref[...], a_ref[...])
    delta = jnp.sum(jnp.where(diagonal(rows), delta, 0.0), axis=0, keepdims=True)
    row = lax.broadcasted_iota(jnp.int32, (EXTRA, rows), 0)
    extra = jnp.zeros((EXTRA, rows), jnp.float32)
    for at, part in enumerate(pieces_of(n_ref[...]) + pieces_of(delta)):
        extra = jnp.where(row == at, part, extra)
    extra_ref[:, :width] = extra.astype(jnp.bfloat16)
    extra_ref[:, width:] = jnp.zeros((EXTRA, width), jnp.bfloat16)
    tails = [
        pltpu.make_async_copy(extra_ref, hop.at[rows:, :], extra_sems.at[bit])
        for bit, hop in enumerate(hops)
    ]
    for tail in tails:
        tail.start()
    for bit in range(len(hops)):
        for move in moves(bit, k_ref, v_ref):
            move.wait()
    for tail in tails:
        tail.wait()


def project(grads, w_refs, start, out_ref):
    part = out_ref.shape[1]
    cols = math.gcd(part, 512)
    for at in range(0, part, cols):
        span = pl.ds(pl.multiple_of(start + at, cols), cols)
        weight = jnp.concatenate([ref[span, :] for ref in w_refs], axis=1)
        out_ref[:, at : at + cols] = dot_nt(grads[...], weight).astype(out_ref.dtype)


def near_kernel(scale, part, q_ref, k_ref, v_ref, g_ref, a_ref, n_ref, wq_ref, wk_ref, wv_ref, *refs):
    grads, front = refs[-2:]
    got = refs[:-2]
    rows, width = q_ref.shape
    me = lax.axis_index("ctx")
    exponent = scale * math.log2(math.e)
    query, key, value, grad = q_ref[...], k_ref[...], v_ref[...], g_ref[...]
    norm = jnp.sum(jnp.where(diagonal(rows), n_ref[...], 0.0), axis=1, keepdims=True)
    delta = delta_of(grad, a_ref[...])
    row_at = lax.broadcasted_iota(jnp.int32, (rows, rows), 0)
    col_at = lax.broadcasted_iota(jnp.int32, (rows, rows), 1)
    probs = jnp.where(col_at <= row_at, jnp.exp2(exponent * (dot_nt(query, key) - norm)), 0.0)
    score_low = (probs * (dot_nt(grad, value) - delta)).astype(jnp.bfloat16)
    query_sum = dot_nn(score_low, key)
    key_sum = dot_tn(score_low, query)
    value_sum = dot_tn(probs.astype(jnp.bfloat16), grad)

    first = jnp.concatenate([ref[:rows, :width] for ref in got], axis=0)
    second = jnp.concatenate([ref[:rows, width:] for ref in got], axis=0)
    extra = jnp.concatenate([ref[rows:, :width] for ref in got], axis=1).astype(jnp.float32)
    norms = (1.0 / scale) * jnp.sum(extra[:PIECES], axis=0, keepdims=True)
    deltas = jnp.sum(extra[PIECES : 2 * PIECES], axis=0, keepdims=True)
    lanes = lax.broadcasted_iota(jnp.int32, (rows, len(got) * rows), 1)
    earlier = ((lanes // rows + 1) ^ me) < me
    scores = dot_nt(jnp.concatenate([query, key], axis=0), first)
    scores = jnp.where(earlier, scores[:rows] - norm, scores[rows:] - norms)
    probs = jnp.exp2(exponent * scores)
    prob_grad = dot_nt(jnp.concatenate([grad, value], axis=0), second)
    prob_grad = jnp.where(earlier, prob_grad[:rows] - delta, prob_grad[rows:] - deltas)
    score_grad = probs * prob_grad
    sides = jnp.concatenate(
        [jnp.where(earlier, score_grad, 0.0), jnp.where(earlier, 0.0, score_grad)], axis=0
    ).astype(jnp.bfloat16)
    both_sum = dot_nn(sides, first)
    value_sum += dot_nn(jnp.where(earlier, 0.0, probs).astype(jnp.bfloat16), second)
    grads[:, :width] = (scale * (query_sum + both_sum[:rows])).astype(jnp.bfloat16)
    grads[:, width : 2 * width] = (scale * (key_sum + both_sum[rows:])).astype(jnp.bfloat16)
    grads[:, 2 * width :] = value_sum.astype(jnp.bfloat16)
    start = (lax.axis_index("head") ^ 3) * part
    project(grads, (wq_ref, wk_ref, wv_ref), start, front)


def far_kernel(part, grads, wq_ref, wk_ref, wv_ref, front, back):
    w_refs = (wq_ref, wk_ref, wv_ref)
    head = lax.axis_index("head")
    start = (head ^ 2) * part
    project(grads, w_refs, start, front)
    project(grads, w_refs, start + part // 2, back)


def close_kernel(part, grads, wq_ref, wk_ref, wv_ref, last, near, mine):
    w_refs = (wq_ref, wk_ref, wv_ref)
    head = lax.axis_index("head")
    project(grads, w_refs, (head ^ 3) * part + part // 2, last)
    project(grads, w_refs, (head ^ 1) * part, near)
    project(grads, w_refs, head * part, mine)


def swap(value, axis, offset):
    size = lax.axis_size(axis)
    return lax.ppermute(value, axis, [(at, at ^ offset) for at in range(size)])


def near_body(own, weights, scale):
    rows, width = own[0].shape
    depth = weights[0].shape[0]
    ctx = lax.axis_size("ctx")
    part = depth // lax.axis_size("head")
    vmem = pl.BlockSpec(memory_space=pltpu.VMEM)
    hbm = pl.BlockSpec(memory_space=pl.ANY)
    params = pltpu.CompilerParams(vmem_limit_bytes=32 * MIB)
    hop = jax.ShapeDtypeStruct((rows + EXTRA, 2 * width), jnp.bfloat16)
    bits = (ctx - 1).bit_length()
    sent = pl.pallas_call(
        send_kernel,
        out_shape=[hop] * bits,
        in_specs=[hbm] * 6,
        out_specs=[hbm] * bits,
        scratch_shapes=[pltpu.VMEM((rows, width), jnp.bfloat16)] * 5
        + [
            pltpu.VMEM((1, rows), jnp.float32),
            pltpu.VMEM((EXTRA, 2 * width), jnp.bfloat16),
            pltpu.SemaphoreType.DMA((6,)),
            pltpu.SemaphoreType.DMA((2 * bits,)),
            pltpu.SemaphoreType.DMA((bits,)),
        ],
        compiler_params=pltpu.CompilerParams(vmem_limit_bytes=56 * MIB),
        cost_estimate=pl.CostEstimate(
            flops=5000000000, bytes_accessed=20 * rows * width, transcendentals=0
        ),
    )(*own)
    got = {at: swap(sent[at.bit_length() - 1], "ctx", at) for at in (1, *range(2, ctx, 2))}
    soon = [at for at in (6,) if at < ctx]
    early, norm = lax.optimization_barrier((tuple(got[at] for at in soon), own[-1]))
    got.update(zip(soon, early))
    own = own[:-1] + (norm * (1.0 / scale),)
    for at in range(2, ctx, 2):
        got[at + 1] = swap(got[at], "ctx", 1)
    got = [got[at] for at in range(1, ctx)]
    half_low = jax.ShapeDtypeStruct((rows, part // 2), jnp.bfloat16)
    half = jax.ShapeDtypeStruct((rows, part // 2), jnp.float32)
    low = jax.ShapeDtypeStruct((rows, part), jnp.bfloat16)
    full = jax.ShapeDtypeStruct((rows, part), jnp.float32)
    grads, front = pl.pallas_call(
        functools.partial(near_kernel, scale, part),
        out_shape=[jax.ShapeDtypeStruct((rows, 3 * width), jnp.bfloat16), half_low],
        in_specs=[vmem] * (ctx + 8),
        out_specs=[vmem] * 2,
        compiler_params=params,
        cost_estimate=pl.CostEstimate(
            flops=14 * rows * rows * ctx * width + 6 * rows * width * part,
            bytes_accessed=4 * rows * ctx * width + 6 * part * width,
            transcendentals=rows * rows * ctx,
        ),
    )(*own, *weights, *got)
    front = swap(front, "head", 1)
    def projected(kernel, outs, operands):
        count = sum(out.shape[1] for out in outs)
        return pl.pallas_call(
            functools.partial(kernel, part),
            out_shape=outs,
            in_specs=[vmem] * (1 + len(weights)),
            out_specs=[vmem] * len(outs),
            compiler_params=params,
            cost_estimate=pl.CostEstimate(
                flops=6 * rows * width * count, bytes_accessed=6 * count * width, transcendentals=0
            ),
        )(*operands)

    two_front, two_back = projected(far_kernel, [half, half], (grads, *weights))
    grads, two_front = lax.optimization_barrier((grads, two_front))
    back, near, total = projected(close_kernel, [half_low, low, full], (grads, *weights))
    back = swap(back, "head", 1)
    near, front = lax.optimization_barrier((near, front))
    front = swap((two_front + front.astype(jnp.float32)).astype(jnp.bfloat16), "head", 2)
    back = swap((two_back + back.astype(jnp.float32)).astype(jnp.bfloat16), "head", 2)
    near = swap(near, "head", 1)
    far_sum = jnp.concatenate([front, back], axis=1).astype(jnp.float32)
    return (total + near.astype(jnp.float32) + far_sum).astype(jnp.bfloat16)


def far_body(own, weights, scale):
    rows, width = own[0].shape
    depth = weights[0].shape[0]
    ctx = lax.axis_size("ctx")
    parts = lax.axis_size("head")
    spot = lax.axis_index("ctx").astype(jnp.int32).reshape(1)
    vmem = pl.BlockSpec(memory_space=pltpu.VMEM)
    smem = pl.BlockSpec(memory_space=pltpu.SMEM)
    hbm = pl.BlockSpec(memory_space=pl.ANY)
    packed = pl.pallas_call(
        pack_kernel,
        out_shape=jax.ShapeDtypeStruct((ctx, rows + EXTRA, 2 * width), jnp.bfloat16),
        in_specs=[smem] + [vmem] * 6,
        out_specs=vmem,
        compiler_params=pltpu.CompilerParams(vmem_limit_bytes=32 * MIB),
    )(spot, *own)
    got = lax.all_to_all(packed, "ctx", split_axis=0, concat_axis=0, tiled=True)
    total = ctx * rows
    group = math.gcd(ctx, 8)
    parted = pl.pallas_call(
        functools.partial(main_kernel, group, scale),
        out_shape=jax.ShapeDtypeStruct((parts, rows, depth // parts), jnp.bfloat16),
        in_specs=[smem] + [vmem] * 7 + [hbm] * 3,
        out_specs=vmem,
        scratch_shapes=[
            pltpu.VMEM((depth, 3 * width), jnp.bfloat16),
            pltpu.VMEM((rows, 3 * width), jnp.bfloat16),
            pltpu.SemaphoreType.DMA((3,)),
        ],
        compiler_params=pltpu.CompilerParams(vmem_limit_bytes=48 * MIB),
        cost_estimate=pl.CostEstimate(
            flops=14 * rows * total * width + 6 * rows * width * depth,
            bytes_accessed=6 * depth * width + 10 * total * width,
            transcendentals=2 * rows * total,
        ),
    )(spot, got, *own, *weights)
    swapped = lax.all_to_all(parted, "head", split_axis=0, concat_axis=0, tiled=True)
    return jnp.sum(swapped.astype(jnp.float32), axis=0).astype(jnp.bfloat16)


def body(
    queries,
    key_rows,
    value_rows,
    out_grad,
    attn_out,
    log_norm,
    query_weight,
    key_weight,
    value_weight,
):
    rows, width = queries.shape
    ctx, parts = lax.axis_size("ctx"), lax.axis_size("head")
    own = (queries, key_rows, value_rows, out_grad, attn_out, log_norm.reshape(1, rows))
    weights = (query_weight, key_weight, value_weight)
    near = ctx <= 8 and parts == 4 and ctx & (ctx - 1) == 0
    return (near_body if near else far_body)(own, weights, width ** (-0.5))


def solution(mesh):
    return jax.shard_map(
        body,
        mesh=mesh,
        in_specs=(P("ctx", "head"),) * 6 + (P(None, "head"),) * 3,
        out_specs=P("ctx", "head"),
        check_vma=False,
    )
```

```python
import functools
import math

import jax
import jax.numpy as jnp
from jax import lax
from jax.experimental import pallas as pl
from jax.experimental.pallas import tpu as pltpu
from jax.sharding import PartitionSpec as P

NT = (((1,), (1,)), ((), ()))
TN = (((0,), (0,)), ((), ()))
PIECES = 3
EXTRA = 16
MIB = 1024 * 1024


def dot_nt(left, right):
    return lax.dot_general(left, right, NT, preferred_element_type=jnp.float32)


def dot_tn(left, right):
    return lax.dot_general(left, right, TN, preferred_element_type=jnp.float32)


def dot_nn(left, right):
    return jnp.dot(left, right, preferred_element_type=jnp.float32)


def pieces_of(value):
    out = []
    rest = value
    for _ in range(PIECES):
        low = rest.astype(jnp.bfloat16).astype(jnp.float32)
        out.append(low)
        rest = rest - low
    return out


def diagonal(rows):
    row_at = lax.broadcasted_iota(jnp.int32, (rows, rows), 0)
    col_at = lax.broadcasted_iota(jnp.int32, (rows, rows), 1)
    return row_at == col_at


def delta_of(grad, attn):
    return jnp.sum(grad.astype(jnp.float32) * attn.astype(jnp.float32), axis=1, keepdims=True)


def pack_kernel(me_ref, q_ref, k_ref, v_ref, g_ref, a_ref, n_ref, out_ref):
    rows, width = q_ref.shape
    me = me_ref[0]
    delta = delta_of(g_ref[...], a_ref[...])
    delta = jnp.sum(jnp.where(diagonal(rows), delta, 0.0), axis=0, keepdims=True)
    row = lax.broadcasted_iota(jnp.int32, (EXTRA, rows), 0)
    extra = jnp.zeros((EXTRA, rows), jnp.float32)
    for at, piece in enumerate(pieces_of(n_ref[...]) + pieces_of(delta)):
        extra = jnp.where(row == at, piece, extra)
    extra = extra.astype(jnp.bfloat16)

    def for_later(at, carry):
        out_ref[at, :rows, :width] = k_ref[...]
        out_ref[at, :rows, width:] = v_ref[...]
        out_ref[at, rows:, :] = jnp.zeros((EXTRA, 2 * width), jnp.bfloat16)
        return carry

    def for_earlier(at, carry):
        out_ref[at, :rows, :width] = q_ref[...]
        out_ref[at, :rows, width:] = g_ref[...]
        out_ref[at, rows:, :width] = extra
        out_ref[at, rows:, width:] = jnp.zeros((EXTRA, width), jnp.bfloat16)
        return carry

    lax.fori_loop(0, me + 1, for_earlier, 0)
    lax.fori_loop(me + 1, out_ref.shape[0], for_later, 0)


def main_kernel(
    group,
    scale,
    me_ref,
    got_ref,
    q_ref,
    k_ref,
    v_ref,
    g_ref,
    a_ref,
    n_ref,
    wq_ref,
    wk_ref,
    wv_ref,
    out_ref,
    w_all,
    grads,
    sems,
):
    rows, width = q_ref.shape
    copies = [
        pltpu.make_async_copy(ref, w_all.at[:, at * width : (at + 1) * width], sems.at[at])
        for at, ref in enumerate((wq_ref, wk_ref, wv_ref))
    ]
    for copy in copies:
        copy.start()
    me = me_ref[0]
    exponent = scale * math.log2(math.e)
    query, key, value, grad = q_ref[...], k_ref[...], v_ref[...], g_ref[...]
    eye = diagonal(rows)
    norm = (1.0 / scale) * jnp.sum(jnp.where(eye, n_ref[...], 0.0), axis=1, keepdims=True)
    delta = delta_of(grad, a_ref[...])

    row_at = lax.broadcasted_iota(jnp.int32, (rows, rows), 0)
    col_at = lax.broadcasted_iota(jnp.int32, (rows, rows), 1)
    probs = jnp.where(col_at <= row_at, jnp.exp2(exponent * (dot_nt(query, key) - norm)), 0.0)
    score_low = (probs * (dot_nt(grad, value) - delta)).astype(jnp.bfloat16)
    query_sum = dot_nn(score_low, key)
    key_sum = dot_tn(score_low, query)
    value_sum = dot_tn(probs.astype(jnp.bfloat16), grad)

    first_side = jnp.concatenate([query, key], axis=0)
    second_side = jnp.concatenate([grad, value], axis=0)

    def step(at, sums):
        both_sum, value_sum = sums
        blocks = [at * group + i for i in range(group)]
        first = jnp.concatenate([got_ref[b, :rows, :width] for b in blocks], axis=0)
        second = jnp.concatenate([got_ref[b, :rows, width:] for b in blocks], axis=0)
        extra = jnp.concatenate([got_ref[b, rows:, :width] for b in blocks], axis=1)
        extra = extra.astype(jnp.float32)
        norms = (1.0 / scale) * jnp.sum(extra[:PIECES], axis=0, keepdims=True)
        deltas = jnp.sum(extra[PIECES : 2 * PIECES], axis=0, keepdims=True)
        block = at * group + lax.broadcasted_iota(jnp.int32, (rows, group * rows), 1) // rows
        earlier, later = block < me, block > me
        scores = dot_nt(first_side, first)
        scores = jnp.where(earlier, scores[:rows] - norm, scores[rows:] - norms)
        probs = jnp.exp2(exponent * jnp.where(block == me, 0.0, scores))
        prob_grad = dot_nt(second_side, second)
        prob_grad = jnp.where(earlier, prob_grad[:rows] - delta, prob_grad[rows:] - deltas)
        score_grad = probs * prob_grad
        sides = jnp.concatenate(
            [jnp.where(earlier, score_grad, 0.0), jnp.where(later, score_grad, 0.0)], axis=0
        ).astype(jnp.bfloat16)
        both_sum += dot_nn(sides, first)
        value_sum += dot_nn(jnp.where(later, probs, 0.0).astype(jnp.bfloat16), second)
        return both_sum, value_sum

    sums = (jnp.concatenate([query_sum, key_sum], axis=0), value_sum)
    count = got_ref.shape[0] // group
    if count == 1:
        sums = step(0, sums)
    else:
        sums = lax.fori_loop(0, count, step, sums)
    grads[:, :width] = (scale * sums[0][:rows]).astype(jnp.bfloat16)
    grads[:, width : 2 * width] = (scale * sums[0][rows:]).astype(jnp.bfloat16)
    grads[:, 2 * width :] = sums[1].astype(jnp.bfloat16)
    for copy in copies:
        copy.wait()
    parts, _, part = out_ref.shape
    cols = math.gcd(part, 512)
    for h in range(parts):
        for at in range(0, part, cols):
            weight = w_all[h * part + at : h * part + at + cols, :]
            out_ref[h, :, at : at + cols] = dot_nt(grads[...], weight).astype(jnp.bfloat16)


def send_kernel(q_in, k_in, v_in, g_in, a_in, n_in, *refs):
    q_ref, k_ref, v_ref, g_ref, a_ref, n_ref, extra_ref, in_sems, row_sems, extra_sems = refs[-10:]
    hops = refs[:-10]
    me = lax.axis_index("ctx")
    rows, width = g_ref.shape
    pairs = (
        (k_in, k_ref),
        (v_in, v_ref),
        (q_in, q_ref),
        (g_in, g_ref),
        (a_in, a_ref),
        (n_in, n_ref),
    )
    loads = [pltpu.make_async_copy(*pair, in_sems.at[at]) for at, pair in enumerate(pairs)]
    for load in loads:
        load.start()

    def moves(bit, first, second):
        return [
            pltpu.make_async_copy(
                src, hops[bit].at[:rows, at * width : (at + 1) * width], row_sems.at[2 * bit + at]
            )
            for at, src in enumerate((first, second))
        ]

    for load in loads:
        load.wait()
    for bit in range(len(hops)):
        later = (me & (1 << bit)) == 0

        @pl.when(later)
        def _():
            for move in moves(bit, k_ref, v_ref):
                move.start()

        @pl.when(jnp.logical_not(later))
        def _():
            for move in moves(bit, q_ref, g_ref):
                move.start()

    delta = delta_of(g_ref[...], a_ref[...])
    delta = jnp.sum(jnp.where(diagonal(rows), delta, 0.0), axis=0, keepdims=True)
    row = lax.broadcasted_iota(jnp.int32, (EXTRA, rows), 0)
    extra = jnp.zeros((EXTRA, rows), jnp.float32)
    for at, part in enumerate(pieces_of(n_ref[...]) + pieces_of(delta)):
        extra = jnp.where(row == at, part, extra)
    extra_ref[:, :width] = extra.astype(jnp.bfloat16)
    extra_ref[:, width:] = jnp.zeros((EXTRA, width), jnp.bfloat16)
    tails = [
        pltpu.make_async_copy(extra_ref, hop.at[rows:, :], extra_sems.at[bit])
        for bit, hop in enumerate(hops)
    ]
    for tail in tails:
        tail.start()
    for bit in range(len(hops)):
        for move in moves(bit, k_ref, v_ref):
            move.wait()
    for tail in tails:
        tail.wait()


def project(grads, w_refs, start, out_ref):
    part = out_ref.shape[1]
    cols = math.gcd(part, 512)
    for at in range(0, part, cols):
        span = pl.ds(pl.multiple_of(start + at, cols), cols)
        weight = jnp.concatenate([ref[span, :] for ref in w_refs], axis=1)
        out_ref[:, at : at + cols] = dot_nt(grads[...], weight).astype(out_ref.dtype)


def pair_sums(scale, offsets, got, query, key, value, grad, norm, delta):
    rows, width = query.shape
    me = lax.axis_index("ctx")
    exponent = scale * math.log2(math.e)
    first = jnp.concatenate([ref[:rows, :width] for ref in got], axis=0)
    second = jnp.concatenate([ref[:rows, width:] for ref in got], axis=0)
    extra = jnp.concatenate([ref[rows:, :width] for ref in got], axis=1).astype(jnp.float32)
    norms = (1.0 / scale) * jnp.sum(extra[:PIECES], axis=0, keepdims=True)
    deltas = jnp.sum(extra[PIECES : 2 * PIECES], axis=0, keepdims=True)
    lanes = lax.broadcasted_iota(jnp.int32, (rows, len(got) * rows), 1)
    offset = jnp.zeros_like(lanes)
    for at, value_at in enumerate(offsets):
        offset = jnp.where(lanes // rows == at, value_at, offset)
    earlier = (offset ^ me) < me
    scores = dot_nt(jnp.concatenate([query, key], axis=0), first)
    scores = jnp.where(earlier, scores[:rows] - norm, scores[rows:] - norms)
    probs = jnp.exp2(exponent * scores)
    prob_grad = dot_nt(jnp.concatenate([grad, value], axis=0), second)
    prob_grad = jnp.where(earlier, prob_grad[:rows] - delta, prob_grad[rows:] - deltas)
    score_grad = probs * prob_grad
    sides = jnp.concatenate(
        [jnp.where(earlier, score_grad, 0.0), jnp.where(earlier, 0.0, score_grad)], axis=0
    ).astype(jnp.bfloat16)
    both_sum = dot_nn(sides, first)
    value_sum = dot_nn(jnp.where(earlier, 0.0, probs).astype(jnp.bfloat16), second)
    return both_sum[:rows], both_sum[rows:], value_sum


def own_columns(q_ref, k_ref, v_ref, g_ref, a_ref, n_ref):
    grad = g_ref[...]
    norm = jnp.sum(jnp.where(diagonal(q_ref.shape[0]), n_ref[...], 0.0), axis=1, keepdims=True)
    return q_ref[...], k_ref[...], v_ref[...], grad, norm, delta_of(grad, a_ref[...])


def first_kernel(scale, offsets, *refs):
    out_ref = refs[-1]
    own = own_columns(*refs[:6])
    query, key, value, grad, norm, delta = own
    rows, width = query.shape
    exponent = scale * math.log2(math.e)
    row_at = lax.broadcasted_iota(jnp.int32, (rows, rows), 0)
    col_at = lax.broadcasted_iota(jnp.int32, (rows, rows), 1)
    probs = jnp.where(col_at <= row_at, jnp.exp2(exponent * (dot_nt(query, key) - norm)), 0.0)
    score_low = (probs * (dot_nt(grad, value) - delta)).astype(jnp.bfloat16)
    sums = pair_sums(scale, offsets, refs[6:-1], *own)
    out_ref[:, :width] = sums[0] + dot_nn(score_low, key)
    out_ref[:, width : 2 * width] = sums[1] + dot_tn(score_low, query)
    out_ref[:, 2 * width :] = sums[2] + dot_tn(probs.astype(jnp.bfloat16), grad)


def near_kernel(scale, part, offsets, *refs):
    grads, front = refs[-2:]
    w_refs, sum_ref, got = refs[6:9], refs[9], refs[10:-2]
    own = own_columns(*refs[:6])
    width = own[0].shape[1]
    sums = pair_sums(scale, offsets, got, *own)
    grads[:, :width] = (scale * (sum_ref[:, :width] + sums[0])).astype(jnp.bfloat16)
    grads[:, width : 2 * width] = (
        scale * (sum_ref[:, width : 2 * width] + sums[1])
    ).astype(jnp.bfloat16)
    grads[:, 2 * width :] = (sum_ref[:, 2 * width :] + sums[2]).astype(jnp.bfloat16)
    project(grads, w_refs, (lax.axis_index("head") ^ 3) * part, front)


def far_kernel(part, grads, wq_ref, wk_ref, wv_ref, front, back):
    w_refs = (wq_ref, wk_ref, wv_ref)
    head = lax.axis_index("head")
    start = (head ^ 2) * part
    project(grads, w_refs, start, front)
    project(grads, w_refs, start + part // 2, back)


def close_kernel(part, grads, wq_ref, wk_ref, wv_ref, last, near, mine):
    w_refs = (wq_ref, wk_ref, wv_ref)
    head = lax.axis_index("head")
    project(grads, w_refs, (head ^ 3) * part + part // 2, last)
    project(grads, w_refs, (head ^ 1) * part, near)
    project(grads, w_refs, head * part, mine)


def swap(value, axis, offset):
    size = lax.axis_size(axis)
    return lax.ppermute(value, axis, [(at, at ^ offset) for at in range(size)])


def near_body(own, weights, scale):
    rows, width = own[0].shape
    depth = weights[0].shape[0]
    ctx = lax.axis_size("ctx")
    part = depth // lax.axis_size("head")
    vmem = pl.BlockSpec(memory_space=pltpu.VMEM)
    hbm = pl.BlockSpec(memory_space=pl.ANY)
    params = pltpu.CompilerParams(vmem_limit_bytes=32 * MIB)
    hop = jax.ShapeDtypeStruct((rows + EXTRA, 2 * width), jnp.bfloat16)
    bits = (ctx - 1).bit_length()
    sent = pl.pallas_call(
        send_kernel,
        out_shape=[hop] * bits,
        in_specs=[hbm] * 6,
        out_specs=[hbm] * bits,
        scratch_shapes=[pltpu.VMEM((rows, width), jnp.bfloat16)] * 5
        + [
            pltpu.VMEM((1, rows), jnp.float32),
            pltpu.VMEM((EXTRA, 2 * width), jnp.bfloat16),
            pltpu.SemaphoreType.DMA((6,)),
            pltpu.SemaphoreType.DMA((2 * bits,)),
            pltpu.SemaphoreType.DMA((bits,)),
        ],
        compiler_params=pltpu.CompilerParams(vmem_limit_bytes=56 * MIB),
        cost_estimate=pl.CostEstimate(
            flops=5000000000, bytes_accessed=20 * rows * width, transcendentals=0
        ),
    )(*own)
    got = {at: swap(sent[at.bit_length() - 1], "ctx", at) for at in (1, *range(2, ctx, 2))}
    soon = [at for at in (6,) if at < ctx]
    early, norm = lax.optimization_barrier((tuple(got[at] for at in soon), own[-1]))
    got.update(zip(soon, early))
    own = own[:-1] + (norm * (1.0 / scale),)
    for at in range(2, ctx, 2):
        got[at + 1] = swap(got[at], "ctx", 1)
    soon = tuple(at for at in got if at == 1 or at % 2 == 0)
    late = tuple(at for at in got if at not in soon)
    half_low = jax.ShapeDtypeStruct((rows, part // 2), jnp.bfloat16)
    half = jax.ShapeDtypeStruct((rows, part // 2), jnp.float32)
    low = jax.ShapeDtypeStruct((rows, part), jnp.bfloat16)
    full = jax.ShapeDtypeStruct((rows, part), jnp.float32)
    sums = pl.pallas_call(
        functools.partial(first_kernel, scale, soon),
        out_shape=jax.ShapeDtypeStruct((rows, 3 * width), jnp.float32),
        in_specs=[vmem] * (6 + len(soon)),
        out_specs=vmem,
        compiler_params=params,
        cost_estimate=pl.CostEstimate(
            flops=14 * rows * rows * len(soon) * width,
            bytes_accessed=4 * rows * len(soon) * width,
            transcendentals=rows * rows * len(soon),
        ),
    )(*own, *[got[at] for at in soon])
    grads, front = pl.pallas_call(
        functools.partial(near_kernel, scale, part, late),
        out_shape=[jax.ShapeDtypeStruct((rows, 3 * width), jnp.bfloat16), half_low],
        in_specs=[vmem] * (10 + len(late)),
        out_specs=[vmem] * 2,
        compiler_params=params,
        cost_estimate=pl.CostEstimate(
            flops=14 * rows * rows * ctx * width + 6 * rows * width * part,
            bytes_accessed=4 * rows * ctx * width + 6 * part * width,
            transcendentals=rows * rows * ctx,
        ),
    )(*own, *weights, sums, *[got[at] for at in late])
    front = swap(front, "head", 1)
    def projected(kernel, outs, operands):
        count = sum(out.shape[1] for out in outs)
        return pl.pallas_call(
            functools.partial(kernel, part),
            out_shape=outs,
            in_specs=[vmem] * (1 + len(weights)),
            out_specs=[vmem] * len(outs),
            compiler_params=params,
            cost_estimate=pl.CostEstimate(
                flops=6 * rows * width * count, bytes_accessed=6 * count * width, transcendentals=0
            ),
        )(*operands)

    two_front, two_back = projected(far_kernel, [half, half], (grads, *weights))
    grads, two_front = lax.optimization_barrier((grads, two_front))
    back, near, total = projected(close_kernel, [half_low, low, full], (grads, *weights))
    back = swap(back, "head", 1)
    near, front = lax.optimization_barrier((near, front))
    front = swap((two_front + front.astype(jnp.float32)).astype(jnp.bfloat16), "head", 2)
    back = swap((two_back + back.astype(jnp.float32)).astype(jnp.bfloat16), "head", 2)
    near = swap(near, "head", 1)
    far_sum = jnp.concatenate([front, back], axis=1).astype(jnp.float32)
    return (total + near.astype(jnp.float32) + far_sum).astype(jnp.bfloat16)


def far_body(own, weights, scale):
    rows, width = own[0].shape
    depth = weights[0].shape[0]
    ctx = lax.axis_size("ctx")
    parts = lax.axis_size("head")
    spot = lax.axis_index("ctx").astype(jnp.int32).reshape(1)
    vmem = pl.BlockSpec(memory_space=pltpu.VMEM)
    smem = pl.BlockSpec(memory_space=pltpu.SMEM)
    hbm = pl.BlockSpec(memory_space=pl.ANY)
    packed = pl.pallas_call(
        pack_kernel,
        out_shape=jax.ShapeDtypeStruct((ctx, rows + EXTRA, 2 * width), jnp.bfloat16),
        in_specs=[smem] + [vmem] * 6,
        out_specs=vmem,
        compiler_params=pltpu.CompilerParams(vmem_limit_bytes=32 * MIB),
    )(spot, *own)
    got = lax.all_to_all(packed, "ctx", split_axis=0, concat_axis=0, tiled=True)
    total = ctx * rows
    group = math.gcd(ctx, 8)
    parted = pl.pallas_call(
        functools.partial(main_kernel, group, scale),
        out_shape=jax.ShapeDtypeStruct((parts, rows, depth // parts), jnp.bfloat16),
        in_specs=[smem] + [vmem] * 7 + [hbm] * 3,
        out_specs=vmem,
        scratch_shapes=[
            pltpu.VMEM((depth, 3 * width), jnp.bfloat16),
            pltpu.VMEM((rows, 3 * width), jnp.bfloat16),
            pltpu.SemaphoreType.DMA((3,)),
        ],
        compiler_params=pltpu.CompilerParams(vmem_limit_bytes=48 * MIB),
        cost_estimate=pl.CostEstimate(
            flops=14 * rows * total * width + 6 * rows * width * depth,
            bytes_accessed=6 * depth * width + 10 * total * width,
            transcendentals=2 * rows * total,
        ),
    )(spot, got, *own, *weights)
    swapped = lax.all_to_all(parted, "head", split_axis=0, concat_axis=0, tiled=True)
    return jnp.sum(swapped.astype(jnp.float32), axis=0).astype(jnp.bfloat16)


def body(
    queries,
    key_rows,
    value_rows,
    out_grad,
    attn_out,
    log_norm,
    query_weight,
    key_weight,
    value_weight,
):
    rows, width = queries.shape
    ctx, parts = lax.axis_size("ctx"), lax.axis_size("head")
    own = (queries, key_rows, value_rows, out_grad, attn_out, log_norm.reshape(1, rows))
    weights = (query_weight, key_weight, value_weight)
    near = ctx <= 8 and parts == 4 and ctx & (ctx - 1) == 0
    return (near_body if near else far_body)(own, weights, width ** (-0.5))


def solution(mesh):
    return jax.shard_map(
        body,
        mesh=mesh,
        in_specs=(P("ctx", "head"),) * 6 + (P(None, "head"),) * 3,
        out_specs=P("ctx", "head"),
        check_vma=False,
    )
```

```python
import functools
import math

import jax
import jax.numpy as jnp
from jax import lax
from jax.experimental import pallas as pl
from jax.experimental.pallas import tpu as pltpu
from jax.sharding import PartitionSpec as P

NT = (((1,), (1,)), ((), ()))
TN = (((0,), (0,)), ((), ()))
PIECES = 3
EXTRA = 16
MIB = 1024 * 1024


def dot_nt(left, right):
    return lax.dot_general(left, right, NT, preferred_element_type=jnp.float32)


def dot_tn(left, right):
    return lax.dot_general(left, right, TN, preferred_element_type=jnp.float32)


def dot_nn(left, right):
    return jnp.dot(left, right, preferred_element_type=jnp.float32)


def pieces_of(value):
    out = []
    rest = value
    for _ in range(PIECES):
        low = rest.astype(jnp.bfloat16).astype(jnp.float32)
        out.append(low)
        rest = rest - low
    return out


def diagonal(rows):
    row_at = lax.broadcasted_iota(jnp.int32, (rows, rows), 0)
    col_at = lax.broadcasted_iota(jnp.int32, (rows, rows), 1)
    return row_at == col_at


def delta_of(grad, attn):
    return jnp.sum(grad.astype(jnp.float32) * attn.astype(jnp.float32), axis=1, keepdims=True)


def pack_kernel(me_ref, q_ref, k_ref, v_ref, g_ref, a_ref, n_ref, out_ref):
    rows, width = q_ref.shape
    me = me_ref[0]
    delta = delta_of(g_ref[...], a_ref[...])
    delta = jnp.sum(jnp.where(diagonal(rows), delta, 0.0), axis=0, keepdims=True)
    row = lax.broadcasted_iota(jnp.int32, (EXTRA, rows), 0)
    extra = jnp.zeros((EXTRA, rows), jnp.float32)
    for at, piece in enumerate(pieces_of(n_ref[...]) + pieces_of(delta)):
        extra = jnp.where(row == at, piece, extra)
    extra = extra.astype(jnp.bfloat16)

    def for_later(at, carry):
        out_ref[at, :rows, :width] = k_ref[...]
        out_ref[at, :rows, width:] = v_ref[...]
        out_ref[at, rows:, :] = jnp.zeros((EXTRA, 2 * width), jnp.bfloat16)
        return carry

    def for_earlier(at, carry):
        out_ref[at, :rows, :width] = q_ref[...]
        out_ref[at, :rows, width:] = g_ref[...]
        out_ref[at, rows:, :width] = extra
        out_ref[at, rows:, width:] = jnp.zeros((EXTRA, width), jnp.bfloat16)
        return carry

    lax.fori_loop(0, me + 1, for_earlier, 0)
    lax.fori_loop(me + 1, out_ref.shape[0], for_later, 0)


def main_kernel(
    group,
    scale,
    me_ref,
    got_ref,
    q_ref,
    k_ref,
    v_ref,
    g_ref,
    a_ref,
    n_ref,
    wq_ref,
    wk_ref,
    wv_ref,
    out_ref,
    w_all,
    grads,
    sems,
):
    rows, width = q_ref.shape
    copies = [
        pltpu.make_async_copy(ref, w_all.at[:, at * width : (at + 1) * width], sems.at[at])
        for at, ref in enumerate((wq_ref, wk_ref, wv_ref))
    ]
    for copy in copies:
        copy.start()
    me = me_ref[0]
    exponent = scale * math.log2(math.e)
    query, key, value, grad = q_ref[...], k_ref[...], v_ref[...], g_ref[...]
    eye = diagonal(rows)
    norm = (1.0 / scale) * jnp.sum(jnp.where(eye, n_ref[...], 0.0), axis=1, keepdims=True)
    delta = delta_of(grad, a_ref[...])

    row_at = lax.broadcasted_iota(jnp.int32, (rows, rows), 0)
    col_at = lax.broadcasted_iota(jnp.int32, (rows, rows), 1)
    probs = jnp.where(col_at <= row_at, jnp.exp2(exponent * (dot_nt(query, key) - norm)), 0.0)
    score_low = (probs * (dot_nt(grad, value) - delta)).astype(jnp.bfloat16)
    query_sum = dot_nn(score_low, key)
    key_sum = dot_tn(score_low, query)
    value_sum = dot_tn(probs.astype(jnp.bfloat16), grad)

    first_side = jnp.concatenate([query, key], axis=0)
    second_side = jnp.concatenate([grad, value], axis=0)

    def step(at, sums):
        both_sum, value_sum = sums
        blocks = [at * group + i for i in range(group)]
        first = jnp.concatenate([got_ref[b, :rows, :width] for b in blocks], axis=0)
        second = jnp.concatenate([got_ref[b, :rows, width:] for b in blocks], axis=0)
        extra = jnp.concatenate([got_ref[b, rows:, :width] for b in blocks], axis=1)
        extra = extra.astype(jnp.float32)
        norms = (1.0 / scale) * jnp.sum(extra[:PIECES], axis=0, keepdims=True)
        deltas = jnp.sum(extra[PIECES : 2 * PIECES], axis=0, keepdims=True)
        block = at * group + lax.broadcasted_iota(jnp.int32, (rows, group * rows), 1) // rows
        earlier, later = block < me, block > me
        scores = dot_nt(first_side, first)
        scores = jnp.where(earlier, scores[:rows] - norm, scores[rows:] - norms)
        probs = jnp.exp2(exponent * jnp.where(block == me, 0.0, scores))
        prob_grad = dot_nt(second_side, second)
        prob_grad = jnp.where(earlier, prob_grad[:rows] - delta, prob_grad[rows:] - deltas)
        score_grad = probs * prob_grad
        sides = jnp.concatenate(
            [jnp.where(earlier, score_grad, 0.0), jnp.where(later, score_grad, 0.0)], axis=0
        ).astype(jnp.bfloat16)
        both_sum += dot_nn(sides, first)
        value_sum += dot_nn(jnp.where(later, probs, 0.0).astype(jnp.bfloat16), second)
        return both_sum, value_sum

    sums = (jnp.concatenate([query_sum, key_sum], axis=0), value_sum)
    count = got_ref.shape[0] // group
    if count == 1:
        sums = step(0, sums)
    else:
        sums = lax.fori_loop(0, count, step, sums)
    grads[:, :width] = (scale * sums[0][:rows]).astype(jnp.bfloat16)
    grads[:, width : 2 * width] = (scale * sums[0][rows:]).astype(jnp.bfloat16)
    grads[:, 2 * width :] = sums[1].astype(jnp.bfloat16)
    for copy in copies:
        copy.wait()
    parts, _, part = out_ref.shape
    cols = math.gcd(part, 512)
    for h in range(parts):
        for at in range(0, part, cols):
            weight = w_all[h * part + at : h * part + at + cols, :]
            out_ref[h, :, at : at + cols] = dot_nt(grads[...], weight).astype(jnp.bfloat16)


def send_kernel(q_in, k_in, v_in, g_in, a_in, n_in, *refs):
    q_ref, k_ref, v_ref, g_ref, a_ref, n_ref, extra_ref, in_sems, row_sems, extra_sems = refs[-10:]
    hops = refs[:-10]
    me = lax.axis_index("ctx")
    rows, width = g_ref.shape
    pairs = (
        (k_in, k_ref),
        (v_in, v_ref),
        (q_in, q_ref),
        (g_in, g_ref),
        (a_in, a_ref),
        (n_in, n_ref),
    )
    loads = [pltpu.make_async_copy(*pair, in_sems.at[at]) for at, pair in enumerate(pairs)]
    for load in loads:
        load.start()

    def moves(bit, first, second):
        return [
            pltpu.make_async_copy(
                src, hops[bit].at[:rows, at * width : (at + 1) * width], row_sems.at[2 * bit + at]
            )
            for at, src in enumerate((first, second))
        ]

    for load in loads[:4]:
        load.wait()
    for bit in range(len(hops)):
        later = (me & (1 << bit)) == 0

        @pl.when(later)
        def _():
            for move in moves(bit, k_ref, v_ref):
                move.start()

        @pl.when(jnp.logical_not(later))
        def _():
            for move in moves(bit, q_ref, g_ref):
                move.start()

    for load in loads[4:]:
        load.wait()
    delta = delta_of(g_ref[...], a_ref[...])
    delta = jnp.sum(jnp.where(diagonal(rows), delta, 0.0), axis=0, keepdims=True)
    row = lax.broadcasted_iota(jnp.int32, (EXTRA, rows), 0)
    extra = jnp.zeros((EXTRA, rows), jnp.float32)
    for at, part in enumerate(pieces_of(n_ref[...]) + pieces_of(delta)):
        extra = jnp.where(row == at, part, extra)
    extra_ref[:, :width] = extra.astype(jnp.bfloat16)
    extra_ref[:, width:] = jnp.zeros((EXTRA, width), jnp.bfloat16)
    tails = [
        pltpu.make_async_copy(extra_ref, hop.at[rows:, :], extra_sems.at[bit])
        for bit, hop in enumerate(hops)
    ]
    for tail in tails:
        tail.start()
    for bit in range(len(hops)):
        for move in moves(bit, k_ref, v_ref):
            move.wait()
    for tail in tails:
        tail.wait()


def project(grads, w_refs, start, out_ref):
    part = out_ref.shape[1]
    cols = math.gcd(part, 512)
    for at in range(0, part, cols):
        span = pl.ds(pl.multiple_of(start + at, cols), cols)
        weight = jnp.concatenate([ref[span, :] for ref in w_refs], axis=1)
        out_ref[:, at : at + cols] = dot_nt(grads[...], weight).astype(out_ref.dtype)


def pair_sums(scale, offsets, got, query, key, value, grad, norm, delta):
    rows, width = query.shape
    me = lax.axis_index("ctx")
    exponent = scale * math.log2(math.e)
    first = jnp.concatenate([ref[:rows, :width] for ref in got], axis=0)
    second = jnp.concatenate([ref[:rows, width:] for ref in got], axis=0)
    extra = jnp.concatenate([ref[rows:, :width] for ref in got], axis=1).astype(jnp.float32)
    norms = (1.0 / scale) * jnp.sum(extra[:PIECES], axis=0, keepdims=True)
    deltas = jnp.sum(extra[PIECES : 2 * PIECES], axis=0, keepdims=True)
    lanes = lax.broadcasted_iota(jnp.int32, (rows, len(got) * rows), 1)
    offset = jnp.zeros_like(lanes)
    for at, value_at in enumerate(offsets):
        offset = jnp.where(lanes // rows == at, value_at, offset)
    earlier = (offset ^ me) < me
    scores = dot_nt(jnp.concatenate([query, key], axis=0), first)
    scores = jnp.where(earlier, scores[:rows] - norm, scores[rows:] - norms)
    probs = jnp.exp2(exponent * scores)
    prob_grad = dot_nt(jnp.concatenate([grad, value], axis=0), second)
    prob_grad = jnp.where(earlier, prob_grad[:rows] - delta, prob_grad[rows:] - deltas)
    score_grad = probs * prob_grad
    sides = jnp.concatenate(
        [jnp.where(earlier, score_grad, 0.0), jnp.where(earlier, 0.0, score_grad)], axis=0
    ).astype(jnp.bfloat16)
    both_sum = dot_nn(sides, first)
    value_sum = dot_nn(jnp.where(earlier, 0.0, probs).astype(jnp.bfloat16), second)
    return both_sum[:rows], both_sum[rows:], value_sum


def own_columns(q_ref, k_ref, v_ref, g_ref, a_ref, n_ref):
    grad = g_ref[...]
    norm = jnp.sum(jnp.where(diagonal(q_ref.shape[0]), n_ref[...], 0.0), axis=1, keepdims=True)
    return q_ref[...], k_ref[...], v_ref[...], grad, norm, delta_of(grad, a_ref[...])


def first_kernel(scale, offsets, *refs):
    out_ref = refs[-1]
    own = own_columns(*refs[:6])
    query, key, value, grad, norm, delta = own
    rows, width = query.shape
    exponent = scale * math.log2(math.e)
    row_at = lax.broadcasted_iota(jnp.int32, (rows, rows), 0)
    col_at = lax.broadcasted_iota(jnp.int32, (rows, rows), 1)
    probs = jnp.where(col_at <= row_at, jnp.exp2(exponent * (dot_nt(query, key) - norm)), 0.0)
    score_low = (probs * (dot_nt(grad, value) - delta)).astype(jnp.bfloat16)
    sums = pair_sums(scale, offsets, refs[6:-1], *own)
    out_ref[:, :width] = sums[0] + dot_nn(score_low, key)
    out_ref[:, width : 2 * width] = sums[1] + dot_tn(score_low, query)
    lane = lax.broadcasted_iota(jnp.int32, (rows, width), 1)
    out_ref[:, 3 * width :] = jnp.where(lane == 0, norm, delta)
    out_ref[:, 2 * width : 3 * width] = sums[2] + dot_tn(probs.astype(jnp.bfloat16), grad)


def near_kernel(scale, part, offsets, *refs):
    grads, front = refs[-2:]
    w_refs, sum_ref, got = refs[4:7], refs[7], refs[8:-2]
    width = refs[0].shape[1]
    columns = sum_ref[:, 3 * width : 3 * width + 1], sum_ref[:, 3 * width + 1 : 3 * width + 2]
    own = [ref[...] for ref in refs[:4]] + list(columns)
    sums = pair_sums(scale, offsets, got, *own)
    grads[:, :width] = (scale * (sum_ref[:, :width] + sums[0])).astype(jnp.bfloat16)
    grads[:, width : 2 * width] = (
        scale * (sum_ref[:, width : 2 * width] + sums[1])
    ).astype(jnp.bfloat16)
    grads[:, 2 * width :] = (sum_ref[:, 2 * width : 3 * width] + sums[2]).astype(jnp.bfloat16)
    project(grads, w_refs, (lax.axis_index("head") ^ 3) * part, front)


def far_kernel(part, grads, wq_ref, wk_ref, wv_ref, front, back):
    w_refs = (wq_ref, wk_ref, wv_ref)
    head = lax.axis_index("head")
    start = (head ^ 2) * part
    project(grads, w_refs, start, front)
    project(grads, w_refs, start + part // 2, back)


def close_kernel(part, grads, wq_ref, wk_ref, wv_ref, last, near, mine):
    w_refs = (wq_ref, wk_ref, wv_ref)
    head = lax.axis_index("head")
    project(grads, w_refs, (head ^ 3) * part + part // 2, last)
    project(grads, w_refs, (head ^ 1) * part, near)
    project(grads, w_refs, head * part, mine)


def swap(value, axis, offset):
    size = lax.axis_size(axis)
    return lax.ppermute(value, axis, [(at, at ^ offset) for at in range(size)])


def near_body(own, weights, scale):
    rows, width = own[0].shape
    depth = weights[0].shape[0]
    ctx = lax.axis_size("ctx")
    part = depth // lax.axis_size("head")
    vmem = pl.BlockSpec(memory_space=pltpu.VMEM)
    hbm = pl.BlockSpec(memory_space=pl.ANY)
    params = pltpu.CompilerParams(vmem_limit_bytes=32 * MIB)
    hop = jax.ShapeDtypeStruct((rows + EXTRA, 2 * width), jnp.bfloat16)
    bits = (ctx - 1).bit_length()
    sent = pl.pallas_call(
        send_kernel,
        out_shape=[hop] * bits,
        in_specs=[hbm] * 6,
        out_specs=[hbm] * bits,
        scratch_shapes=[pltpu.VMEM((rows, width), jnp.bfloat16)] * 5
        + [
            pltpu.VMEM((1, rows), jnp.float32),
            pltpu.VMEM((EXTRA, 2 * width), jnp.bfloat16),
            pltpu.SemaphoreType.DMA((6,)),
            pltpu.SemaphoreType.DMA((2 * bits,)),
            pltpu.SemaphoreType.DMA((bits,)),
        ],
        compiler_params=pltpu.CompilerParams(vmem_limit_bytes=56 * MIB),
        cost_estimate=pl.CostEstimate(
            flops=5000000000, bytes_accessed=20 * rows * width, transcendentals=0
        ),
    )(*own)
    got = {at: swap(sent[at.bit_length() - 1], "ctx", at) for at in (1, *range(2, ctx, 2))}
    soon = [at for at in (6,) if at < ctx]
    early, norm = lax.optimization_barrier((tuple(got[at] for at in soon), own[-1]))
    got.update(zip(soon, early))
    own = own[:-1] + (norm * (1.0 / scale),)
    for at in range(2, ctx, 2):
        got[at + 1] = swap(got[at], "ctx", 1)
    soon = tuple(at for at in got if at == 1 or at % 2 == 0)
    late = tuple(at for at in got if at not in soon)
    half_low = jax.ShapeDtypeStruct((rows, part // 2), jnp.bfloat16)
    half = jax.ShapeDtypeStruct((rows, part // 2), jnp.float32)
    low = jax.ShapeDtypeStruct((rows, part), jnp.bfloat16)
    full = jax.ShapeDtypeStruct((rows, part), jnp.float32)
    sums = pl.pallas_call(
        functools.partial(first_kernel, scale, soon),
        out_shape=jax.ShapeDtypeStruct((rows, 4 * width), jnp.float32),
        in_specs=[vmem] * (6 + len(soon)),
        out_specs=vmem,
        compiler_params=params,
        cost_estimate=pl.CostEstimate(
            flops=14 * rows * rows * len(soon) * width,
            bytes_accessed=4 * rows * len(soon) * width,
            transcendentals=rows * rows * len(soon),
        ),
    )(*own, *[got[at] for at in soon])
    grads, front = pl.pallas_call(
        functools.partial(near_kernel, scale, part, late),
        out_shape=[jax.ShapeDtypeStruct((rows, 3 * width), jnp.bfloat16), half_low],
        in_specs=[vmem] * (8 + len(late)),
        out_specs=[vmem] * 2,
        compiler_params=params,
        cost_estimate=pl.CostEstimate(
            flops=14 * rows * rows * ctx * width + 6 * rows * width * part,
            bytes_accessed=4 * rows * ctx * width + 6 * part * width,
            transcendentals=rows * rows * ctx,
        ),
    )(*own[:4], *weights, sums, *[got[at] for at in late])
    front = swap(front, "head", 1)
    def projected(kernel, outs, operands):
        count = sum(out.shape[1] for out in outs)
        return pl.pallas_call(
            functools.partial(kernel, part),
            out_shape=outs,
            in_specs=[vmem] * (1 + len(weights)),
            out_specs=[vmem] * len(outs),
            compiler_params=params,
            cost_estimate=pl.CostEstimate(
                flops=6 * rows * width * count, bytes_accessed=6 * count * width, transcendentals=0
            ),
        )(*operands)

    two_front, two_back = projected(far_kernel, [half, half], (grads, *weights))
    grads, two_front = lax.optimization_barrier((grads, two_front))
    back, near, total = projected(close_kernel, [half_low, low, full], (grads, *weights))
    back = swap(back, "head", 1)
    near, front = lax.optimization_barrier((near, front))
    front = swap((two_front + front.astype(jnp.float32)).astype(jnp.bfloat16), "head", 2)
    back = swap((two_back + back.astype(jnp.float32)).astype(jnp.bfloat16), "head", 2)
    near = swap(near, "head", 1)
    far_sum = jnp.concatenate([front, back], axis=1).astype(jnp.float32)
    return (total + near.astype(jnp.float32) + far_sum).astype(jnp.bfloat16)


def far_body(own, weights, scale):
    rows, width = own[0].shape
    depth = weights[0].shape[0]
    ctx = lax.axis_size("ctx")
    parts = lax.axis_size("head")
    spot = lax.axis_index("ctx").astype(jnp.int32).reshape(1)
    vmem = pl.BlockSpec(memory_space=pltpu.VMEM)
    smem = pl.BlockSpec(memory_space=pltpu.SMEM)
    hbm = pl.BlockSpec(memory_space=pl.ANY)
    packed = pl.pallas_call(
        pack_kernel,
        out_shape=jax.ShapeDtypeStruct((ctx, rows + EXTRA, 2 * width), jnp.bfloat16),
        in_specs=[smem] + [vmem] * 6,
        out_specs=vmem,
        compiler_params=pltpu.CompilerParams(vmem_limit_bytes=32 * MIB),
    )(spot, *own)
    got = lax.all_to_all(packed, "ctx", split_axis=0, concat_axis=0, tiled=True)
    total = ctx * rows
    group = math.gcd(ctx, 8)
    parted = pl.pallas_call(
        functools.partial(main_kernel, group, scale),
        out_shape=jax.ShapeDtypeStruct((parts, rows, depth // parts), jnp.bfloat16),
        in_specs=[smem] + [vmem] * 7 + [hbm] * 3,
        out_specs=vmem,
        scratch_shapes=[
            pltpu.VMEM((depth, 3 * width), jnp.bfloat16),
            pltpu.VMEM((rows, 3 * width), jnp.bfloat16),
            pltpu.SemaphoreType.DMA((3,)),
        ],
        compiler_params=pltpu.CompilerParams(vmem_limit_bytes=48 * MIB),
        cost_estimate=pl.CostEstimate(
            flops=14 * rows * total * width + 6 * rows * width * depth,
            bytes_accessed=6 * depth * width + 10 * total * width,
            transcendentals=2 * rows * total,
        ),
    )(spot, got, *own, *weights)
    swapped = lax.all_to_all(parted, "head", split_axis=0, concat_axis=0, tiled=True)
    return jnp.sum(swapped.astype(jnp.float32), axis=0).astype(jnp.bfloat16)


def body(
    queries,
    key_rows,
    value_rows,
    out_grad,
    attn_out,
    log_norm,
    query_weight,
    key_weight,
    value_weight,
):
    rows, width = queries.shape
    ctx, parts = lax.axis_size("ctx"), lax.axis_size("head")
    own = (queries, key_rows, value_rows, out_grad, attn_out, log_norm.reshape(1, rows))
    weights = (query_weight, key_weight, value_weight)
    near = ctx <= 8 and parts == 4 and ctx & (ctx - 1) == 0
    return (near_body if near else far_body)(own, weights, width ** (-0.5))


def solution(mesh):
    return jax.shard_map(
        body,
        mesh=mesh,
        in_specs=(P("ctx", "head"),) * 6 + (P(None, "head"),) * 3,
        out_specs=P("ctx", "head"),
        check_vma=False,
    )
```

```python
import functools
import math

import jax
import jax.numpy as jnp
from jax import lax
from jax.experimental import pallas as pl
from jax.experimental.pallas import tpu as pltpu
from jax.sharding import PartitionSpec as P

NT = (((1,), (1,)), ((), ()))
TN = (((0,), (0,)), ((), ()))
PIECES = 3
EXTRA = 16
MIB = 1024 * 1024


def dot_nt(left, right):
    return lax.dot_general(left, right, NT, preferred_element_type=jnp.float32)


def dot_tn(left, right):
    return lax.dot_general(left, right, TN, preferred_element_type=jnp.float32)


def dot_nn(left, right):
    return jnp.dot(left, right, preferred_element_type=jnp.float32)


def pieces_of(value):
    out = []
    rest = value
    for _ in range(PIECES):
        low = rest.astype(jnp.bfloat16).astype(jnp.float32)
        out.append(low)
        rest = rest - low
    return out


def diagonal(rows):
    row_at = lax.broadcasted_iota(jnp.int32, (rows, rows), 0)
    col_at = lax.broadcasted_iota(jnp.int32, (rows, rows), 1)
    return row_at == col_at


def delta_of(grad, attn):
    return jnp.sum(grad.astype(jnp.float32) * attn.astype(jnp.float32), axis=1, keepdims=True)


def pack_kernel(me_ref, q_ref, k_ref, v_ref, g_ref, a_ref, n_ref, out_ref):
    rows, width = q_ref.shape
    me = me_ref[0]
    delta = delta_of(g_ref[...], a_ref[...])
    delta = jnp.sum(jnp.where(diagonal(rows), delta, 0.0), axis=0, keepdims=True)
    row = lax.broadcasted_iota(jnp.int32, (EXTRA, rows), 0)
    extra = jnp.zeros((EXTRA, rows), jnp.float32)
    for at, piece in enumerate(pieces_of(n_ref[...]) + pieces_of(delta)):
        extra = jnp.where(row == at, piece, extra)
    extra = extra.astype(jnp.bfloat16)

    def for_later(at, carry):
        out_ref[at, :rows, :width] = k_ref[...]
        out_ref[at, :rows, width:] = v_ref[...]
        out_ref[at, rows:, :] = jnp.zeros((EXTRA, 2 * width), jnp.bfloat16)
        return carry

    def for_earlier(at, carry):
        out_ref[at, :rows, :width] = q_ref[...]
        out_ref[at, :rows, width:] = g_ref[...]
        out_ref[at, rows:, :width] = extra
        out_ref[at, rows:, width:] = jnp.zeros((EXTRA, width), jnp.bfloat16)
        return carry

    lax.fori_loop(0, me + 1, for_earlier, 0)
    lax.fori_loop(me + 1, out_ref.shape[0], for_later, 0)


def main_kernel(
    group,
    scale,
    me_ref,
    got_ref,
    q_ref,
    k_ref,
    v_ref,
    g_ref,
    a_ref,
    n_ref,
    wq_ref,
    wk_ref,
    wv_ref,
    out_ref,
    w_all,
    grads,
    sems,
):
    rows, width = q_ref.shape
    copies = [
        pltpu.make_async_copy(ref, w_all.at[:, at * width : (at + 1) * width], sems.at[at])
        for at, ref in enumerate((wq_ref, wk_ref, wv_ref))
    ]
    for copy in copies:
        copy.start()
    me = me_ref[0]
    exponent = scale * math.log2(math.e)
    query, key, value, grad = q_ref[...], k_ref[...], v_ref[...], g_ref[...]
    eye = diagonal(rows)
    norm = (1.0 / scale) * jnp.sum(jnp.where(eye, n_ref[...], 0.0), axis=1, keepdims=True)
    delta = delta_of(grad, a_ref[...])

    row_at = lax.broadcasted_iota(jnp.int32, (rows, rows), 0)
    col_at = lax.broadcasted_iota(jnp.int32, (rows, rows), 1)
    probs = jnp.where(col_at <= row_at, jnp.exp2(exponent * (dot_nt(query, key) - norm)), 0.0)
    score_low = (probs * (dot_nt(grad, value) - delta)).astype(jnp.bfloat16)
    query_sum = dot_nn(score_low, key)
    key_sum = dot_tn(score_low, query)
    value_sum = dot_tn(probs.astype(jnp.bfloat16), grad)

    first_side = jnp.concatenate([query, key], axis=0)
    second_side = jnp.concatenate([grad, value], axis=0)

    def step(at, sums):
        both_sum, value_sum = sums
        blocks = [at * group + i for i in range(group)]
        first = jnp.concatenate([got_ref[b, :rows, :width] for b in blocks], axis=0)
        second = jnp.concatenate([got_ref[b, :rows, width:] for b in blocks], axis=0)
        extra = jnp.concatenate([got_ref[b, rows:, :width] for b in blocks], axis=1)
        extra = extra.astype(jnp.float32)
        norms = (1.0 / scale) * jnp.sum(extra[:PIECES], axis=0, keepdims=True)
        deltas = jnp.sum(extra[PIECES : 2 * PIECES], axis=0, keepdims=True)
        block = at * group + lax.broadcasted_iota(jnp.int32, (rows, group * rows), 1) // rows
        earlier, later = block < me, block > me
        scores = dot_nt(first_side, first)
        scores = jnp.where(earlier, scores[:rows] - norm, scores[rows:] - norms)
        probs = jnp.exp2(exponent * jnp.where(block == me, 0.0, scores))
        prob_grad = dot_nt(second_side, second)
        prob_grad = jnp.where(earlier, prob_grad[:rows] - delta, prob_grad[rows:] - deltas)
        score_grad = probs * prob_grad
        sides = jnp.concatenate(
            [jnp.where(earlier, score_grad, 0.0), jnp.where(later, score_grad, 0.0)], axis=0
        ).astype(jnp.bfloat16)
        both_sum += dot_nn(sides, first)
        value_sum += dot_nn(jnp.where(later, probs, 0.0).astype(jnp.bfloat16), second)
        return both_sum, value_sum

    sums = (jnp.concatenate([query_sum, key_sum], axis=0), value_sum)
    count = got_ref.shape[0] // group
    if count == 1:
        sums = step(0, sums)
    else:
        sums = lax.fori_loop(0, count, step, sums)
    grads[:, :width] = (scale * sums[0][:rows]).astype(jnp.bfloat16)
    grads[:, width : 2 * width] = (scale * sums[0][rows:]).astype(jnp.bfloat16)
    grads[:, 2 * width :] = sums[1].astype(jnp.bfloat16)
    for copy in copies:
        copy.wait()
    parts, _, part = out_ref.shape
    cols = math.gcd(part, 512)
    for h in range(parts):
        for at in range(0, part, cols):
            weight = w_all[h * part + at : h * part + at + cols, :]
            out_ref[h, :, at : at + cols] = dot_nt(grads[...], weight).astype(jnp.bfloat16)


def send_kernel(q_in, k_in, v_in, g_in, a_in, n_in, *refs):
    q_ref, k_ref, v_ref, g_ref, a_ref, n_ref, extra_ref, in_sems, row_sems, extra_sems = refs[-10:]
    hops = refs[:-10]
    me = lax.axis_index("ctx")
    rows, width = g_ref.shape
    pairs = (
        (k_in, k_ref),
        (v_in, v_ref),
        (q_in, q_ref),
        (g_in, g_ref),
        (a_in, a_ref),
        (n_in, n_ref),
    )
    loads = [pltpu.make_async_copy(*pair, in_sems.at[at]) for at, pair in enumerate(pairs)]
    for load in loads:
        load.start()

    def moves(bit, first, second):
        return [
            pltpu.make_async_copy(
                src, hops[bit].at[:rows, at * width : (at + 1) * width], row_sems.at[2 * bit + at]
            )
            for at, src in enumerate((first, second))
        ]

    for load in loads[:4]:
        load.wait()
    for bit in range(len(hops)):
        later = (me & (1 << bit)) == 0

        @pl.when(later)
        def _():
            for move in moves(bit, k_ref, v_ref):
                move.start()

        @pl.when(jnp.logical_not(later))
        def _():
            for move in moves(bit, q_ref, g_ref):
                move.start()

    for load in loads[4:]:
        load.wait()
    delta = delta_of(g_ref[...], a_ref[...])
    delta = jnp.sum(jnp.where(diagonal(rows), delta, 0.0), axis=0, keepdims=True)
    row = lax.broadcasted_iota(jnp.int32, (EXTRA, rows), 0)
    extra = jnp.zeros((EXTRA, rows), jnp.float32)
    for at, part in enumerate(pieces_of(n_ref[...]) + pieces_of(delta)):
        extra = jnp.where(row == at, part, extra)
    extra_ref[:, :width] = extra.astype(jnp.bfloat16)
    extra_ref[:, width:] = jnp.zeros((EXTRA, width), jnp.bfloat16)
    tails = [
        pltpu.make_async_copy(extra_ref, hop.at[rows:, :], extra_sems.at[bit])
        for bit, hop in enumerate(hops)
    ]
    for tail in tails:
        tail.start()
    for bit in range(len(hops)):
        for move in moves(bit, k_ref, v_ref):
            move.wait()
    for tail in tails:
        tail.wait()


def project(grads, w_refs, start, out_ref):
    part = out_ref.shape[1]
    cols = math.gcd(part, 512)
    for at in range(0, part, cols):
        span = pl.ds(pl.multiple_of(start + at, cols), cols)
        weight = jnp.concatenate([ref[span, :] for ref in w_refs], axis=1)
        out_ref[:, at : at + cols] = dot_nt(grads[...], weight).astype(out_ref.dtype)


def pair_sums(scale, offsets, got, query, key, value, grad, norm, delta):
    rows, width = query.shape
    me = lax.axis_index("ctx")
    exponent = scale * math.log2(math.e)
    first = jnp.concatenate([ref[:rows, :width] for ref in got], axis=0)
    second = jnp.concatenate([ref[:rows, width:] for ref in got], axis=0)
    extra = jnp.concatenate([ref[rows:, :width] for ref in got], axis=1).astype(jnp.float32)
    norms = (1.0 / scale) * jnp.sum(extra[:PIECES], axis=0, keepdims=True)
    deltas = jnp.sum(extra[PIECES : 2 * PIECES], axis=0, keepdims=True)
    lanes = lax.broadcasted_iota(jnp.int32, (rows, len(got) * rows), 1)
    offset = jnp.zeros_like(lanes)
    for at, value_at in enumerate(offsets):
        offset = jnp.where(lanes // rows == at, value_at, offset)
    earlier = (offset ^ me) < me
    scores = dot_nt(jnp.concatenate([query, key], axis=0), first)
    scores = jnp.where(earlier, scores[:rows] - norm, scores[rows:] - norms)
    probs = jnp.exp2(exponent * scores)
    prob_grad = dot_nt(jnp.concatenate([grad, value], axis=0), second)
    prob_grad = jnp.where(earlier, prob_grad[:rows] - delta, prob_grad[rows:] - deltas)
    score_grad = probs * prob_grad
    sides = jnp.concatenate(
        [jnp.where(earlier, score_grad, 0.0), jnp.where(earlier, 0.0, score_grad)], axis=0
    ).astype(jnp.bfloat16)
    both_sum = dot_nn(sides, first)
    value_sum = dot_nn(jnp.where(earlier, 0.0, probs).astype(jnp.bfloat16), second)
    return both_sum[:rows], both_sum[rows:], value_sum


def own_columns(q_ref, k_ref, v_ref, g_ref, a_ref, n_ref):
    grad = g_ref[...]
    norm = jnp.sum(jnp.where(diagonal(q_ref.shape[0]), n_ref[...], 0.0), axis=1, keepdims=True)
    return q_ref[...], k_ref[...], v_ref[...], grad, norm, delta_of(grad, a_ref[...])


def first_kernel(scale, offsets, *refs):
    out_ref = refs[-1]
    own = own_columns(*refs[:6])
    query, key, value, grad, norm, delta = own
    rows, width = query.shape
    exponent = scale * math.log2(math.e)
    row_at = lax.broadcasted_iota(jnp.int32, (rows, rows), 0)
    col_at = lax.broadcasted_iota(jnp.int32, (rows, rows), 1)
    probs = jnp.where(col_at <= row_at, jnp.exp2(exponent * (dot_nt(query, key) - norm)), 0.0)
    score_low = (probs * (dot_nt(grad, value) - delta)).astype(jnp.bfloat16)
    sums = pair_sums(scale, offsets, refs[6:-1], *own)
    out_ref[:, :width] = sums[0] + dot_nn(score_low, key)
    out_ref[:, width : 2 * width] = sums[1] + dot_tn(score_low, query)
    lane = lax.broadcasted_iota(jnp.int32, (rows, width), 1)
    out_ref[:, 3 * width :] = jnp.where(lane == 0, norm, delta)
    out_ref[:, 2 * width : 3 * width] = sums[2] + dot_tn(probs.astype(jnp.bfloat16), grad)


def near_kernel(scale, part, offsets, *refs):
    grads, front = refs[-2:]
    w_refs, sum_ref, got = refs[4:7], refs[7], refs[8:-2]
    width = refs[0].shape[1]
    columns = sum_ref[:, 3 * width : 3 * width + 1], sum_ref[:, 3 * width + 1 : 3 * width + 2]
    own = [ref[...] for ref in refs[:4]] + list(columns)
    sums = pair_sums(scale, offsets, got, *own)
    grads[:, :width] = (scale * (sum_ref[:, :width] + sums[0])).astype(jnp.bfloat16)
    grads[:, width : 2 * width] = (
        scale * (sum_ref[:, width : 2 * width] + sums[1])
    ).astype(jnp.bfloat16)
    grads[:, 2 * width :] = (sum_ref[:, 2 * width : 3 * width] + sums[2]).astype(jnp.bfloat16)
    project(grads, w_refs, (lax.axis_index("head") ^ 3) * part, front)


def far_kernel(part, grads, wq_ref, wk_ref, wv_ref, front, back):
    w_refs = (wq_ref, wk_ref, wv_ref)
    head = lax.axis_index("head")
    start = (head ^ 2) * part
    project(grads, w_refs, start, front)
    project(grads, w_refs, start + part // 2, back)


def close_kernel(part, grads, wq_ref, wk_ref, wv_ref, last, near, mine):
    w_refs = (wq_ref, wk_ref, wv_ref)
    head = lax.axis_index("head")
    project(grads, w_refs, (head ^ 3) * part + part // 2, last)
    project(grads, w_refs, (head ^ 1) * part, near)
    project(grads, w_refs, head * part, mine)


def swap(value, axis, offset):
    size = lax.axis_size(axis)
    return lax.ppermute(value, axis, [(at, at ^ offset) for at in range(size)])


def near_body(own, weights, scale):
    rows, width = own[0].shape
    depth = weights[0].shape[0]
    ctx = lax.axis_size("ctx")
    part = depth // lax.axis_size("head")
    vmem = pl.BlockSpec(memory_space=pltpu.VMEM)
    hbm = pl.BlockSpec(memory_space=pl.ANY)
    params = pltpu.CompilerParams(vmem_limit_bytes=32 * MIB)
    hop = jax.ShapeDtypeStruct((rows + EXTRA, 2 * width), jnp.bfloat16)
    bits = (ctx - 1).bit_length()
    sent = pl.pallas_call(
        send_kernel,
        out_shape=[hop] * bits,
        in_specs=[hbm] * 6,
        out_specs=[hbm] * bits,
        scratch_shapes=[pltpu.VMEM((rows, width), jnp.bfloat16)] * 5
        + [
            pltpu.VMEM((1, rows), jnp.float32),
            pltpu.VMEM((EXTRA, 2 * width), jnp.bfloat16),
            pltpu.SemaphoreType.DMA((6,)),
            pltpu.SemaphoreType.DMA((2 * bits,)),
            pltpu.SemaphoreType.DMA((bits,)),
        ],
        compiler_params=pltpu.CompilerParams(vmem_limit_bytes=56 * MIB),
        cost_estimate=pl.CostEstimate(
            flops=5000000000, bytes_accessed=20 * rows * width, transcendentals=0
        ),
    )(*own)
    got = {at: swap(sent[at.bit_length() - 1], "ctx", at) for at in (1, *range(2, ctx, 2))}
    soon = [at for at in (4, 6) if at < ctx]
    early, norm = lax.optimization_barrier((tuple(got[at] for at in soon), own[-1]))
    got.update(zip(soon, early))
    own = own[:-1] + (norm * (1.0 / scale),)
    for at in range(2, ctx, 2):
        got[at + 1] = swap(got[at], "ctx", 1)
    soon = tuple(at for at in got if at == 1 or at % 2 == 0)
    late = tuple(at for at in got if at not in soon)
    half_low = jax.ShapeDtypeStruct((rows, part // 2), jnp.bfloat16)
    half = jax.ShapeDtypeStruct((rows, part // 2), jnp.float32)
    low = jax.ShapeDtypeStruct((rows, part), jnp.bfloat16)
    full = jax.ShapeDtypeStruct((rows, part), jnp.float32)
    sums = pl.pallas_call(
        functools.partial(first_kernel, scale, soon),
        out_shape=jax.ShapeDtypeStruct((rows, 4 * width), jnp.float32),
        in_specs=[vmem] * (6 + len(soon)),
        out_specs=vmem,
        compiler_params=params,
        cost_estimate=pl.CostEstimate(
            flops=14 * rows * rows * len(soon) * width,
            bytes_accessed=4 * rows * len(soon) * width,
            transcendentals=rows * rows * len(soon),
        ),
    )(*own, *[got[at] for at in soon])
    grads, front = pl.pallas_call(
        functools.partial(near_kernel, scale, part, late),
        out_shape=[jax.ShapeDtypeStruct((rows, 3 * width), jnp.bfloat16), half_low],
        in_specs=[vmem] * (8 + len(late)),
        out_specs=[vmem] * 2,
        compiler_params=params,
        cost_estimate=pl.CostEstimate(
            flops=14 * rows * rows * ctx * width + 6 * rows * width * part,
            bytes_accessed=4 * rows * ctx * width + 6 * part * width,
            transcendentals=rows * rows * ctx,
        ),
    )(*own[:4], *weights, sums, *[got[at] for at in late])
    front = swap(front, "head", 1)
    def projected(kernel, outs, operands):
        count = sum(out.shape[1] for out in outs)
        return pl.pallas_call(
            functools.partial(kernel, part),
            out_shape=outs,
            in_specs=[vmem] * (1 + len(weights)),
            out_specs=[vmem] * len(outs),
            compiler_params=params,
            cost_estimate=pl.CostEstimate(
                flops=6 * rows * width * count, bytes_accessed=6 * count * width, transcendentals=0
            ),
        )(*operands)

    two_front, two_back = projected(far_kernel, [half, half], (grads, *weights))
    grads, two_front = lax.optimization_barrier((grads, two_front))
    back, near, total = projected(close_kernel, [half_low, low, full], (grads, *weights))
    back = swap(back, "head", 1)
    near, front = lax.optimization_barrier((near, front))
    front = swap((two_front + front.astype(jnp.float32)).astype(jnp.bfloat16), "head", 2)
    back = swap((two_back + back.astype(jnp.float32)).astype(jnp.bfloat16), "head", 2)
    near = swap(near, "head", 1)
    far_sum = jnp.concatenate([front, back], axis=1).astype(jnp.float32)
    return (total + near.astype(jnp.float32) + far_sum).astype(jnp.bfloat16)


def far_body(own, weights, scale):
    rows, width = own[0].shape
    depth = weights[0].shape[0]
    ctx = lax.axis_size("ctx")
    parts = lax.axis_size("head")
    spot = lax.axis_index("ctx").astype(jnp.int32).reshape(1)
    vmem = pl.BlockSpec(memory_space=pltpu.VMEM)
    smem = pl.BlockSpec(memory_space=pltpu.SMEM)
    hbm = pl.BlockSpec(memory_space=pl.ANY)
    packed = pl.pallas_call(
        pack_kernel,
        out_shape=jax.ShapeDtypeStruct((ctx, rows + EXTRA, 2 * width), jnp.bfloat16),
        in_specs=[smem] + [vmem] * 6,
        out_specs=vmem,
        compiler_params=pltpu.CompilerParams(vmem_limit_bytes=32 * MIB),
    )(spot, *own)
    got = lax.all_to_all(packed, "ctx", split_axis=0, concat_axis=0, tiled=True)
    total = ctx * rows
    group = math.gcd(ctx, 8)
    parted = pl.pallas_call(
        functools.partial(main_kernel, group, scale),
        out_shape=jax.ShapeDtypeStruct((parts, rows, depth // parts), jnp.bfloat16),
        in_specs=[smem] + [vmem] * 7 + [hbm] * 3,
        out_specs=vmem,
        scratch_shapes=[
            pltpu.VMEM((depth, 3 * width), jnp.bfloat16),
            pltpu.VMEM((rows, 3 * width), jnp.bfloat16),
            pltpu.SemaphoreType.DMA((3,)),
        ],
        compiler_params=pltpu.CompilerParams(vmem_limit_bytes=48 * MIB),
        cost_estimate=pl.CostEstimate(
            flops=14 * rows * total * width + 6 * rows * width * depth,
            bytes_accessed=6 * depth * width + 10 * total * width,
            transcendentals=2 * rows * total,
        ),
    )(spot, got, *own, *weights)
    swapped = lax.all_to_all(parted, "head", split_axis=0, concat_axis=0, tiled=True)
    return jnp.sum(swapped.astype(jnp.float32), axis=0).astype(jnp.bfloat16)


def body(
    queries,
    key_rows,
    value_rows,
    out_grad,
    attn_out,
    log_norm,
    query_weight,
    key_weight,
    value_weight,
):
    rows, width = queries.shape
    ctx, parts = lax.axis_size("ctx"), lax.axis_size("head")
    own = (queries, key_rows, value_rows, out_grad, attn_out, log_norm.reshape(1, rows))
    weights = (query_weight, key_weight, value_weight)
    near = ctx <= 8 and parts == 4 and ctx & (ctx - 1) == 0
    return (near_body if near else far_body)(own, weights, width ** (-0.5))


def solution(mesh):
    return jax.shard_map(
        body,
        mesh=mesh,
        in_specs=(P("ctx", "head"),) * 6 + (P(None, "head"),) * 3,
        out_specs=P("ctx", "head"),
        check_vma=False,
    )
```
